32 devices in a mesh: dp: 4 (over y, x), row: 4 (over z), col: 2 (over core).
Axes of the slice: x: 2, y: 2, z: 4, core: 2. Of those that a mesh axis runs over, the one named last changes fastest.
Arguments:
- tokens: bfloat16 [16384, 1024], P(('dp', 'row'), 'col'), may hold values from -6 to 6
- segment: int32 [16, 1024], P(('dp', 'row')), may hold values from 0 to 3, never falling along the last dimension, each value on 1 to 512 neighbouring positions
- cotangent: bfloat16 [16384, 1024], P(('dp', 'row'), 'col'), may hold values from -6 to 6
- w_query: bfloat16 [1024, 1024], P('row', 'col'), may hold values from -0.1875 to 0.1875
- b_query: bfloat16 [1024], P('col'), may hold values from -2 to 2
- w_key: bfloat16 [1024, 1024], P('row', 'col'), may hold values from -0.1875 to 0.1875
- w_value: bfloat16 [1024, 1024], P('row', 'col'), may hold values from -0.1875 to 0.1875
- b_value: bfloat16 [1024], P('col'), may hold values from -2 to 2
- w_out: bfloat16 [1024, 1024], P('row', 'col'), may hold values from -1.5 to 1.5
- b_out: bfloat16 [1024], P('col'), may hold values from -2 to 2
- w_up: bfloat16 [1024, 4096], P('row', 'col'), may hold values from -0.1875 to 0.1875
- b_up: bfloat16 [4096], P('col'), may hold values from -2 to 2
- w_down: bfloat16 [4096, 1024], P('row', 'col'), may hold values from -0.09375 to 0.09375
- b_down: bfloat16 [1024], P('col'), may hold values from -2 to 2
- gain_one: bfloat16 [1024], P('col'), may hold values from 0.5 to 1.5
- shift_one: bfloat16 [1024], P('col'), may hold values from -2 to 2
- gain_two: bfloat16 [1024], P('col'), may hold values from 0.5 to 1.5
- shift_two: bfloat16 [1024], P('col'), may hold values from -2 to 2
Outputs:
- output: bfloat16 [16384, 1024], P(('dp', 'row'), 'col')
- d_tokens: bfloat16 [16384, 1024], P(('dp', 'row'), 'col')
- d_w_query: float32 [1024, 1024], P('row', 'col')
- d_b_query: float32 [1024], P('col')
- d_w_key: float32 [1024, 1024], P('row', 'col')
- d_w_value: float32 [1024, 1024], P('row', 'col')
- d_b_value: float32 [1024], P('col')
- d_w_out: float32 [1024, 1024], P('row', 'col')
- d_b_out: float32 [1024], P('col')
- d_w_up: float32 [1024, 4096], P('row', 'col')
- d_b_up: float32 [4096], P('col')
- d_w_down: float32 [4096, 1024], P('row', 'col')
- d_b_down: float32 [1024], P('col')
- d_gain_one: float32 [1024], P('col')
- d_shift_one: float32 [1024], P('col')
- d_gain_two: float32 [1024], P('col')
- d_shift_two: float32 [1024], P('col')
The draws below stay inside these ranges and needn't reach their ends.
Inputs may be any that keep to these rules, and one draw needn't show every extreme that they name: `segment`: within each row (the 1024 tokens of one group) the numbers never fall; each number marks one sequence of 1 to 512 tokens, and some sequence has exactly 512.
All inputs are finite; a program needn't handle non-finite values.
Results may differ from the reference program's by a relative error of at most 0.018.
Values may be sent and summed in bfloat16 or wider, within the bound.
No kernel may reach another device: no remote copies, remote signals or barrier semaphores. Data moves between devices by JAX's collectives and lax.ppermute only.
A program may use at most 192 MiB of HBM per device.

```python
import math
import jax
import jax.numpy as jnp
import numpy as np
from jax import lax

D = 1024
HEADS = 16
HEAD_DIM = 64
FF = 4096
TOK_DEV = 1024
MAXLEN = 512
SEQS = 4
BINS = 16
TOKENS = 16384


def level_of(own_key, dims, shards, least, top_value):
    def one(axis_at, parts):
        steps = jax.random.uniform(jax.random.fold_in(jax.random.fold_in(own_key, 6), axis_at), (parts,), jnp.float32, least / len(shards), top_value / len(shards))
        return jnp.repeat(jnp.exp(steps), dims[axis_at] // parts).reshape((-1,) + (1,) * (len(dims) - axis_at - 1))

    level = one(*shards[0])
    for cut in shards[1:]:
        level = level * one(*cut)
    return level


def length_profile(count, total, reach, skew):
    portions = [(1 << 20) // math.isqrt(rank ** skew) + 1 for rank in range(2, count + 1)]
    rest, holding = total - reach - (count - 1), [1] * (count - 1)
    while rest > 0:
        candidates = [i for i in range(count - 1) if holding[i] < reach]
        whole, remaining = sum([portions[i] for i in candidates]), rest
        for i in candidates:
            addition = min(reach - holding[i], max(1, remaining * portions[i] // whole), rest)
            holding[i] = holding[i] + addition
            rest = rest - addition
    return np.array([reach] + holding)


def ragged_sizes(key, amount, total, most, lean):
    if amount == 2:
        one = jax.random.randint(key, (), max(1, total - most), min(most, total - 1) + 1)
        return jnp.stack([one, total - one])
    lengths = jnp.asarray(length_profile(amount, total, most, lean), jnp.int32)
    couples = (amount - 1) // 2
    source_of, receiver = lengths[1:1 + 2 * couples:2], lengths[2:2 + 2 * couples:2]
    room = jnp.minimum(source_of - 1, most - receiver)
    passed = jax.random.randint(jax.random.fold_in(key, 1), (couples,), 0, 1 << 20) % (room + 1)
    lengths = lengths.at[1:1 + 2 * couples:2].set(source_of - passed).at[2:2 + 2 * couples:2].set(receiver + passed)
    return lengths[jax.random.permutation(jax.random.fold_in(key, 2), amount)]


def bell_draw(own_key, extent, scale, reach, shards=(), held_as=jnp.bfloat16):
    level = level_of(own_key, extent, shards, -0.22, 0.18) if shards else 1.0
    values = jax.random.normal(own_key, extent, jnp.float32) * scale * level
    return jnp.minimum(jnp.maximum(values, -reach), reach).astype(held_as)


def setup_inputs(seed: int = 0) -> dict:
    arg_keys = jax.random.split(jax.random.key(seed), 19)
    tokens = bell_draw(arg_keys[0], (TOKENS, D), 1.0, 6.0, ((0, 16), (1, 2)))
    segment = jax.vmap(lambda own: jnp.searchsorted(jnp.cumsum(ragged_sizes(own, SEQS, TOK_DEV, MAXLEN, 2)), jnp.arange(TOK_DEV), side="right"))(jax.random.split(arg_keys[1], BINS)).reshape((BINS, TOK_DEV)).astype(jnp.int32)
    cotangent = bell_draw(arg_keys[2], (TOKENS, D), 1.0, 6.0, ((0, 16), (1, 2)))
    w_query = bell_draw(arg_keys[3], (D, D), D ** -0.5, 0.1875, ((0, 4), (1, 2)))
    b_query = bell_draw(arg_keys[4], (D,), 0.3, 2.0, ((0, 2),))
    w_key = bell_draw(arg_keys[5], (D, D), D ** -0.5, 0.1875, ((0, 4), (1, 2)))
    w_value = bell_draw(arg_keys[6], (D, D), D ** -0.5, 0.1875, ((0, 4), (1, 2)))
    b_value = bell_draw(arg_keys[7], (D,), 0.3, 2.0, ((0, 2),))
    w_out = bell_draw(arg_keys[8], (D, D), (D // 64) ** -0.5, 1.5, ((0, 4), (1, 2)))
    b_out = bell_draw(arg_keys[9], (D,), 0.3, 2.0, ((0, 2),))
    w_up = bell_draw(arg_keys[10], (D, FF), D ** -0.5, 0.1875, ((0, 4), (1, 2)))
    b_up = bell_draw(arg_keys[11], (FF,), 0.3, 2.0, ((0, 2),))
    w_down = bell_draw(arg_keys[12], (FF, D), FF ** -0.5, 0.09375, ((0, 4), (1, 2)))
    b_down = bell_draw(arg_keys[13], (D,), 0.3, 2.0, ((0, 2),))
    gain_one = jnp.clip(1.0 + 0.1 * jax.random.normal(arg_keys[14], (D,), jnp.float32), 0.5, 1.5).astype(jnp.bfloat16)
    shift_one = bell_draw(arg_keys[15], (D,), 0.3, 2.0, ((0, 2),))
    gain_two = jnp.clip(1.0 + 0.1 * jax.random.normal(arg_keys[16], (D,), jnp.float32), 0.5, 1.5).astype(jnp.bfloat16)
    shift_two = bell_draw(arg_keys[17], (D,), 0.3, 2.0, ((0, 2),))
    return {"tokens": tokens, "segment": segment, "cotangent": cotangent, "w_query": w_query, "b_query": b_query, "w_key": w_key, "w_value": w_value, "b_value": b_value, "w_out": w_out, "b_out": b_out, "w_up": w_up, "b_up": b_up, "w_down": w_down, "b_down": b_down, "gain_one": gain_one, "shift_one": shift_one, "gain_two": gain_two, "shift_two": shift_two}


@jax.custom_vjp
def low(v):
    return lax.optimization_barrier(v.astype(jnp.bfloat16)).astype(jnp.float32)

@jax.custom_vjp
def low_back(v):
    return v

def low_keep(v):
    return (low(v), None)

def low_pass(kept, grad):
    return (grad,)

def back_keep(v):
    return (v, None)

def back_low(kept, grad):
    return (low(grad),)
low.defvjp(low_keep, low_pass)
low_back.defvjp(back_keep, back_low)
EPSILON = 1e-05
SCALE = 0.125
HIGHEST = lax.Precision.HIGHEST

def product(left, right):
    return jnp.dot(left, right, precision=HIGHEST, preferred_element_type=jnp.float32)

def layer_norm(resid, gain, shift):
    center = lax.optimization_barrier(jnp.mean(resid, axis=1, keepdims=True))
    spread = lax.optimization_barrier(jnp.mean(resid * resid, axis=1, keepdims=True)) - center * center
    return (resid - center) * lax.rsqrt(spread + EPSILON) * gain + shift

def bin_attention(query_rows, key_rows, value_rows, segment_ids):
    block = min(512, TOK_DEV)
    pieces = []
    for begin in range(0, TOK_DEV, block):
        query_block = query_rows[begin:begin + block]
        raw = jnp.einsum('qhd,khd->hqk', query_block, key_rows, precision=HIGHEST) * SCALE
        scores = low_back(raw)
        same = segment_ids[begin:begin + block, None] == segment_ids[None, :]
        scores = jnp.where(same[None], scores, -1e+30)
        row_top = lax.optimization_barrier(jnp.max(scores, axis=2, keepdims=True))
        expo = jnp.exp(scores - row_top)
        probs = low(expo / lax.optimization_barrier(jnp.sum(expo, axis=2, keepdims=True)))
        pieces.append(jnp.einsum('hqk,khd->qhd', probs, value_rows, precision=HIGHEST))
    return jnp.concatenate(pieces, axis=0)

def attention(query_rows, key_rows, value_rows, segment):
    four = (BINS, TOK_DEV, HEADS, HEAD_DIM)
    stepper = jax.checkpoint(bin_attention)

    def scan_body(carry, items):
        return (carry, stepper(items[0], items[1], items[2], items[3]))
    unused, context = lax.scan(scan_body, jnp.zeros((), jnp.float32), (query_rows.reshape(four), key_rows.reshape(four), value_rows.reshape(four), segment))
    return context.reshape(TOKENS, D)

def reference(tokens, segment, cotangent, w_query, b_query, w_key, w_value, b_value, w_out, b_out, w_up, b_up, w_down, b_down, gain_one, shift_one, gain_two, shift_two):

    def forward(inputs, wq_f, bq_f, wk_f, wv_f, bv_f, wo_f, bo_f, wu_f, bu_f, wd_f, bd_f, ga_f, sa_f, gb_f, sb_f):
        query_rows = low(low_back(product(inputs, wq_f) + bq_f))
        key_rows = low(low_back(product(inputs, wk_f)))
        value_rows = low(low_back(product(inputs, wv_f) + bv_f))
        context = low(low_back(attention(query_rows, key_rows, value_rows, segment)))
        branch = low_back(product(context, wo_f) + bo_f)
        hidden = low(layer_norm(inputs + branch, ga_f, sa_f))
        pre_act = low_back(product(hidden, wu_f) + bu_f)
        activated = low(jax.nn.gelu(pre_act, approximate=False))
        ffn_out = low_back(product(activated, wd_f) + bd_f)
        return layer_norm(hidden + ffn_out, gb_f, sb_f)
    output, pullback = jax.vjp(forward, tokens.astype(jnp.float32), w_query.astype(jnp.float32), b_query.astype(jnp.float32), w_key.astype(jnp.float32), w_value.astype(jnp.float32), b_value.astype(jnp.float32), w_out.astype(jnp.float32), b_out.astype(jnp.float32), w_up.astype(jnp.float32), b_up.astype(jnp.float32), w_down.astype(jnp.float32), b_down.astype(jnp.float32), gain_one.astype(jnp.float32), shift_one.astype(jnp.float32), gain_two.astype(jnp.float32), shift_two.astype(jnp.float32))
    grads = pullback(cotangent.astype(jnp.float32))
    return (output.astype(jnp.bfloat16), grads[0].astype(jnp.bfloat16), grads[1], grads[2], grads[3], grads[4], grads[5], grads[6], grads[7], grads[8], grads[9], grads[10], grads[11], grads[12], grads[13], grads[14], grads[15])
```

```python
import jax
import jax.numpy as jnp
from jax import lax
from jax.sharding import PartitionSpec as P

HEAD_DIM = 64


EPSILON = 1e-05
SCALE = 0.125


def matmul(left, right):
    return jnp.dot(left, right, preferred_element_type=jnp.float32)


def matmul_tn(left, right):
    return lax.dot_general(
        left, right, (((0,), (0,)), ((), ())), preferred_element_type=jnp.float32
    )


def matmul_nt(left, right):
    return lax.dot_general(
        left, right, (((1,), (1,)), ((), ())), preferred_element_type=jnp.float32
    )


def masked_scores(query_block, key_three, segment_ids, begin, block):
    raw = (
        jnp.einsum("qhd,khd->hqk", query_block, key_three, preferred_element_type=jnp.float32)
        * SCALE
    )
    same = segment_ids[begin : begin + block, None] == segment_ids[None, :]
    return jnp.where(same[None], raw, -1e30)


def attend(queries, key_rows, value_rows, segment_ids):
    count = queries.shape[0]
    heads_here = queries.shape[1] // HEAD_DIM
    block = min(512, count)
    query_three = queries.reshape(count, heads_here, HEAD_DIM)
    key_three = key_rows.reshape(count, heads_here, HEAD_DIM)
    value_three = value_rows.reshape(count, heads_here, HEAD_DIM)
    pieces = []
    totals = []
    for begin in range(0, count, block):
        scores = masked_scores(
            query_three[begin : begin + block], key_three, segment_ids, begin, block
        )
        row_top = jnp.max(scores, axis=2, keepdims=True)
        expo = jnp.exp(scores - row_top)
        total = jnp.sum(expo, axis=2, keepdims=True)
        probs = (expo / total).astype(jnp.bfloat16)
        pieces.append(
            jnp.einsum("hqk,khd->qhd", probs, value_three, preferred_element_type=jnp.float32)
        )
        totals.append((row_top + jnp.log(total))[:, :, 0])
    context = (
        jnp.concatenate(pieces, axis=0).reshape(count, heads_here * HEAD_DIM).astype(jnp.bfloat16)
    )
    return (context, jnp.concatenate(totals, axis=1))


def attend_back(queries, key_rows, value_rows, segment_ids, log_total, d_context):
    count = queries.shape[0]
    heads_here = queries.shape[1] // HEAD_DIM
    block = min(512, count)
    query_three = queries.reshape(count, heads_here, HEAD_DIM)
    key_three = key_rows.reshape(count, heads_here, HEAD_DIM)
    value_three = value_rows.reshape(count, heads_here, HEAD_DIM)
    grad_three = d_context.reshape(count, heads_here, HEAD_DIM)
    d_keys = jnp.zeros((count, heads_here, HEAD_DIM), jnp.float32)
    d_values = jnp.zeros((count, heads_here, HEAD_DIM), jnp.float32)
    pieces = []
    for begin in range(0, count, block):
        query_block = query_three[begin : begin + block]
        grad_block = grad_three[begin : begin + block]
        scores = masked_scores(query_block, key_three, segment_ids, begin, block)
        probs = jnp.exp(scores - log_total[:, begin : begin + block, None])
        d_probs = jnp.einsum(
            "qhd,khd->hqk", grad_block, value_three, preferred_element_type=jnp.float32
        )
        inner = jnp.sum(probs * d_probs, axis=2, keepdims=True)
        d_scores = (probs * (d_probs - inner)).astype(jnp.bfloat16)
        pieces.append(
            jnp.einsum("hqk,khd->qhd", d_scores, key_three, preferred_element_type=jnp.float32)
            * SCALE
        )
        d_keys = (
            d_keys
            + jnp.einsum("hqk,qhd->khd", d_scores, query_block, preferred_element_type=jnp.float32)
            * SCALE
        )
        d_values = d_values + jnp.einsum(
            "hqk,qhd->khd",
            probs.astype(jnp.bfloat16),
            grad_block,
            preferred_element_type=jnp.float32,
        )
    width = heads_here * HEAD_DIM
    d_queries = jnp.concatenate(pieces, axis=0).reshape(count, width).astype(jnp.bfloat16)
    return (
        d_queries,
        d_keys.reshape(count, width).astype(jnp.bfloat16),
        d_values.reshape(count, width).astype(jnp.bfloat16),
    )


def column_sum(values):
    return jnp.sum(values.astype(jnp.float32), axis=0)


def swapped(part):
    return lax.ppermute(part, "col", [(0, 1), (1, 0)])


def ordered(own, other, core, axis):
    return jnp.where(
        core == 0,
        jnp.concatenate([own, other], axis=axis),
        jnp.concatenate([other, own], axis=axis),
    )


def whole_features(part, core):
    return ordered(part, swapped(part), core, part.ndim - 1)


def half_of(values, index, axis):
    size = values.shape[axis] // 2
    return lax.dynamic_slice_in_dim(values, index * size, size, axis)


def whole_weight(block):
    rows = block.shape[0] // lax.axis_size("dp")
    part = lax.dynamic_slice_in_dim(block, lax.axis_index("dp") * rows, rows, 0)
    return lax.all_gather(part, ("row", "dp"), axis=0, tiled=True)


def reduced_weight(grad):
    part = lax.psum_scatter(grad, ("row", "dp"), scatter_dimension=0, tiled=True)
    return lax.all_gather(part, "dp", axis=0, tiled=True).astype(jnp.float32)


def norm_forward(resid, gain, shift):
    center = jnp.mean(resid, axis=1, keepdims=True)
    inverse = lax.rsqrt(
        jnp.mean(resid * resid, axis=1, keepdims=True) - center * center + EPSILON
    )
    normed = (resid - center) * inverse
    return (normed * gain + shift, normed, inverse)


def norm_backward(grad, normed, inverse, gain):
    scaled = grad * gain
    first = jnp.mean(scaled, axis=1, keepdims=True)
    second = jnp.mean(scaled * normed, axis=1, keepdims=True)
    return inverse * (scaled - first - normed * second)


def body(
    tokens,
    segment,
    cotangent,
    w_query,
    b_query,
    w_key,
    w_value,
    b_value,
    w_out,
    b_out,
    w_up,
    b_up,
    w_down,
    b_down,
    gain_one,
    shift_one,
    gain_two,
    shift_two,
):
    core = lax.axis_index("col")
    half = w_query.shape[1]
    w_qkv = whole_weight(jnp.concatenate([w_query, w_key, w_value], axis=1))
    wo_half = whole_weight(w_out)
    wu = whole_weight(w_up)
    wd_half = whole_weight(w_down)
    token_rows = whole_features(tokens, core)
    cotangent_rows = whole_features(cotangent, core)
    vectors = whole_features(
        jnp.stack([b_out, b_down, gain_one, shift_one, gain_two, shift_two]), core
    ).astype(jnp.float32)
    bias_out, bias_down, gain1, shift1, gain2, shift2 = [vectors[i] for i in range(6)]
    wo = whole_features(wo_half, core)
    wd = ordered(
        half_of(wd_half, core, 0), swapped(half_of(wd_half, 1 - core, 0)), core, 1
    )
    segment_ids = segment[0]

    b_qkv = jnp.concatenate([b_query, jnp.zeros_like(b_query), b_value]).astype(jnp.float32)
    qkv = (matmul(token_rows, w_qkv) + b_qkv).astype(jnp.bfloat16)
    queries, key_rows, value_rows = (qkv[:, i * half : (i + 1) * half] for i in range(3))
    context, log_total = attend(queries, key_rows, value_rows, segment_ids)
    context_rows = whole_features(context, core)
    first_sum = token_rows.astype(jnp.float32) + (matmul(context_rows, wo) + bias_out)
    hidden_f, normed_one, inverse_one = norm_forward(first_sum, gain1, shift1)
    hidden = hidden_f.astype(jnp.bfloat16)
    pre_act = matmul(hidden, wu) + b_up.astype(jnp.float32)
    cdf = 0.5 * (1.0 + lax.erf(pre_act * (0.5**0.5)))
    activated = (pre_act * cdf).astype(jnp.bfloat16)
    slope = cdf + pre_act * (jnp.exp(-0.5 * pre_act * pre_act) * 0.3989422804014327)
    part = matmul(activated, wd).astype(jnp.bfloat16)
    ffn_out = part.astype(jnp.float32) + swapped(part).astype(jnp.float32) + bias_down
    second_sum = hidden.astype(jnp.float32) + ffn_out
    final, normed_two, inverse_two = norm_forward(second_sum, gain2, shift2)
    output = half_of(final.astype(jnp.bfloat16), core, 1)
    y = cotangent_rows.astype(jnp.float32)
    second_grad = norm_backward(y, normed_two, inverse_two, gain2)
    d_gain_two = jnp.sum(y * normed_two, axis=0)
    d_shift_two = jnp.sum(y, axis=0)
    ffn_grad = second_grad.astype(jnp.bfloat16)
    d_w_down = matmul_tn(activated, ffn_grad).astype(jnp.bfloat16)
    d_w_down = ordered(
        half_of(d_w_down, core, 1), swapped(half_of(d_w_down, 1 - core, 1)), core, 0
    )
    o_w_down = reduced_weight(d_w_down)
    d_b_down = column_sum(ffn_grad)
    pre_grad = (matmul_nt(ffn_grad, wd) * slope).astype(jnp.bfloat16)
    d_w_up = matmul_tn(hidden, pre_grad).astype(jnp.bfloat16)
    o_w_up = reduced_weight(d_w_up)
    d_b_up = column_sum(pre_grad)
    hidden_part = matmul_nt(pre_grad, wu).astype(jnp.bfloat16)
    hidden_grad = second_grad + (
        hidden_part.astype(jnp.float32) + swapped(hidden_part).astype(jnp.float32)
    )
    first_grad = norm_backward(hidden_grad, normed_one, inverse_one, gain1)
    d_gain_one = jnp.sum(hidden_grad * normed_one, axis=0)
    d_shift_one = jnp.sum(hidden_grad, axis=0)
    branch_grad = first_grad.astype(jnp.bfloat16)
    branch_half = half_of(branch_grad, core, 1)
    d_w_out = matmul_tn(context_rows, branch_half).astype(jnp.bfloat16)
    o_w_out = reduced_weight(d_w_out)
    d_b_out = column_sum(branch_grad)
    context_grad = matmul_nt(branch_grad, half_of(wo, core, 0)).astype(jnp.bfloat16)
    query_grad, key_grad, value_grad = attend_back(
        queries, key_rows, value_rows, segment_ids, log_total, context_grad
    )
    qkv_grad = jnp.concatenate([query_grad, key_grad, value_grad], axis=1)
    d_w_qkv = matmul_tn(token_rows, qkv_grad).astype(jnp.bfloat16)
    o_w_qkv = reduced_weight(d_w_qkv)
    d_b_qkv = column_sum(qkv_grad)
    token_part = matmul_nt(qkv_grad, w_qkv).astype(jnp.bfloat16)
    token_sum = half_of(token_part, core, 1).astype(jnp.float32) + swapped(
        half_of(token_part, 1 - core, 1)
    ).astype(jnp.float32)
    d_tokens = (token_sum + half_of(first_grad, core, 1)).astype(jnp.bfloat16)

    wide = half_of(
        jnp.stack([d_b_out, d_b_down, d_gain_one, d_shift_one, d_gain_two, d_shift_two]), core, 1
    )
    sums = lax.psum(
        jnp.concatenate([wide.reshape(-1), d_b_qkv, d_b_up]).reshape(-1, 128), ("row", "dp")
    ).reshape(-1)
    pieces = [sums[i * half : (i + 1) * half] for i in range(9)]
    return (
        output,
        d_tokens,
        o_w_qkv[:, :half],
        pieces[6],
        o_w_qkv[:, half : 2 * half],
        o_w_qkv[:, 2 * half :],
        pieces[8],
        o_w_out,
        pieces[0],
        o_w_up,
        sums[9 * half :],
        o_w_down,
        pieces[1],
        pieces[2],
        pieces[3],
        pieces[4],
        pieces[5],
    )


def solution(mesh):
    in_specs = (
        P(("dp", "row"), "col"),
        P(("dp", "row"), None),
        P(("dp", "row"), "col"),
        P("row", "col"),
        P("col"),
        P("row", "col"),
        P("row", "col"),
        P("col"),
        P("row", "col"),
        P("col"),
        P("row", "col"),
        P("col"),
        P("row", "col"),
        P("col"),
        P("col"),
        P("col"),
        P("col"),
        P("col"),
    )
    out_specs = (
        P(("dp", "row"), "col"),
        P(("dp", "row"), "col"),
        P("row", "col"),
        P("col"),
        P("row", "col"),
        P("row", "col"),
        P("col"),
        P("row", "col"),
        P("col"),
        P("row", "col"),
        P("col"),
        P("row", "col"),
        P("col"),
        P("col"),
        P("col"),
        P("col"),
        P("col"),
    )
    return jax.shard_map(body, mesh=mesh, in_specs=in_specs, out_specs=out_specs, check_vma=False)
```

```python
import jax
import jax.numpy as jnp
from jax import lax
from jax.experimental import pallas as pl
from jax.experimental.pallas import tpu as pltpu
from jax.sharding import PartitionSpec as P

HEAD_DIM = 64


EPSILON = 1e-05
SCALE = 0.125
LOG2E = 1.4426950408889634
PAIR = 2 * HEAD_DIM
Q_BLOCK = 256


def dot_nt(left, right):
    return lax.dot_general(
        left, right, (((1,), (1,)), ((), ())), preferred_element_type=jnp.float32
    )


def dot_nn(left, right):
    return lax.dot_general(
        left, right, (((1,), (0,)), ((), ())), preferred_element_type=jnp.float32
    )


def only_head(block, head):
    lane = lax.broadcasted_iota(jnp.int32, block.shape, 1)
    return jnp.where(lane // HEAD_DIM == head, block, jnp.zeros_like(block))


def attend_kernel(seg_col, seg_row, q_ref, k_ref, v_ref, ctx_ref, lse_ref, vt_ref):
    @pl.when(pl.program_id(1) == 0)
    def _():
        vt_ref[...] = v_ref[...].T

    same = seg_col[...] == seg_row[...]
    parts = []
    for head in range(2):
        scores = dot_nt(k_ref[...], only_head(q_ref[...], head)) * (SCALE * LOG2E)
        scores = jnp.where(same, scores, -1e30)
        top = jnp.max(scores, axis=0, keepdims=True)
        expo = jnp.exp2(scores - top)
        total = jnp.sum(expo, axis=0, keepdims=True)
        out = dot_nn(
            vt_ref[head * HEAD_DIM : (head + 1) * HEAD_DIM, :], expo.astype(jnp.bfloat16)
        )
        parts.append(out / total)
        lse_ref[0, head : head + 1, :] = top + jnp.log2(total)
    ctx_ref[...] = jnp.concatenate(parts, axis=0).T.astype(jnp.bfloat16)


def attend_back_kernel(
    seg_col, seg_row, q_ref, k_ref, v_ref, lse_ref, do_ref, dq_ref, dk_ref, dv_ref, kt_ref, dk_acc, dv_acc
):
    step = pl.program_id(1)

    @pl.when(step == 0)
    def _():
        kt_ref[...] = k_ref[...].T
        dk_acc[...] = jnp.zeros_like(dk_acc)
        dv_acc[...] = jnp.zeros_like(dv_acc)

    same = seg_col[...] == seg_row[...]
    parts = []
    for head in range(2):
        query = only_head(q_ref[...], head)
        grad = only_head(do_ref[...], head)
        scores = dot_nt(k_ref[...], query) * (SCALE * LOG2E)
        probs = jnp.where(same, jnp.exp2(scores - lse_ref[0, head : head + 1, :]), 0.0)
        d_probs = dot_nt(v_ref[...], grad)
        inner = jnp.sum(probs * d_probs, axis=0, keepdims=True)
        d_scores = (probs * (d_probs - inner)).astype(jnp.bfloat16)
        dv_acc[...] += dot_nn(probs.astype(jnp.bfloat16), grad)
        dk_acc[...] += dot_nn(d_scores, query)
        parts.append(
            dot_nn(kt_ref[head * HEAD_DIM : (head + 1) * HEAD_DIM, :], d_scores)
        )
    dq_ref[...] = (jnp.concatenate(parts, axis=0) * SCALE).T.astype(jnp.bfloat16)

    @pl.when(step == pl.num_programs(1) - 1)
    def _():
        dk_ref[...] = (dk_acc[...] * SCALE).astype(jnp.bfloat16)
        dv_ref[...] = dv_acc[...].astype(jnp.bfloat16)


def attention_specs(count, pairs, block):
    seg_col = pl.BlockSpec((count, 1), lambda h, i: (0, 0))
    seg_row = pl.BlockSpec((1, block), lambda h, i: (0, i))
    query = pl.BlockSpec((block, PAIR), lambda h, i: (i, h))
    key = pl.BlockSpec((count, PAIR), lambda h, i: (0, pairs + h))
    value = pl.BlockSpec((count, PAIR), lambda h, i: (0, 2 * pairs + h))
    lse = pl.BlockSpec((1, 2, block), lambda h, i: (h, 0, i))
    return seg_col, seg_row, query, key, value, lse


def attend(qkv, segment):
    count = qkv.shape[0]
    pairs = qkv.shape[1] // (3 * PAIR)
    block = min(Q_BLOCK, count)
    seg_col, seg_row, query, key, value, lse = attention_specs(count, pairs, block)
    return pl.pallas_call(
        attend_kernel,
        grid=(pairs, count // block),
        in_specs=[seg_col, seg_row, query, key, value],
        out_specs=[query, lse],
        out_shape=[
            jax.ShapeDtypeStruct((count, pairs * PAIR), jnp.bfloat16),
            jax.ShapeDtypeStruct((pairs, 2, count), jnp.float32),
        ],
        scratch_shapes=[pltpu.VMEM((PAIR, count), jnp.bfloat16)],
        compiler_params=pltpu.CompilerParams(vmem_limit_bytes=32 << 20),
        cost_estimate=pl.CostEstimate(
            flops=16 * count * count * PAIR * pairs,
            bytes_accessed=10 * count * pairs * PAIR,
            transcendentals=2 * count * count * pairs,
        ),
    )(segment.reshape(-1, 1), segment, qkv, qkv, qkv)


def attend_back(qkv, segment, lse_rows, d_context):
    count = qkv.shape[0]
    pairs = qkv.shape[1] // (3 * PAIR)
    block = min(Q_BLOCK, count)
    seg_col, seg_row, query, key, value, lse = attention_specs(count, pairs, block)
    whole = pl.BlockSpec((count, PAIR), lambda h, i: (0, h))
    shape = jax.ShapeDtypeStruct((count, pairs * PAIR), jnp.bfloat16)
    return pl.pallas_call(
        attend_back_kernel,
        grid=(pairs, count // block),
        in_specs=[seg_col, seg_row, query, key, value, lse, query],
        out_specs=[query, whole, whole],
        out_shape=[shape, shape, shape],
        scratch_shapes=[
            pltpu.VMEM((PAIR, count), jnp.bfloat16),
            pltpu.VMEM((count, PAIR), jnp.float32),
            pltpu.VMEM((count, PAIR), jnp.float32),
        ],
        compiler_params=pltpu.CompilerParams(vmem_limit_bytes=32 << 20),
        cost_estimate=pl.CostEstimate(
            flops=40 * count * count * PAIR * pairs,
            bytes_accessed=20 * count * pairs * PAIR,
            transcendentals=2 * count * count * pairs,
        ),
    )(segment.reshape(-1, 1), segment, qkv, qkv, qkv, lse_rows, d_context)


def matmul(left, right):
    return jnp.dot(left, right, preferred_element_type=jnp.float32)


def matmul_tn(left, right):
    return lax.dot_general(
        left, right, (((0,), (0,)), ((), ())), preferred_element_type=jnp.float32
    )


def matmul_nt(left, right):
    return lax.dot_general(
        left, right, (((1,), (1,)), ((), ())), preferred_element_type=jnp.float32
    )


def column_sum(values):
    return jnp.sum(values.astype(jnp.float32), axis=0)


def swapped(part):
    return lax.ppermute(part, "col", [(0, 1), (1, 0)])


def swapped_rows(part):
    other = swapped(part)
    cut = other.shape[1] // 2
    return jnp.concatenate([other[:, cut:], other[:, :cut]], axis=1).astype(jnp.float32)


def partner(part, axis, bit):
    size = lax.axis_size(axis)
    return lax.ppermute(part, axis, [(i, i ^ bit) for i in range(size)])


def shifted(part, step):
    size = lax.axis_size("row")
    return lax.ppermute(part, "row", [(i, (i + step) % size) for i in range(size)])


def after(values, earlier):
    return lax.optimization_barrier((values, earlier))[0]


def is_small_grid(rows):
    return lax.axis_size("row") == 4 and lax.axis_size("dp") == 4 and rows % 128 == 0


def place_kernel(idx, own, s1, s2, s3, near_x, near_y, far_a, far_b, out, sems):
    quarter = s1.shape[0]
    rows = own.shape[0]
    part = quarter // 2

    def at(step, corner, skip, size):
        start = idx[step] * rows + idx[4 + corner] * quarter + skip
        return out.at[pl.ds(pl.multiple_of(start, part), size), :]

    moves = [(own, out.at[pl.ds(pl.multiple_of(idx[0] * rows, rows), rows), :])]
    for step, ref in ((1, s1), (2, s2), (3, s3)):
        piece = pl.ds((step - 1) * quarter, quarter)
        moves.append((ref, at(step, 0, 0, quarter)))
        moves.append((near_x.at[piece, :], at(step, 1, 0, quarter)))
        moves.append((near_y.at[piece, :], at(step, 2, 0, quarter)))
    moves.append((far_a.at[pl.ds(0, quarter), :], at(1, 3, 0, quarter)))
    moves.append((far_a.at[pl.ds(quarter, part), :], at(2, 3, 0, part)))
    moves.append((far_b.at[pl.ds(0, part), :], at(2, 3, part, part)))
    moves.append((far_b.at[pl.ds(part, quarter), :], at(3, 3, 0, quarter)))
    copies = [
        pltpu.make_async_copy(source, target, sems.at[i])
        for i, (source, target) in enumerate(moves)
    ]
    for copy in copies:
        copy.start()
    for copy in copies:
        copy.wait()


def place(idx, own, *pieces):
    rows, width = own.shape
    return pl.pallas_call(
        place_kernel,
        in_specs=[pl.BlockSpec(memory_space=pltpu.SMEM)]
        + [pl.BlockSpec(memory_space=pl.ANY)] * 8,
        out_specs=pl.BlockSpec(memory_space=pl.ANY),
        out_shape=jax.ShapeDtypeStruct((4 * rows, width), own.dtype),
        scratch_shapes=[pltpu.SemaphoreType.DMA((14,))],
        cost_estimate=pl.CostEstimate(
            flops=0, bytes_accessed=8 * rows * width * 2, transcendentals=0
        ),
    )(idx, own, *pieces)


def whole_weights(blocks):
    core, corner = lax.axis_index("col"), lax.axis_index("dp")
    size = lax.axis_size("row")
    if not all(is_small_grid(block.shape[0]) for block in blocks):
        wholes = []
        for block in blocks:
            rows = block.shape[0] // lax.axis_size("dp")
            part = lax.dynamic_slice_in_dim(block, corner * rows, rows, 0)
            full = lax.all_gather(part, ("row", "dp"), axis=0, tiled=True)
            cut = full.shape[0] // 2
            wholes.append(
                jnp.where(core == 0, full, jnp.concatenate([full[cut:], full[:cut]], axis=0))
            )
        return wholes
    place_z = (lax.axis_index("row") + size // 2 * core + size - jnp.arange(size)) % size
    idx = jnp.concatenate([place_z, corner ^ jnp.arange(4)]).astype(jnp.int32)
    wholes = []
    earlier_z = earlier_xy = None
    for block in blocks:
        quarter = block.shape[0] // 4
        part = lax.dynamic_slice_in_dim(block, corner * quarter, quarter, 0)
        if earlier_z is not None:
            part = after(part, earlier_z)
        ring = [shifted(part, step) for step in (1, 2, 3)]
        earlier_z = ring[0]
        stack = jnp.concatenate(ring, axis=0)
        if earlier_xy is not None:
            stack = after(stack, earlier_xy)
        near_x = partner(stack, "dp", 1)
        near_y = partner(stack, "dp", 2)
        cut = stack.shape[0] // 2
        far_a = partner(near_y[:cut], "dp", 1)
        far_b = partner(near_x[cut:], "dp", 2)
        earlier_xy = near_x
        wholes.append(place(idx, block, *ring, near_x, near_y, far_a, far_b))
    return wholes


def pick(values, axis, index):
    return lax.dynamic_index_in_dim(values, index, axis, keepdims=False)


def added(*parts):
    total = parts[0].astype(jnp.float32)
    for part in parts[1:]:
        total = total + part.astype(jnp.float32)
    return total.astype(jnp.bfloat16)


def reduced_weight(grad):
    core, corner, level = lax.axis_index("col"), lax.axis_index("dp"), lax.axis_index("row")
    size = lax.axis_size("row")
    if not is_small_grid(grad.shape[0] // size):
        cut = grad.shape[0] // 2
        grad = jnp.where(core == 0, grad, jnp.concatenate([grad[cut:], grad[:cut]], axis=0))
        part = lax.psum_scatter(grad, ("row", "dp"), scatter_dimension=0, tiled=True)
        return lax.all_gather(part, "dp", axis=0, tiled=True).astype(jnp.float32)
    a, b = corner // 2, corner % 2
    width = grad.shape[1]
    six = grad.reshape(2, 2, 2, 2, -1, width)
    first, second = six[0], six[1]
    got_first = partner(pick(first, 2, 1 - b), "dp", 1)
    got_second = partner(pick(second, 1, 1 - a), "dp", 2)
    send_first = added(pick(pick(first, 2, b), 1, 1 - a), pick(got_first, 1, 1 - a))
    send_second = added(pick(pick(second, 1, a), 1, 1 - b), pick(got_second, 1, 1 - b))
    far_first = partner(send_first, "dp", 2)
    far_second = partner(send_second, "dp", 1)
    keep_first = added(pick(pick(first, 2, b), 1, a), pick(got_first, 1, a), far_first)
    keep_second = added(pick(pick(second, 1, a), 1, b), pick(got_second, 1, b), far_second)
    levels = jnp.concatenate([keep_first, keep_second], axis=0)

    def of_level(index):
        return pick(levels, 0, (index + size // 2 * core) % size)

    total = added(
        of_level(level), *[shifted(of_level((level + step) % size), step) for step in (1, 2, 3)]
    )
    others = [total] + [partner(total, "dp", bit) for bit in (1, 2, 3)]
    return jnp.concatenate(
        [
            jnp.where(
                a == 0,
                jnp.where(b == 0, others[k], others[k ^ 1]),
                jnp.where(b == 0, others[k ^ 2], others[k ^ 3]),
            )
            for k in range(4)
        ],
        axis=0,
    ).astype(jnp.float32)


def reduced_vector(values):
    values = values.reshape(-1, 128)
    if not is_small_grid(128):
        return lax.psum(values, ("row", "dp")).reshape(-1)
    for axis in ("dp", "row"):
        for bit in (1, 2):
            values = values + partner(values, axis, bit)
    return values.reshape(-1)


def norm_forward(resid, gain, shift):
    center = jnp.mean(resid, axis=1, keepdims=True)
    inverse = lax.rsqrt(
        jnp.mean(resid * resid, axis=1, keepdims=True) - center * center + EPSILON
    )
    normed = (resid - center) * inverse
    return (normed * gain + shift, normed, inverse)


def norm_backward(grad, normed, inverse, gain):
    scaled = grad * gain
    first = jnp.mean(scaled, axis=1, keepdims=True)
    second = jnp.mean(scaled * normed, axis=1, keepdims=True)
    return inverse * (scaled - first - normed * second)


def body(
    tokens,
    segment,
    cotangent,
    w_query,
    b_query,
    w_key,
    w_value,
    b_value,
    w_out,
    b_out,
    w_up,
    b_up,
    w_down,
    b_down,
    gain_one,
    shift_one,
    gain_two,
    shift_two,
):
    half = w_query.shape[1]
    token_rows = jnp.concatenate([tokens, swapped(tokens)], axis=1)
    w_qkv, wo_half, wu, wd_half = whole_weights(
        [jnp.concatenate([w_query, w_key, w_value], axis=1), w_out, w_up, w_down]
    )
    cotangent_rows = jnp.concatenate([cotangent, swapped(cotangent)], axis=1)
    own_vectors = jnp.stack([b_out, b_down, gain_one, shift_one, gain_two, shift_two])
    vectors = jnp.concatenate([own_vectors, swapped(own_vectors)], axis=1).astype(jnp.float32)
    bias_out, bias_down, gain1, shift1, gain2, shift2 = [vectors[i] for i in range(6)]
    wo_other = swapped(wo_half)
    wo = jnp.concatenate(
        [wo_half, jnp.concatenate([wo_other[half:], wo_other[:half]], axis=0)], axis=1
    )
    units = w_up.shape[1]
    wd = jnp.concatenate([wd_half[:units], swapped(wd_half[units:])], axis=1)

    b_qkv = jnp.concatenate([b_query, jnp.zeros_like(b_query), b_value]).astype(jnp.float32)
    qkv = (matmul(token_rows, w_qkv) + b_qkv).astype(jnp.bfloat16)
    context, lse_rows = attend(qkv, segment)
    context_rows = jnp.concatenate([context, swapped(context)], axis=1)
    first_sum = token_rows.astype(jnp.float32) + (matmul(context_rows, wo) + bias_out)
    hidden_f, normed_one, inverse_one = norm_forward(first_sum, gain1, shift1)
    hidden = hidden_f.astype(jnp.bfloat16)
    pre_act = matmul(hidden, wu) + b_up.astype(jnp.float32)
    cdf = 0.5 * (1.0 + lax.erf(pre_act * (0.5**0.5)))
    activated = (pre_act * cdf).astype(jnp.bfloat16)
    slope = cdf + pre_act * (jnp.exp(-0.5 * pre_act * pre_act) * 0.3989422804014327)
    part = matmul(activated, wd).astype(jnp.bfloat16)
    ffn_out = part.astype(jnp.float32) + swapped_rows(part) + bias_down
    second_sum = hidden.astype(jnp.float32) + ffn_out
    final, normed_two, inverse_two = norm_forward(second_sum, gain2, shift2)
    output = final[:, :half].astype(jnp.bfloat16)
    y = cotangent_rows.astype(jnp.float32)
    second_grad = norm_backward(y, normed_two, inverse_two, gain2)
    d_gain_two = jnp.sum(y * normed_two, axis=0)
    d_shift_two = jnp.sum(y, axis=0)
    ffn_grad = second_grad.astype(jnp.bfloat16)
    d_w_down = matmul_tn(activated, ffn_grad).astype(jnp.bfloat16)
    o_w_down = reduced_weight(
        jnp.concatenate([d_w_down[:, :half], swapped(d_w_down[:, half:])], axis=0)
    )
    d_b_down = column_sum(ffn_grad)
    pre_grad = (matmul_nt(ffn_grad, wd) * slope).astype(jnp.bfloat16)
    o_w_up = reduced_weight(matmul_tn(hidden, pre_grad).astype(jnp.bfloat16))
    d_b_up = column_sum(pre_grad)
    hidden_part = matmul_nt(pre_grad, wu).astype(jnp.bfloat16)
    hidden_grad = second_grad + (
        hidden_part.astype(jnp.float32) + swapped_rows(hidden_part)
    )
    first_grad = norm_backward(hidden_grad, normed_one, inverse_one, gain1)
    d_gain_one = jnp.sum(hidden_grad * normed_one, axis=0)
    d_shift_one = jnp.sum(hidden_grad, axis=0)
    branch_grad = first_grad.astype(jnp.bfloat16)
    o_w_out = reduced_weight(matmul_tn(context_rows, branch_grad[:, :half]).astype(jnp.bfloat16))
    d_b_out = column_sum(branch_grad)
    wide = jnp.stack([d_b_out, d_b_down, d_gain_one, d_shift_one, d_gain_two, d_shift_two])
    sums = reduced_vector(jnp.concatenate([wide[:, :half].reshape(-1), d_b_up]))
    context_grad = matmul_nt(branch_grad, wo[:half]).astype(jnp.bfloat16)
    qkv_grad = jnp.concatenate(attend_back(qkv, segment, lse_rows, context_grad), axis=1)
    o_w_qkv = reduced_weight(matmul_tn(token_rows, qkv_grad).astype(jnp.bfloat16))
    d_b_qkv = column_sum(qkv_grad)
    d_b_qv = reduced_vector(jnp.concatenate([d_b_qkv[:half], d_b_qkv[2 * half :]]))
    token_part = matmul_nt(qkv_grad, w_qkv).astype(jnp.bfloat16)
    token_sum = token_part[:, :half].astype(jnp.float32) + swapped(
        token_part[:, half:]
    ).astype(jnp.float32)
    d_tokens = (token_sum + first_grad[:, :half]).astype(jnp.bfloat16)
    pieces = [sums[i * half : (i + 1) * half] for i in range(6)]
    return (
        output,
        d_tokens,
        o_w_qkv[:, :half],
        d_b_qv[:half],
        o_w_qkv[:, half : 2 * half],
        o_w_qkv[:, 2 * half :],
        d_b_qv[half:],
        o_w_out,
        pieces[0],
        o_w_up,
        sums[6 * half :],
        o_w_down,
        pieces[1],
        pieces[2],
        pieces[3],
        pieces[4],
        pieces[5],
    )


def solution(mesh):
    in_specs = (
        P(("dp", "row"), "col"),
        P(("dp", "row"), None),
        P(("dp", "row"), "col"),
        P("row", "col"),
        P("col"),
        P("row", "col"),
        P("row", "col"),
        P("col"),
        P("row", "col"),
        P("col"),
        P("row", "col"),
        P("col"),
        P("row", "col"),
        P("col"),
        P("col"),
        P("col"),
        P("col"),
        P("col"),
    )
    out_specs = (
        P(("dp", "row"), "col"),
        P(("dp", "row"), "col"),
        P("row", "col"),
        P("col"),
        P("row", "col"),
        P("row", "col"),
        P("col"),
        P("row", "col"),
        P("col"),
        P("row", "col"),
        P("col"),
        P("row", "col"),
        P("col"),
        P("col"),
        P("col"),
        P("col"),
        P("col"),
    )
    return jax.shard_map(body, mesh=mesh, in_specs=in_specs, out_specs=out_specs, check_vma=False)
```

```python
import jax
import jax.numpy as jnp
from jax import lax
from jax.experimental import pallas as pl
from jax.experimental.pallas import tpu as pltpu
from jax.sharding import PartitionSpec as P

HEAD_DIM = 64


EPSILON = 1e-05
SCALE = 0.125
LOG2E = 1.4426950408889634
PAIR = 2 * HEAD_DIM
Q_BLOCK = 256


def dot_nt(left, right):
    return lax.dot_general(
        left, right, (((1,), (1,)), ((), ())), preferred_element_type=jnp.float32
    )


def dot_nn(left, right):
    return lax.dot_general(
        left, right, (((1,), (0,)), ((), ())), preferred_element_type=jnp.float32
    )


def only_head(block, head):
    lane = lax.broadcasted_iota(jnp.int32, block.shape, 1)
    return jnp.where(lane // HEAD_DIM == head, block, jnp.zeros_like(block))


def attend_kernel(seg_col, seg_row, q_ref, k_ref, v_ref, ctx_ref, lse_ref, vt_ref):
    @pl.when(pl.program_id(1) == 0)
    def _():
        vt_ref[...] = v_ref[...].T

    same = seg_col[...] == seg_row[...]
    parts = []
    for head in range(2):
        scores = dot_nt(k_ref[...], only_head(q_ref[...], head)) * (SCALE * LOG2E)
        scores = jnp.where(same, scores, -1e30)
        top = jnp.max(scores, axis=0, keepdims=True)
        expo = jnp.exp2(scores - top)
        total = jnp.sum(expo, axis=0, keepdims=True)
        out = dot_nn(
            vt_ref[head * HEAD_DIM : (head + 1) * HEAD_DIM, :], expo.astype(jnp.bfloat16)
        )
        parts.append(out / total)
        lse_ref[0, head : head + 1, :] = top + jnp.log2(total)
    ctx_ref[...] = jnp.concatenate(parts, axis=0).T.astype(jnp.bfloat16)


def attend_back_kernel(
    seg_col, seg_row, q_ref, k_ref, v_ref, lse_ref, do_ref, dq_ref, dk_ref, dv_ref, kt_ref, dk_acc, dv_acc
):
    step = pl.program_id(1)

    @pl.when(step == 0)
    def _():
        kt_ref[...] = k_ref[...].T
        dk_acc[...] = jnp.zeros_like(dk_acc)
        dv_acc[...] = jnp.zeros_like(dv_acc)

    same = seg_col[...] == seg_row[...]
    parts = []
    for head in range(2):
        query = only_head(q_ref[...], head)
        grad = only_head(do_ref[...], head)
        scores = dot_nt(k_ref[...], query) * (SCALE * LOG2E)
        probs = jnp.where(same, jnp.exp2(scores - lse_ref[0, head : head + 1, :]), 0.0)
        d_probs = dot_nt(v_ref[...], grad)
        inner = jnp.sum(probs * d_probs, axis=0, keepdims=True)
        d_scores = (probs * (d_probs - inner)).astype(jnp.bfloat16)
        dv_acc[...] += dot_nn(probs.astype(jnp.bfloat16), grad)
        dk_acc[...] += dot_nn(d_scores, query)
        parts.append(
            dot_nn(kt_ref[head * HEAD_DIM : (head + 1) * HEAD_DIM, :], d_scores)
        )
    dq_ref[...] = (jnp.concatenate(parts, axis=0) * SCALE).T.astype(jnp.bfloat16)

    @pl.when(step == pl.num_programs(1) - 1)
    def _():
        dk_ref[...] = (dk_acc[...] * SCALE).astype(jnp.bfloat16)
        dv_ref[...] = dv_acc[...].astype(jnp.bfloat16)


def attention_specs(count, pairs, block, skip=0):
    seg_col = pl.BlockSpec((count, 1), lambda h, i: (0, 0))
    seg_row = pl.BlockSpec((1, block), lambda h, i: (0, i))
    query = pl.BlockSpec((block, PAIR), lambda h, i: (i, skip + h))
    key = pl.BlockSpec((count, PAIR), lambda h, i: (0, pairs + skip + h))
    value = pl.BlockSpec((count, PAIR), lambda h, i: (0, 2 * pairs + skip + h))
    lse = pl.BlockSpec((1, 2, block), lambda h, i: (skip + h, 0, i))
    return seg_col, seg_row, query, key, value, lse


def attend(qkv, segment):
    count = qkv.shape[0]
    pairs = qkv.shape[1] // (3 * PAIR)
    block = min(Q_BLOCK, count)
    seg_col, seg_row, query, key, value, lse = attention_specs(count, pairs, block)
    return pl.pallas_call(
        attend_kernel,
        grid=(pairs, count // block),
        in_specs=[seg_col, seg_row, query, key, value],
        out_specs=[query, lse],
        out_shape=[
            jax.ShapeDtypeStruct((count, pairs * PAIR), jnp.bfloat16),
            jax.ShapeDtypeStruct((pairs, 2, count), jnp.float32),
        ],
        scratch_shapes=[pltpu.VMEM((PAIR, count), jnp.bfloat16)],
        compiler_params=pltpu.CompilerParams(vmem_limit_bytes=32 << 20),
        cost_estimate=pl.CostEstimate(
            flops=16 * count * count * PAIR * pairs,
            bytes_accessed=10 * count * pairs * PAIR,
            transcendentals=2 * count * count * pairs,
        ),
    )(segment.reshape(-1, 1), segment, qkv, qkv, qkv)


def attend_back(qkv, segment, lse_rows, d_context, turn, turns):
    count = qkv.shape[0]
    pairs = qkv.shape[1] // (3 * PAIR)
    here = pairs // turns
    block = min(Q_BLOCK, count)
    seg_col, seg_row, query, key, value, lse = attention_specs(count, pairs, block, turn * here)
    d_query = pl.BlockSpec((block, PAIR), lambda h, i: (i, h))
    d_whole = pl.BlockSpec((count, PAIR), lambda h, i: (0, h))
    shape = jax.ShapeDtypeStruct((count, here * PAIR), jnp.bfloat16)
    return pl.pallas_call(
        attend_back_kernel,
        grid=(here, count // block),
        in_specs=[seg_col, seg_row, query, key, value, lse, query],
        out_specs=[d_query, d_whole, d_whole],
        out_shape=[shape, shape, shape],
        scratch_shapes=[
            pltpu.VMEM((PAIR, count), jnp.bfloat16),
            pltpu.VMEM((count, PAIR), jnp.float32),
            pltpu.VMEM((count, PAIR), jnp.float32),
        ],
        compiler_params=pltpu.CompilerParams(vmem_limit_bytes=32 << 20),
        cost_estimate=pl.CostEstimate(
            flops=40 * count * count * PAIR * here,
            bytes_accessed=20 * count * here * PAIR,
            transcendentals=2 * count * count * here,
        ),
    )(segment.reshape(-1, 1), segment, qkv, qkv, qkv, lse_rows, d_context)


def matmul(left, right):
    return jnp.dot(left, right, preferred_element_type=jnp.float32)


def matmul_tn(left, right):
    return lax.dot_general(
        left, right, (((0,), (0,)), ((), ())), preferred_element_type=jnp.float32
    )


def matmul_nt(left, right):
    return lax.dot_general(
        left, right, (((1,), (1,)), ((), ())), preferred_element_type=jnp.float32
    )


def column_sum(values):
    return jnp.sum(values.astype(jnp.float32), axis=0)


def swapped(part):
    return lax.ppermute(part, "col", [(0, 1), (1, 0)])


def swapped_rows(part):
    other = swapped(part)
    cut = other.shape[1] // 2
    return jnp.concatenate([other[:, cut:], other[:, :cut]], axis=1).astype(jnp.float32)


def partner(part, axis, bit):
    size = lax.axis_size(axis)
    return lax.ppermute(part, axis, [(i, i ^ bit) for i in range(size)])


def shifted(part, step):
    size = lax.axis_size("row")
    return lax.ppermute(part, "row", [(i, (i + step) % size) for i in range(size)])


def after(values, earlier):
    return lax.optimization_barrier((values, earlier))[0]


def is_small_grid(rows):
    return lax.axis_size("row") == 4 and lax.axis_size("dp") == 4 and rows % 128 == 0


def place_kernel(idx, own, ring, near_x, near_y, far_a, far_b, *outs):
    step = pl.program_id(0)
    quarter = ring.shape[0]
    part = quarter // 2
    begin = 0
    for out in outs:
        columns = slice(begin, begin + out.shape[1])
        begin = begin + out.shape[1]

        def put(corner, skip, value):
            start = pl.multiple_of(idx[4 + corner] * quarter + skip, part)
            out[pl.ds(start, value.shape[0]), :] = value

        @pl.when(step == 0)
        def _():
            out[...] = own[:, columns]

        @pl.when(step > 0)
        def _():
            put(0, 0, ring[:, columns])
            put(1, 0, near_x[:, columns])
            put(2, 0, near_y[:, columns])

        @pl.when(step == 1)
        def _():
            put(3, 0, far_a[:quarter, columns])

        @pl.when(step == 2)
        def _():
            put(3, 0, far_a[quarter:, columns])
            put(3, part, far_b[:part, columns])

        @pl.when(step == 3)
        def _():
            put(3, 0, far_b[part:, columns])


def place(idx, own, ring, near_x, near_y, far_a, far_b, widths):
    rows, width = own.shape
    fixed = [pl.BlockSpec(part.shape, lambda s, idx: (0, 0)) for part in (own, far_a, far_b)]
    moving = pl.BlockSpec((rows // 4, width), lambda s, idx: (jnp.maximum(s - 1, 0), 0))
    return pl.pallas_call(
        place_kernel,
        grid_spec=pltpu.PrefetchScalarGridSpec(
            num_scalar_prefetch=1,
            grid=(4,),
            in_specs=[fixed[0], moving, moving, moving, fixed[1], fixed[2]],
            out_specs=[pl.BlockSpec((rows, w), lambda s, idx: (idx[s], 0)) for w in widths],
        ),
        out_shape=[jax.ShapeDtypeStruct((4 * rows, w), own.dtype) for w in widths],
        compiler_params=pltpu.CompilerParams(vmem_limit_bytes=40 << 20),
        cost_estimate=pl.CostEstimate(
            flops=0, bytes_accessed=8 * rows * width * 2, transcendentals=0
        ),
    )(idx, own, ring, near_x, near_y, far_a, far_b)


def natural_order(whole):
    cut = whole.shape[0] // 2
    return jnp.where(
        lax.axis_index("col") == 0, whole, jnp.concatenate([whole[cut:], whole[:cut]], axis=0)
    )


def gathered(block):
    rows = block.shape[0] // lax.axis_size("dp")
    part = lax.dynamic_slice_in_dim(block, lax.axis_index("dp") * rows, rows, 0)
    return natural_order(lax.all_gather(part, ("row", "dp"), axis=0, tiled=True))


def whole_weights(groups):
    core, corner = lax.axis_index("col"), lax.axis_index("dp")
    size = lax.axis_size("row")
    if not all(is_small_grid(block.shape[0]) for group in groups for block in group):
        return [[gathered(block) for block in group] for group in groups]
    place_z = (lax.axis_index("row") + size // 2 * core + size - jnp.arange(size)) % size
    idx = jnp.concatenate([place_z, corner ^ jnp.arange(4)]).astype(jnp.int32)
    owns = [jnp.concatenate(group, axis=1) if len(group) > 1 else group[0] for group in groups]
    stacks = []
    for own in owns:
        quarter = own.shape[0] // 4
        part = lax.dynamic_slice_in_dim(own, corner * quarter, quarter, 0)
        if stacks:
            part = after(part, stacks[-1])
        stacks.append(
            jnp.concatenate([shifted(part, step) for step in (1, 2, 3)], axis=0)
        )
    wholes = []
    earlier = None
    for own, stack, group in zip(owns, stacks, groups):
        if earlier is not None:
            stack = after(stack, earlier)
        near_x = partner(stack, "dp", 1)
        near_y = partner(stack, "dp", 2)
        cut = stack.shape[0] // 2
        far_a = partner(near_y[:cut], "dp", 1)
        far_b = partner(near_x[cut:], "dp", 2)
        earlier = (far_a, far_b)
        widths = [block.shape[1] for block in group]
        wholes.append(place(idx, own, stack, near_x, near_y, far_a, far_b, widths))
    return wholes


def pick(values, axis, index):
    return lax.dynamic_index_in_dim(values, index, axis, keepdims=False)


def added(*parts):
    total = parts[0].astype(jnp.float32)
    for part in parts[1:]:
        total = total + part.astype(jnp.float32)
    return total.astype(jnp.bfloat16)


class Reduction:
    def __init__(self, first, second):
        corner = lax.axis_index("dp")
        self.a, self.b = corner // 2, corner % 2
        self.direct = not is_small_grid(2 * first.shape[0] // lax.axis_size("row"))
        self.step = 0
        if self.direct:
            self.whole = jnp.concatenate([first, second], axis=0)
        else:
            width = first.shape[1]
            self.first = first.reshape(2, 2, 2, -1, width)
            self.second = second.reshape(2, 2, 2, -1, width)

    def sends(self):
        if self.direct:
            return []
        a, b = self.a, self.b
        if self.step == 0:
            return [pick(self.first, 2, 1 - b), pick(self.second, 1, 1 - a)]
        if self.step == 1:
            one, two = self.got
            self.keep = (
                pick(pick(self.first, 2, b), 1, a),
                pick(one, 1, a),
                pick(pick(self.second, 1, a), 1, b),
                pick(two, 1, b),
            )
            return [
                added(pick(pick(self.first, 2, b), 1, 1 - a), pick(one, 1, 1 - a)),
                added(pick(pick(self.second, 1, a), 1, 1 - b), pick(two, 1, 1 - b)),
            ]
        if self.step == 2:
            levels = jnp.concatenate(
                [added(*self.keep[:2], self.got[0]), added(*self.keep[2:], self.got[1])], axis=0
            )
            size = lax.axis_size("row")
            place_z = lax.axis_index("row") + size // 2 * lax.axis_index("col")
            parts = [pick(levels, 0, (place_z + step) % size) for step in range(4)]
            self.mine = parts[0]
            return parts[1:]
        self.total = added(self.mine, *self.got)
        return [self.total]

    def go(self, sends):
        if self.direct:
            return
        if self.step == 0:
            self.got = [partner(sends[0], "dp", 1), partner(sends[1], "dp", 2)]
        elif self.step == 1:
            self.got = [partner(sends[0], "dp", 2), partner(sends[1], "dp", 1)]
        elif self.step == 2:
            self.got = [shifted(part, step) for part, step in zip(sends, (1, 2, 3))]
        else:
            self.got = [sends[0]] + [partner(sends[0], "dp", bit) for bit in (1, 2, 3)]
        self.step = self.step + 1

    def advance(self, values=None):
        sends = self.sends()
        if values is not None:
            values, *sends = lax.optimization_barrier((values, *sends))
        self.go(sends)
        return values

    def result(self):
        if self.direct:
            whole = natural_order(self.whole)
            part = lax.psum_scatter(whole, ("row", "dp"), scatter_dimension=0, tiled=True)
            return lax.all_gather(part, "dp", axis=0, tiled=True).astype(jnp.float32)
        while self.step < 4:
            self.advance()
        got = self.got
        return jnp.concatenate(
            [
                jnp.where(
                    self.a == 0,
                    jnp.where(self.b == 0, got[k], got[k ^ 1]),
                    jnp.where(self.b == 0, got[k ^ 2], got[k ^ 3]),
                )
                for k in range(4)
            ],
            axis=0,
        ).astype(jnp.float32)


def reduced_vector(values):
    values = values.reshape(-1, 128)
    if not is_small_grid(128):
        return lax.psum(values, ("row", "dp")).reshape(-1)
    for axis in ("dp", "row"):
        for bit in (1, 2):
            values = values + partner(values, axis, bit)
    return values.reshape(-1)


def norm_forward(resid, gain, shift):
    center = jnp.mean(resid, axis=1, keepdims=True)
    inverse = lax.rsqrt(
        jnp.mean(resid * resid, axis=1, keepdims=True) - center * center + EPSILON
    )
    normed = (resid - center) * inverse
    return (normed * gain + shift, normed, inverse)


def norm_backward(grad, normed, inverse, gain):
    scaled = grad * gain
    first = jnp.mean(scaled, axis=1, keepdims=True)
    second = jnp.mean(scaled * normed, axis=1, keepdims=True)
    return inverse * (scaled - first - normed * second)


def body(
    tokens,
    segment,
    cotangent,
    w_query,
    b_query,
    w_key,
    w_value,
    b_value,
    w_out,
    b_out,
    w_up,
    b_up,
    w_down,
    b_down,
    gain_one,
    shift_one,
    gain_two,
    shift_two,
):
    half = w_query.shape[1]
    token_rows = jnp.concatenate([tokens, swapped(tokens)], axis=1)
    (w_qkv,), (wo_half, wu), (wd_half,) = whole_weights(
        [[jnp.concatenate([w_query, w_key, w_value], axis=1)], [w_out, w_up], [w_down]]
    )
    cotangent_rows = jnp.concatenate([cotangent, swapped(cotangent)], axis=1)
    own_vectors = jnp.stack([b_out, b_down, gain_one, shift_one, gain_two, shift_two])
    vectors = jnp.concatenate([own_vectors, swapped(own_vectors)], axis=1).astype(jnp.float32)
    bias_out, bias_down, gain1, shift1, gain2, shift2 = [vectors[i] for i in range(6)]
    wo_other = swapped(wo_half)
    wo = jnp.concatenate(
        [wo_half, jnp.concatenate([wo_other[half:], wo_other[:half]], axis=0)], axis=1
    )
    units = w_up.shape[1]
    wd = jnp.concatenate([wd_half[:units], swapped(wd_half[units:])], axis=1)

    b_qkv = jnp.concatenate([b_query, jnp.zeros_like(b_query), b_value]).astype(jnp.float32)
    qkv = (matmul(token_rows, w_qkv) + b_qkv).astype(jnp.bfloat16)
    context, lse_rows = attend(qkv, segment)
    context_rows = jnp.concatenate([context, swapped(context)], axis=1)
    first_sum = token_rows.astype(jnp.float32) + (matmul(context_rows, wo) + bias_out)
    hidden_f, normed_one, inverse_one = norm_forward(first_sum, gain1, shift1)
    hidden = hidden_f.astype(jnp.bfloat16)
    pre_act = matmul(hidden, wu) + b_up.astype(jnp.float32)
    cdf = 0.5 * (1.0 + lax.erf(pre_act * (0.5**0.5)))
    activated = (pre_act * cdf).astype(jnp.bfloat16)
    slope = cdf + pre_act * (jnp.exp(-0.5 * pre_act * pre_act) * 0.3989422804014327)
    part = matmul(activated, wd).astype(jnp.bfloat16)
    ffn_out = part.astype(jnp.float32) + swapped_rows(part) + bias_down
    second_sum = hidden.astype(jnp.float32) + ffn_out
    final, normed_two, inverse_two = norm_forward(second_sum, gain2, shift2)
    output = final[:, :half].astype(jnp.bfloat16)
    y = cotangent_rows.astype(jnp.float32)
    second_grad = norm_backward(y, normed_two, inverse_two, gain2)
    d_gain_two = jnp.sum(y * normed_two, axis=0)
    d_shift_two = jnp.sum(y, axis=0)
    ffn_grad = second_grad.astype(jnp.bfloat16)
    d_down_other = swapped(matmul_tn(activated, ffn_grad[:, half:]).astype(jnp.bfloat16))
    d_down_own = matmul_tn(activated, ffn_grad[:, :half]).astype(jnp.bfloat16)
    d_b_down = column_sum(ffn_grad)
    pre_grad = (matmul_nt(ffn_grad, wd) * slope).astype(jnp.bfloat16)
    d_b_up = column_sum(pre_grad)
    down = Reduction(d_down_own, d_down_other)
    pre_grad = down.advance(pre_grad)
    hidden_part = matmul_nt(pre_grad, wu).astype(jnp.bfloat16)
    hidden_other = swapped_rows(hidden_part)
    d_w_up = matmul_tn(hidden, pre_grad).astype(jnp.bfloat16)
    up = Reduction(d_w_up[:half], d_w_up[half:])
    hidden_part = up.advance(hidden_part)
    hidden_grad = second_grad + (hidden_part.astype(jnp.float32) + hidden_other)
    first_grad = norm_backward(hidden_grad, normed_one, inverse_one, gain1)
    d_gain_one = jnp.sum(hidden_grad * normed_one, axis=0)
    d_shift_one = jnp.sum(hidden_grad, axis=0)
    branch_grad = first_grad.astype(jnp.bfloat16)
    branch_grad = down.advance(branch_grad)
    d_b_out = column_sum(branch_grad)
    wide = jnp.stack([d_b_out, d_b_down, d_gain_one, d_shift_one, d_gain_two, d_shift_two])
    context_grad = matmul_nt(branch_grad, wo[:half]).astype(jnp.bfloat16)
    d_w_out = matmul_tn(context_rows, branch_grad[:, :half]).astype(jnp.bfloat16)
    out = Reduction(d_w_out[:half], d_w_out[half:])
    context_grad = out.advance(context_grad)
    grads = list(attend_back(qkv, segment, lse_rows, context_grad, 0, 2))
    grads[0] = up.advance(grads[0])
    context_grad = down.advance(lax.optimization_barrier((context_grad, *grads))[0])
    grads_more = attend_back(qkv, segment, lse_rows, context_grad, 1, 2)
    qkv_grad = jnp.concatenate(
        [part for pair in zip(grads, grads_more) for part in pair], axis=1
    )
    qkv_grad = up.advance(qkv_grad)
    qkv_grad = out.advance(qkv_grad)
    d_w_qkv = matmul_tn(token_rows, qkv_grad).astype(jnp.bfloat16)
    w_qkv_grad = Reduction(d_w_qkv[:half], d_w_qkv[half:])
    qkv_grad = w_qkv_grad.advance(qkv_grad)
    token_part = matmul_nt(qkv_grad, w_qkv).astype(jnp.bfloat16)
    token_other = swapped(token_part[:, half:])
    token_part = down.advance(token_part)
    d_b_qkv = column_sum(qkv_grad)
    token_sum = token_part[:, :half].astype(jnp.float32) + token_other.astype(jnp.float32)
    d_tokens = (token_sum + first_grad[:, :half]).astype(jnp.bfloat16)
    sums = reduced_vector(jnp.concatenate([wide[:, :half].reshape(-1), d_b_up]))
    d_b_qv = reduced_vector(jnp.concatenate([d_b_qkv[:half], d_b_qkv[2 * half :]]))
    o_w_down, o_w_up, o_w_out = down.result(), up.result(), out.result()
    o_w_qkv = w_qkv_grad.result()
    pieces = [sums[i * half : (i + 1) * half] for i in range(6)]
    return (
        output,
        d_tokens,
        o_w_qkv[:, :half],
        d_b_qv[:half],
        o_w_qkv[:, half : 2 * half],
        o_w_qkv[:, 2 * half :],
        d_b_qv[half:],
        o_w_out,
        pieces[0],
        o_w_up,
        sums[6 * half :],
        o_w_down,
        pieces[1],
        pieces[2],
        pieces[3],
        pieces[4],
        pieces[5],
    )


def solution(mesh):
    in_specs = (
        P(("dp", "row"), "col"),
        P(("dp", "row"), None),
        P(("dp", "row"), "col"),
        P("row", "col"),
        P("col"),
        P("row", "col"),
        P("row", "col"),
        P("col"),
        P("row", "col"),
        P("col"),
        P("row", "col"),
        P("col"),
        P("row", "col"),
        P("col"),
        P("col"),
        P("col"),
        P("col"),
        P("col"),
    )
    out_specs = (
        P(("dp", "row"), "col"),
        P(("dp", "row"), "col"),
        P("row", "col"),
        P("col"),
        P("row", "col"),
        P("row", "col"),
        P("col"),
        P("row", "col"),
        P("col"),
        P("row", "col"),
        P("col"),
        P("row", "col"),
        P("col"),
        P("col"),
        P("col"),
        P("col"),
        P("col"),
    )
    return jax.shard_map(body, mesh=mesh, in_specs=in_specs, out_specs=out_specs, check_vma=False)
```

```python
import jax
import jax.numpy as jnp
from jax import lax
from jax.experimental import pallas as pl
from jax.experimental.pallas import tpu as pltpu
from jax.sharding import PartitionSpec as P

HEAD_DIM = 64


EPSILON = 1e-05
SCALE = 0.125
LOG2E = 1.4426950408889634
PAIR = 2 * HEAD_DIM
Q_BLOCK = 256
NO_COST = pl.CostEstimate(flops=0, bytes_accessed=0, transcendentals=0)


def dot_nt(left, right):
    return lax.dot_general(
        left, right, (((1,), (1,)), ((), ())), preferred_element_type=jnp.float32
    )


def dot_nn(left, right):
    return lax.dot_general(
        left, right, (((1,), (0,)), ((), ())), preferred_element_type=jnp.float32
    )


def only_head(block, head):
    lane = lax.broadcasted_iota(jnp.int32, block.shape, 1)
    return jnp.where(lane // HEAD_DIM == head, block, jnp.zeros_like(block))


def attend_kernel(seg_col, seg_row, q_ref, k_ref, v_ref, ctx_ref, lse_ref, vt_ref):
    @pl.when(pl.program_id(1) == 0)
    def _():
        vt_ref[...] = v_ref[...].T

    same = seg_col[...] == seg_row[...]
    parts = []
    for head in range(2):
        scores = dot_nt(k_ref[...], only_head(q_ref[...], head)) * (SCALE * LOG2E)
        scores = jnp.where(same, scores, -1e30)
        top = jnp.max(scores, axis=0, keepdims=True)
        expo = jnp.exp2(scores - top)
        total = jnp.sum(expo, axis=0, keepdims=True)
        out = dot_nn(
            vt_ref[head * HEAD_DIM : (head + 1) * HEAD_DIM, :], expo.astype(jnp.bfloat16)
        )
        parts.append(out / total)
        lse_ref[0, head : head + 1, :] = top + jnp.log2(total)
    ctx_ref[...] = jnp.concatenate(parts, axis=0).T.astype(jnp.bfloat16)


def attend_back_kernel(
    seg_col, seg_row, q_ref, k_ref, v_ref, lse_ref, do_ref, dq_ref, dk_ref, dv_ref, kt_ref, dk_acc, dv_acc
):
    step = pl.program_id(1)

    @pl.when(step == 0)
    def _():
        kt_ref[...] = k_ref[...].T
        dk_acc[...] = jnp.zeros_like(dk_acc)
        dv_acc[...] = jnp.zeros_like(dv_acc)

    same = seg_col[...] == seg_row[...]
    parts = []
    for head in range(2):
        query = only_head(q_ref[...], head)
        grad = only_head(do_ref[...], head)
        scores = dot_nt(k_ref[...], query) * (SCALE * LOG2E)
        probs = jnp.where(same, jnp.exp2(scores - lse_ref[0, head : head + 1, :]), 0.0)
        d_probs = dot_nt(v_ref[...], grad)
        inner = jnp.sum(probs * d_probs, axis=0, keepdims=True)
        d_scores = (probs * (d_probs - inner)).astype(jnp.bfloat16)
        dv_acc[...] += dot_nn(probs.astype(jnp.bfloat16), grad)
        dk_acc[...] += dot_nn(d_scores, query)
        parts.append(
            dot_nn(kt_ref[head * HEAD_DIM : (head + 1) * HEAD_DIM, :], d_scores)
        )
    dq_ref[...] = (jnp.concatenate(parts, axis=0) * SCALE).T.astype(jnp.bfloat16)

    @pl.when(step == pl.num_programs(1) - 1)
    def _():
        dk_ref[...] = (dk_acc[...] * SCALE).astype(jnp.bfloat16)
        dv_ref[...] = dv_acc[...].astype(jnp.bfloat16)


def attention_specs(count, pairs, block, skip=0):
    seg_col = pl.BlockSpec((count, 1), lambda h, i: (0, 0))
    seg_row = pl.BlockSpec((1, block), lambda h, i: (0, i))
    query = pl.BlockSpec((block, PAIR), lambda h, i: (i, skip + h))
    key = pl.BlockSpec((count, PAIR), lambda h, i: (0, pairs + skip + h))
    value = pl.BlockSpec((count, PAIR), lambda h, i: (0, 2 * pairs + skip + h))
    lse = pl.BlockSpec((1, 2, block), lambda h, i: (h, 0, i))
    return seg_col, seg_row, query, key, value, lse


def attend(qkv, segment, turn, turns):
    count = qkv.shape[0]
    pairs = qkv.shape[1] // (3 * PAIR)
    here = pairs // turns
    block = min(Q_BLOCK, count)
    seg_col, seg_row, query, key, value, lse = attention_specs(count, pairs, block, turn * here)
    return pl.pallas_call(
        attend_kernel,
        grid=(here, count // block),
        in_specs=[seg_col, seg_row, query, key, value],
        out_specs=[pl.BlockSpec((block, PAIR), lambda h, i: (i, h)), lse],
        out_shape=[
            jax.ShapeDtypeStruct((count, here * PAIR), jnp.bfloat16),
            jax.ShapeDtypeStruct((here, 2, count), jnp.float32),
        ],
        scratch_shapes=[pltpu.VMEM((PAIR, count), jnp.bfloat16)],
        compiler_params=pltpu.CompilerParams(vmem_limit_bytes=32 << 20),
        cost_estimate=NO_COST,
    )(segment.reshape(-1, 1), segment, qkv, qkv, qkv)


def attend_back(qkv, segment, lse_rows, d_context, turn, turns):
    count = qkv.shape[0]
    pairs = qkv.shape[1] // (3 * PAIR)
    here = pairs // turns
    block = min(Q_BLOCK, count)
    seg_col, seg_row, query, key, value, lse = attention_specs(count, pairs, block, turn * here)
    d_query = pl.BlockSpec((block, PAIR), lambda h, i: (i, h))
    d_whole = pl.BlockSpec((count, PAIR), lambda h, i: (0, h))
    shape = jax.ShapeDtypeStruct((count, here * PAIR), jnp.bfloat16)
    return pl.pallas_call(
        attend_back_kernel,
        grid=(here, count // block),
        in_specs=[seg_col, seg_row, query, key, value, lse, query],
        out_specs=[d_query, d_whole, d_whole],
        out_shape=[shape, shape, shape],
        scratch_shapes=[
            pltpu.VMEM((PAIR, count), jnp.bfloat16),
            pltpu.VMEM((count, PAIR), jnp.float32),
            pltpu.VMEM((count, PAIR), jnp.float32),
        ],
        compiler_params=pltpu.CompilerParams(vmem_limit_bytes=32 << 20),
        cost_estimate=NO_COST,
    )(segment.reshape(-1, 1), segment, qkv, qkv, qkv, lse_rows, d_context)


def matmul(left, right):
    return jnp.dot(left, right, preferred_element_type=jnp.float32)


def matmul_tn(left, right):
    return lax.dot_general(
        left, right, (((0,), (0,)), ((), ())), preferred_element_type=jnp.float32
    )


def matmul_nt(left, right):
    return lax.dot_general(
        left, right, (((1,), (1,)), ((), ())), preferred_element_type=jnp.float32
    )


def column_sum(values):
    return jnp.sum(values.astype(jnp.float32), axis=0)


def swapped(part):
    return lax.ppermute(part, "col", [(0, 1), (1, 0)])


def swapped_rows(part):
    other = swapped(part)
    cut = other.shape[1] // 2
    return jnp.concatenate([other[:, cut:], other[:, :cut]], axis=1).astype(jnp.float32)


def partner(part, axis, bit):
    size = lax.axis_size(axis)
    return lax.ppermute(part, axis, [(i, i ^ bit) for i in range(size)])


def shifted(part, step):
    size = lax.axis_size("row")
    return lax.ppermute(part, "row", [(i, (i + step) % size) for i in range(size)])


def is_small_grid(rows):
    return lax.axis_size("row") == 4 and lax.axis_size("dp") == 4 and rows % 128 == 0


def place_kernel(idx, own, ring, near_x, near_y, far_a, far_b, *outs):
    step = pl.program_id(0)
    quarter = ring.shape[0]
    part = quarter // 2
    begin = 0
    for out in outs:
        columns = slice(begin, begin + out.shape[1])
        begin = begin + out.shape[1]

        def put(corner, skip, value):
            start = pl.multiple_of(idx[4 + corner] * quarter + skip, part)
            out[pl.ds(start, value.shape[0]), :] = value

        @pl.when(step == 0)
        def _():
            out[...] = own[:, columns]

        @pl.when(step > 0)
        def _():
            put(0, 0, ring[:, columns])
            put(1, 0, near_x[:, columns])
            put(2, 0, near_y[:, columns])

        @pl.when(step == 1)
        def _():
            put(3, 0, far_a[:quarter, columns])

        @pl.when(step == 2)
        def _():
            put(3, 0, far_a[quarter:, columns])
            put(3, part, far_b[:part, columns])

        @pl.when(step == 3)
        def _():
            put(3, 0, far_b[part:, columns])


def place(idx, own, ring, near_x, near_y, far_a, far_b, widths):
    rows, width = own.shape
    fixed = [pl.BlockSpec(part.shape, lambda s, idx: (0, 0)) for part in (own, far_a, far_b)]
    moving = pl.BlockSpec((rows // 4, width), lambda s, idx: (jnp.maximum(s - 1, 0), 0))
    return pl.pallas_call(
        place_kernel,
        grid_spec=pltpu.PrefetchScalarGridSpec(
            num_scalar_prefetch=1,
            grid=(4,),
            in_specs=[fixed[0], moving, moving, moving, fixed[1], fixed[2]],
            out_specs=[pl.BlockSpec((rows, w), lambda s, idx: (idx[s], 0)) for w in widths],
        ),
        out_shape=[jax.ShapeDtypeStruct((4 * rows, w), own.dtype) for w in widths],
        compiler_params=pltpu.CompilerParams(vmem_limit_bytes=40 << 20),
        cost_estimate=pl.CostEstimate(
            flops=0, bytes_accessed=8 * rows * width * 2, transcendentals=0
        ),
    )(idx, own, ring, near_x, near_y, far_a, far_b)


def natural_order(whole):
    cut = whole.shape[0] // 2
    return jnp.where(
        lax.axis_index("col") == 0, whole, jnp.concatenate([whole[cut:], whole[:cut]], axis=0)
    )


def gathered(block):
    rows = block.shape[0] // lax.axis_size("dp")
    part = lax.dynamic_slice_in_dim(block, lax.axis_index("dp") * rows, rows, 0)
    return natural_order(lax.all_gather(part, ("row", "dp"), axis=0, tiled=True))


def sync_kernel(*refs):
    pass


def sync(arrays):
    arrays = list(arrays)
    return pl.pallas_call(
        sync_kernel,
        in_specs=[pl.BlockSpec(memory_space=pl.ANY)] * len(arrays),
        out_specs=[pl.BlockSpec(memory_space=pl.ANY)] * len(arrays),
        out_shape=[jax.ShapeDtypeStruct(part.shape, part.dtype) for part in arrays],
        input_output_aliases={i: i for i in range(len(arrays))},
        cost_estimate=NO_COST,
    )(*arrays)


def checkpoint(value, *movers):
    counts = [len(mover.got) for mover in movers]
    if sum(counts):
        value, *got = sync([value] + [part for mover in movers for part in mover.got])
        for mover, count in zip(movers, counts):
            mover.got, got = got[:count], got[count:]
    sends = [mover.sends() for mover in movers]
    if sum(len(some) for some in sends):
        value, *flat = sync([value] + [part for some in sends for part in some])
        for mover, some in zip(movers, sends):
            mover.go(flat[: len(some)])
            flat = flat[len(some) :]
    return value


class Gather:
    def __init__(self, group, early):
        self.group = group
        self.got = []
        self.direct = not all(is_small_grid(block.shape[0]) for block in group)
        if self.direct:
            return
        core, self.corner = lax.axis_index("col"), lax.axis_index("dp")
        self.level, self.size = lax.axis_index("row"), lax.axis_size("row")
        place_z = self.level + self.size // 2 * core + self.size - jnp.arange(self.size)
        self.idx = jnp.concatenate([place_z % self.size, self.corner ^ jnp.arange(4)])
        self.own = jnp.concatenate(group, axis=1) if len(group) > 1 else group[0]
        self.quarter = self.own.shape[0] // 4
        part = lax.dynamic_slice_in_dim(self.own, self.corner * self.quarter, self.quarter, 0)
        self.early = early
        if early:
            self.got = [shifted(part, step) for step in (1, 2, 3)]
        else:
            self.got = [lax.all_gather(part, "row", axis=0, tiled=True)]
        self.step = 0

    def sends(self):
        if self.direct:
            return []
        if self.step == 0:
            if self.early:
                pieces = self.got
            else:
                pieces = [
                    lax.dynamic_slice_in_dim(
                        self.got[0],
                        (self.level + self.size - step) % self.size * self.quarter,
                        self.quarter,
                        0,
                    )
                    for step in (1, 2, 3)
                ]
            return [jnp.concatenate(pieces, axis=0)]
        near_x, near_y = self.got
        self.near = self.got
        cut = near_x.shape[0] // 2
        return [near_y[:cut], near_x[cut:]]

    def go(self, sends):
        if self.direct:
            return
        if self.step == 0:
            self.stack = sends[0]
            self.got = [partner(sends[0], "dp", 1), partner(sends[0], "dp", 2)]
        else:
            self.got = [partner(sends[0], "dp", 1), partner(sends[1], "dp", 2)]
        self.step = self.step + 1

    def result(self):
        if self.direct:
            return [gathered(block) for block in self.group]
        while self.step < 2:
            self.go(self.sends())
        widths = [block.shape[1] for block in self.group]
        idx = self.idx.astype(jnp.int32)
        return place(idx, self.own, self.stack, *self.near, *self.got, widths)


def pick(values, axis, index):
    return lax.dynamic_index_in_dim(values, index, axis, keepdims=False)


def added(*parts):
    total = parts[0].astype(jnp.float32)
    for part in parts[1:]:
        total = total + part.astype(jnp.float32)
    return total.astype(jnp.bfloat16)


class Reduction:
    def __init__(self, first, second):
        corner = lax.axis_index("dp")
        self.a, self.b = corner // 2, corner % 2
        self.direct = not is_small_grid(2 * first.shape[0] // lax.axis_size("row"))
        self.step = 0
        self.got = []
        if self.direct:
            self.whole = jnp.concatenate([first, second], axis=0)
        else:
            width = first.shape[1]
            self.first = first.reshape(2, 2, 2, -1, width)
            self.second = second.reshape(2, 2, 2, -1, width)

    def sends(self):
        if self.direct:
            return []
        a, b = self.a, self.b
        if self.step == 0:
            return [pick(self.first, 2, 1 - b), pick(self.second, 1, 1 - a)]
        if self.step == 1:
            one, two = self.got
            self.keep = (
                pick(pick(self.first, 2, b), 1, a),
                pick(one, 1, a),
                pick(pick(self.second, 1, a), 1, b),
                pick(two, 1, b),
            )
            return [
                added(pick(pick(self.first, 2, b), 1, 1 - a), pick(one, 1, 1 - a)),
                added(pick(pick(self.second, 1, a), 1, 1 - b), pick(two, 1, 1 - b)),
            ]
        if self.step == 2:
            levels = jnp.concatenate(
                [added(*self.keep[:2], self.got[0]), added(*self.keep[2:], self.got[1])], axis=0
            )
            size = lax.axis_size("row")
            place_z = lax.axis_index("row") + size // 2 * lax.axis_index("col")
            parts = [pick(levels, 0, (place_z + step) % size) for step in range(4)]
            self.mine = parts[0]
            return parts[1:]
        self.total = added(self.mine, *self.got)
        return [self.total]

    def go(self, sends):
        if self.direct:
            return
        if self.step == 0:
            self.got = [partner(sends[0], "dp", 1), partner(sends[1], "dp", 2)]
        elif self.step == 1:
            self.got = [partner(sends[0], "dp", 2), partner(sends[1], "dp", 1)]
        elif self.step == 2:
            self.got = [shifted(part, step) for part, step in zip(sends, (1, 2, 3))]
        else:
            self.got = [sends[0]] + [partner(sends[0], "dp", bit) for bit in (1, 2, 3)]
        self.step = self.step + 1

    def result(self):
        if self.direct:
            whole = natural_order(self.whole)
            part = lax.psum_scatter(whole, ("row", "dp"), scatter_dimension=0, tiled=True)
            return lax.all_gather(part, "dp", axis=0, tiled=True).astype(jnp.float32)
        while self.step < 4:
            self.go(self.sends())
        got = self.got
        return jnp.concatenate(
            [
                jnp.where(
                    self.a == 0,
                    jnp.where(self.b == 0, got[k], got[k ^ 1]),
                    jnp.where(self.b == 0, got[k ^ 2], got[k ^ 3]),
                )
                for k in range(4)
            ],
            axis=0,
        ).astype(jnp.float32)


def reduced_vector(values):
    values = values.reshape(-1, 128)
    if not is_small_grid(128):
        return lax.psum(values, ("row", "dp")).reshape(-1)
    for axis in ("dp", "row"):
        for bit in (1, 2):
            values = values + partner(values, axis, bit)
    return values.reshape(-1)


def norm_forward(resid, gain, shift):
    center = jnp.mean(resid, axis=1, keepdims=True)
    inverse = lax.rsqrt(
        jnp.mean(resid * resid, axis=1, keepdims=True) - center * center + EPSILON
    )
    normed = (resid - center) * inverse
    return (normed * gain + shift, normed, inverse)


def norm_backward(grad, normed, inverse, gain):
    scaled = grad * gain
    first = jnp.mean(scaled, axis=1, keepdims=True)
    second = jnp.mean(scaled * normed, axis=1, keepdims=True)
    return inverse * (scaled - first - normed * second)


def body(
    tokens,
    segment,
    cotangent,
    w_query,
    b_query,
    w_key,
    w_value,
    b_value,
    w_out,
    b_out,
    w_up,
    b_up,
    w_down,
    b_down,
    gain_one,
    shift_one,
    gain_two,
    shift_two,
):
    half = w_query.shape[1]
    token_rows = jnp.concatenate([tokens, swapped(tokens)], axis=1)
    take_qkv = Gather([jnp.concatenate([w_query, w_key, w_value], axis=1)], True)
    take_out_up = Gather([w_out, w_up], False)
    take_down = Gather([w_down], False)
    token_rows = checkpoint(token_rows, take_qkv)
    token_rows = checkpoint(token_rows, take_qkv)
    (w_qkv,) = take_qkv.result()
    cotangent_rows = jnp.concatenate([cotangent, swapped(cotangent)], axis=1)
    own_vectors = jnp.stack([b_out, b_down, gain_one, shift_one, gain_two, shift_two])
    vectors = jnp.concatenate([own_vectors, swapped(own_vectors)], axis=1).astype(jnp.float32)
    bias_out, bias_down, gain1, shift1, gain2, shift2 = [vectors[i] for i in range(6)]
    b_qkv = jnp.concatenate([b_query, jnp.zeros_like(b_query), b_value]).astype(jnp.float32)
    qkv = (matmul(token_rows, w_qkv) + b_qkv).astype(jnp.bfloat16)
    qkv = checkpoint(qkv, take_out_up)
    context_one, lse_one = attend(qkv, segment, 0, 2)
    context_one = checkpoint(context_one, take_out_up, take_down)
    qkv, context_one = sync([qkv, context_one])
    other_one = swapped(context_one)
    context_two, lse_two = attend(qkv, segment, 1, 2)
    context_rows = jnp.concatenate(
        [context_one, context_two, other_one, swapped(context_two)], axis=1
    )
    wo_half, wu = take_out_up.result()
    wo_other = swapped(wo_half)
    wo = jnp.concatenate(
        [wo_half, jnp.concatenate([wo_other[half:], wo_other[:half]], axis=0)], axis=1
    )
    first_sum = token_rows.astype(jnp.float32) + (matmul(context_rows, wo) + bias_out)
    hidden_f, normed_one, inverse_one = norm_forward(first_sum, gain1, shift1)
    hidden = hidden_f.astype(jnp.bfloat16)
    hidden = checkpoint(hidden, take_down)
    pre_act = matmul(hidden, wu) + b_up.astype(jnp.float32)
    cdf = 0.5 * (1.0 + lax.erf(pre_act * (0.5**0.5)))
    activated = (pre_act * cdf).astype(jnp.bfloat16)
    slope = cdf + pre_act * (jnp.exp(-0.5 * pre_act * pre_act) * 0.3989422804014327)
    (wd_half,) = take_down.result()
    units = w_up.shape[1]
    wd = jnp.concatenate([wd_half[:units], swapped(wd_half[units:])], axis=1)
    part = matmul(activated, wd).astype(jnp.bfloat16)
    ffn_out = part.astype(jnp.float32) + swapped_rows(part) + bias_down
    second_sum = hidden.astype(jnp.float32) + ffn_out
    final, normed_two, inverse_two = norm_forward(second_sum, gain2, shift2)
    output = final[:, :half].astype(jnp.bfloat16)
    y = cotangent_rows.astype(jnp.float32)
    second_grad = norm_backward(y, normed_two, inverse_two, gain2)
    d_gain_two = jnp.sum(y * normed_two, axis=0)
    d_shift_two = jnp.sum(y, axis=0)
    ffn_grad = second_grad.astype(jnp.bfloat16)
    d_down_other = swapped(matmul_tn(activated, ffn_grad[:, half:]).astype(jnp.bfloat16))
    d_down_own = matmul_tn(activated, ffn_grad[:, :half]).astype(jnp.bfloat16)
    d_b_down = column_sum(ffn_grad)
    pre_grad = (matmul_nt(ffn_grad, wd) * slope).astype(jnp.bfloat16)
    d_b_up = column_sum(pre_grad)
    down = Reduction(d_down_own, d_down_other)
    pre_grad = checkpoint(pre_grad, down)
    hidden_part = matmul_nt(pre_grad, wu).astype(jnp.bfloat16)
    hidden_other = swapped_rows(hidden_part)
    d_w_up = matmul_tn(hidden, pre_grad).astype(jnp.bfloat16)
    up = Reduction(d_w_up[:half], d_w_up[half:])
    hidden_part = checkpoint(hidden_part, up)
    hidden_grad = second_grad + (hidden_part.astype(jnp.float32) + hidden_other)
    first_grad = norm_backward(hidden_grad, normed_one, inverse_one, gain1)
    d_gain_one = jnp.sum(hidden_grad * normed_one, axis=0)
    d_shift_one = jnp.sum(hidden_grad, axis=0)
    branch_grad = first_grad.astype(jnp.bfloat16)
    d_b_out = column_sum(branch_grad)
    wide = jnp.stack([d_b_out, d_b_down, d_gain_one, d_shift_one, d_gain_two, d_shift_two])
    context_grad = matmul_nt(branch_grad, wo[:half]).astype(jnp.bfloat16)
    d_w_out = matmul_tn(context_rows, branch_grad[:, :half]).astype(jnp.bfloat16)
    out = Reduction(d_w_out[:half], d_w_out[half:])
    context_grad = checkpoint(context_grad, down)
    grads_one = attend_back(qkv, segment, lse_one, context_grad, 0, 2)
    grads_one = [checkpoint(grads_one[0], up, down, out), *grads_one[1:]]
    grads_one[0], context_grad = sync([grads_one[0], context_grad])
    grads_two = attend_back(qkv, segment, lse_two, context_grad, 1, 2)
    grads_two = [checkpoint(grads_two[0], up, out), *grads_two[1:]]
    qkv_grad = jnp.concatenate(
        [part for pair in zip(grads_one, grads_two) for part in pair], axis=1
    )
    d_w_qkv = matmul_tn(token_rows, qkv_grad).astype(jnp.bfloat16)
    d_b_qkv = column_sum(qkv_grad)
    proj = Reduction(d_w_qkv[:half], d_w_qkv[half:])
    qkv_grad = checkpoint(qkv_grad, proj)
    token_part = matmul_nt(qkv_grad, w_qkv).astype(jnp.bfloat16)
    token_other = swapped(token_part[:, half:])
    token_sum = token_part[:, :half].astype(jnp.float32) + token_other.astype(jnp.float32)
    d_tokens = (token_sum + first_grad[:, :half]).astype(jnp.bfloat16)
    d_tokens = checkpoint(d_tokens, down, out)
    sums = reduced_vector(jnp.concatenate([wide[:, :half].reshape(-1), d_b_up]))
    d_tokens = checkpoint(d_tokens, proj)
    d_tokens = checkpoint(d_tokens, up, out)
    d_tokens = checkpoint(d_tokens, proj)
    d_b_qv = reduced_vector(jnp.concatenate([d_b_qkv[:half], d_b_qkv[2 * half :]]))
    o_w_down, o_w_up, o_w_out = down.result(), up.result(), out.result()
    o_w_qkv = proj.result()
    pieces = [sums[i * half : (i + 1) * half] for i in range(6)]
    return (
        output,
        d_tokens,
        o_w_qkv[:, :half],
        d_b_qv[:half],
        o_w_qkv[:, half : 2 * half],
        o_w_qkv[:, 2 * half :],
        d_b_qv[half:],
        o_w_out,
        pieces[0],
        o_w_up,
        sums[6 * half :],
        o_w_down,
        pieces[1],
        pieces[2],
        pieces[3],
        pieces[4],
        pieces[5],
    )


def solution(mesh):
    in_specs = (
        P(("dp", "row"), "col"),
        P(("dp", "row"), None),
        P(("dp", "row"), "col"),
        P("row", "col"),
        P("col"),
        P("row", "col"),
        P("row", "col"),
        P("col"),
        P("row", "col"),
        P("col"),
        P("row", "col"),
        P("col"),
        P("row", "col"),
        P("col"),
        P("col"),
        P("col"),
        P("col"),
        P("col"),
    )
    out_specs = (
        P(("dp", "row"), "col"),
        P(("dp", "row"), "col"),
        P("row", "col"),
        P("col"),
        P("row", "col"),
        P("row", "col"),
        P("col"),
        P("row", "col"),
        P("col"),
        P("row", "col"),
        P("col"),
        P("row", "col"),
        P("col"),
        P("col"),
        P("col"),
        P("col"),
        P("col"),
    )
    return jax.shard_map(body, mesh=mesh, in_specs=in_specs, out_specs=out_specs, check_vma=False)
```

```python
import jax
import jax.numpy as jnp
from jax import lax
from jax.experimental import pallas as pl
from jax.experimental.pallas import tpu as pltpu
from jax.sharding import PartitionSpec as P

HEAD_DIM = 64


EPSILON = 1e-05
SCALE = 0.125
LOG2E = 1.4426950408889634
PAIR = 2 * HEAD_DIM
Q_BLOCK = 256
NO_COST = pl.CostEstimate(flops=0, bytes_accessed=0, transcendentals=0)


def dot_nt(left, right):
    return lax.dot_general(
        left, right, (((1,), (1,)), ((), ())), preferred_element_type=jnp.float32
    )


def dot_nn(left, right):
    return lax.dot_general(
        left, right, (((1,), (0,)), ((), ())), preferred_element_type=jnp.float32
    )


def only_head(block, head):
    lane = lax.broadcasted_iota(jnp.int32, block.shape, 1)
    return jnp.where(lane // HEAD_DIM == head, block, jnp.zeros_like(block))


def attend_kernel(seg_col, seg_row, q_ref, k_ref, v_ref, ctx_ref, lse_ref, vt_ref):
    @pl.when(pl.program_id(1) == 0)
    def _():
        vt_ref[...] = v_ref[...].T

    same = seg_col[...] == seg_row[...]
    parts = []
    for head in range(2):
        scores = dot_nt(k_ref[...], only_head(q_ref[...], head)) * (SCALE * LOG2E)
        scores = jnp.where(same, scores, -1e30)
        top = jnp.max(scores, axis=0, keepdims=True)
        expo = jnp.exp2(scores - top)
        total = jnp.sum(expo, axis=0, keepdims=True)
        out = dot_nn(
            vt_ref[head * HEAD_DIM : (head + 1) * HEAD_DIM, :], expo.astype(jnp.bfloat16)
        )
        parts.append(out / total)
        lse_ref[0, head : head + 1, :] = top + jnp.log2(total)
    ctx_ref[...] = jnp.concatenate(parts, axis=0).T.astype(jnp.bfloat16)


def attend_back_kernel(
    seg_col, seg_row, q_ref, k_ref, v_ref, lse_ref, do_ref, dq_ref, dk_ref, dv_ref, kt_ref, dk_acc, dv_acc
):
    step = pl.program_id(1)

    @pl.when(step == 0)
    def _():
        kt_ref[...] = k_ref[...].T
        dk_acc[...] = jnp.zeros_like(dk_acc)
        dv_acc[...] = jnp.zeros_like(dv_acc)

    same = seg_col[...] == seg_row[...]
    parts = []
    for head in range(2):
        query = only_head(q_ref[...], head)
        grad = only_head(do_ref[...], head)
        scores = dot_nt(k_ref[...], query) * (SCALE * LOG2E)
        probs = jnp.where(same, jnp.exp2(scores - lse_ref[0, head : head + 1, :]), 0.0)
        d_probs = dot_nt(v_ref[...], grad)
        inner = jnp.sum(probs * d_probs, axis=0, keepdims=True)
        d_scores = (probs * (d_probs - inner)).astype(jnp.bfloat16)
        dv_acc[...] += dot_nn(probs.astype(jnp.bfloat16), grad)
        dk_acc[...] += dot_nn(d_scores, query)
        parts.append(
            dot_nn(kt_ref[head * HEAD_DIM : (head + 1) * HEAD_DIM, :], d_scores)
        )
    dq_ref[...] = (jnp.concatenate(parts, axis=0) * SCALE).T.astype(jnp.bfloat16)

    @pl.when(step == pl.num_programs(1) - 1)
    def _():
        dk_ref[...] = (dk_acc[...] * SCALE).astype(jnp.bfloat16)
        dv_ref[...] = dv_acc[...].astype(jnp.bfloat16)


def attention_specs(count, pairs, block, skip=0):
    seg_col = pl.BlockSpec((count, 1), lambda h, i: (0, 0))
    seg_row = pl.BlockSpec((1, block), lambda h, i: (0, i))
    query = pl.BlockSpec((block, PAIR), lambda h, i: (i, skip + h))
    key = pl.BlockSpec((count, PAIR), lambda h, i: (0, pairs + skip + h))
    value = pl.BlockSpec((count, PAIR), lambda h, i: (0, 2 * pairs + skip + h))
    lse = pl.BlockSpec((1, 2, block), lambda h, i: (h, 0, i))
    return seg_col, seg_row, query, key, value, lse


def attend(qkv, segment, turn, turns):
    count = qkv.shape[0]
    pairs = qkv.shape[1] // (3 * PAIR)
    here = pairs // turns
    block = min(Q_BLOCK, count)
    seg_col, seg_row, query, key, value, lse = attention_specs(count, pairs, block, turn * here)
    return pl.pallas_call(
        attend_kernel,
        grid=(here, count // block),
        in_specs=[seg_col, seg_row, query, key, value],
        out_specs=[pl.BlockSpec((block, PAIR), lambda h, i: (i, h)), lse],
        out_shape=[
            jax.ShapeDtypeStruct((count, here * PAIR), jnp.bfloat16),
            jax.ShapeDtypeStruct((here, 2, count), jnp.float32),
        ],
        scratch_shapes=[pltpu.VMEM((PAIR, count), jnp.bfloat16)],
        compiler_params=pltpu.CompilerParams(vmem_limit_bytes=32 << 20),
        cost_estimate=NO_COST,
    )(segment.reshape(-1, 1), segment, qkv, qkv, qkv)


def attend_back(qkv, segment, lse_rows, d_context, turn, turns):
    count = qkv.shape[0]
    pairs = qkv.shape[1] // (3 * PAIR)
    here = pairs // turns
    block = min(Q_BLOCK, count)
    seg_col, seg_row, query, key, value, lse = attention_specs(count, pairs, block, turn * here)
    d_query = pl.BlockSpec((block, PAIR), lambda h, i: (i, h))
    d_whole = pl.BlockSpec((count, PAIR), lambda h, i: (0, h))
    shape = jax.ShapeDtypeStruct((count, here * PAIR), jnp.bfloat16)
    return pl.pallas_call(
        attend_back_kernel,
        grid=(here, count // block),
        in_specs=[seg_col, seg_row, query, key, value, lse, query],
        out_specs=[d_query, d_whole, d_whole],
        out_shape=[shape, shape, shape],
        scratch_shapes=[
            pltpu.VMEM((PAIR, count), jnp.bfloat16),
            pltpu.VMEM((count, PAIR), jnp.float32),
            pltpu.VMEM((count, PAIR), jnp.float32),
        ],
        compiler_params=pltpu.CompilerParams(vmem_limit_bytes=32 << 20),
        cost_estimate=NO_COST,
    )(segment.reshape(-1, 1), segment, qkv, qkv, qkv, lse_rows, d_context)


def matmul(left, right):
    return jnp.dot(left, right, preferred_element_type=jnp.float32)


def matmul_tn(left, right):
    return lax.dot_general(
        left, right, (((0,), (0,)), ((), ())), preferred_element_type=jnp.float32
    )


def matmul_nt(left, right):
    return lax.dot_general(
        left, right, (((1,), (1,)), ((), ())), preferred_element_type=jnp.float32
    )


def column_sum(values):
    return jnp.sum(values.astype(jnp.float32), axis=0)


def swapped(part):
    return lax.ppermute(part, "col", [(0, 1), (1, 0)])


def swapped_rows(part):
    other = swapped(part)
    cut = other.shape[1] // 2
    return jnp.concatenate([other[:, cut:], other[:, :cut]], axis=1).astype(jnp.float32)


def partner(part, axis, bit):
    size = lax.axis_size(axis)
    return lax.ppermute(part, axis, [(i, i ^ bit) for i in range(size)])


def shifted(part, step):
    size = lax.axis_size("row")
    return lax.ppermute(part, "row", [(i, (i + step) % size) for i in range(size)])


def is_small_grid(rows):
    return lax.axis_size("row") == 4 and lax.axis_size("dp") == 4 and rows % 128 == 0


def place_kernel(idx, own, ring, near_x, near_y, far_a, far_b, *outs):
    step = pl.program_id(0)
    quarter = ring.shape[0]
    part = quarter // 2
    begin = 0
    for out in outs:
        columns = slice(begin, begin + out.shape[1])
        begin = begin + out.shape[1]

        def put(corner, skip, value):
            start = pl.multiple_of(idx[4 + corner] * quarter + skip, part)
            out[pl.ds(start, value.shape[0]), :] = value

        @pl.when(step == 0)
        def _():
            out[...] = own[:, columns]

        @pl.when(step > 0)
        def _():
            put(0, 0, ring[:, columns])
            put(1, 0, near_x[:, columns])
            put(2, 0, near_y[:, columns])

        @pl.when(step == 1)
        def _():
            put(3, 0, far_a[:quarter, columns])

        @pl.when(step == 2)
        def _():
            put(3, 0, far_a[quarter:, columns])
            put(3, part, far_b[:part, columns])

        @pl.when(step == 3)
        def _():
            put(3, 0, far_b[part:, columns])


def place(idx, own, ring, near_x, near_y, far_a, far_b, widths):
    rows, width = own.shape
    fixed = [pl.BlockSpec(part.shape, lambda s, idx: (0, 0)) for part in (own, far_a, far_b)]
    moving = pl.BlockSpec((rows // 4, width), lambda s, idx: (jnp.maximum(s - 1, 0), 0))
    return pl.pallas_call(
        place_kernel,
        grid_spec=pltpu.PrefetchScalarGridSpec(
            num_scalar_prefetch=1,
            grid=(4,),
            in_specs=[fixed[0], moving, moving, moving, fixed[1], fixed[2]],
            out_specs=[pl.BlockSpec((rows, w), lambda s, idx: (idx[s], 0)) for w in widths],
        ),
        out_shape=[jax.ShapeDtypeStruct((4 * rows, w), own.dtype) for w in widths],
        compiler_params=pltpu.CompilerParams(vmem_limit_bytes=40 << 20),
        cost_estimate=pl.CostEstimate(
            flops=0, bytes_accessed=8 * rows * width * 2, transcendentals=0
        ),
    )(idx, own, ring, near_x, near_y, far_a, far_b)


def natural_order(whole):
    cut = whole.shape[0] // 2
    return jnp.where(
        lax.axis_index("col") == 0, whole, jnp.concatenate([whole[cut:], whole[:cut]], axis=0)
    )


def gathered(block):
    rows = block.shape[0] // lax.axis_size("dp")
    part = lax.dynamic_slice_in_dim(block, lax.axis_index("dp") * rows, rows, 0)
    return natural_order(lax.all_gather(part, ("row", "dp"), axis=0, tiled=True))


def sync_kernel(*refs):
    pass


def sync(arrays):
    arrays = list(arrays)
    return pl.pallas_call(
        sync_kernel,
        in_specs=[pl.BlockSpec(memory_space=pl.ANY)] * len(arrays),
        out_specs=[pl.BlockSpec(memory_space=pl.ANY)] * len(arrays),
        out_shape=[jax.ShapeDtypeStruct(part.shape, part.dtype) for part in arrays],
        input_output_aliases={i: i for i in range(len(arrays))},
        cost_estimate=NO_COST,
    )(*arrays)


def checkpoint(value, *movers):
    counts = [len(mover.got) for mover in movers]
    if sum(counts):
        value, *got = sync([value] + [part for mover in movers for part in mover.got])
        for mover, count in zip(movers, counts):
            mover.got, got = got[:count], got[count:]
    sends = [mover.sends() for mover in movers]
    if sum(len(some) for some in sends):
        value, *flat = sync([value] + [part for some in sends for part in some])
        for mover, some in zip(movers, sends):
            mover.go(flat[: len(some)])
            flat = flat[len(some) :]
    return value


class Gather:
    def __init__(self, group, early):
        self.group = group
        self.got = []
        self.direct = not all(is_small_grid(block.shape[0]) for block in group)
        if self.direct:
            return
        core, self.corner = lax.axis_index("col"), lax.axis_index("dp")
        self.level, self.size = lax.axis_index("row"), lax.axis_size("row")
        place_z = self.level + self.size // 2 * core + self.size - jnp.arange(self.size)
        self.idx = jnp.concatenate([place_z % self.size, self.corner ^ jnp.arange(4)])
        self.own = jnp.concatenate(group, axis=1) if len(group) > 1 else group[0]
        self.quarter = self.own.shape[0] // 4
        part = lax.dynamic_slice_in_dim(self.own, self.corner * self.quarter, self.quarter, 0)
        self.part = part
        self.early = early
        self.step = -1

    def sends(self):
        if self.direct:
            return []
        if self.step == -1:
            return [self.part]
        if self.step == 0:
            if self.early:
                pieces = self.got
            else:
                pieces = [
                    lax.dynamic_slice_in_dim(
                        self.got[0],
                        (self.level + self.size - step) % self.size * self.quarter,
                        self.quarter,
                        0,
                    )
                    for step in (1, 2, 3)
                ]
            return [jnp.concatenate(pieces, axis=0)]
        near_x, near_y = self.got
        self.near = self.got
        cut = near_x.shape[0] // 2
        return [near_y[:cut], near_x[cut:]]

    def go(self, sends):
        if self.direct:
            return
        if self.step == -1:
            if self.early:
                self.got = [shifted(sends[0], step) for step in (1, 2, 3)]
            else:
                self.got = [lax.all_gather(sends[0], "row", axis=0, tiled=True)]
        elif self.step == 0:
            self.stack = sends[0]
            self.got = [partner(sends[0], "dp", 1), partner(sends[0], "dp", 2)]
        else:
            self.got = [partner(sends[0], "dp", 1), partner(sends[1], "dp", 2)]
        self.step = self.step + 1

    def result(self):
        if self.direct:
            return [gathered(block) for block in self.group]
        while self.step < 2:
            self.go(self.sends())
        widths = [block.shape[1] for block in self.group]
        idx = self.idx.astype(jnp.int32)
        return place(idx, self.own, self.stack, *self.near, *self.got, widths)


def pick(values, axis, index):
    return lax.dynamic_index_in_dim(values, index, axis, keepdims=False)


def added(*parts):
    total = parts[0].astype(jnp.float32)
    for part in parts[1:]:
        total = total + part.astype(jnp.float32)
    return total.astype(jnp.bfloat16)


class Reduction:
    def __init__(self, first, second):
        corner = lax.axis_index("dp")
        self.a, self.b = corner // 2, corner % 2
        self.direct = not is_small_grid(2 * first.shape[0] // lax.axis_size("row"))
        self.step = 0
        self.got = []
        if self.direct:
            self.whole = jnp.concatenate([first, second], axis=0)
        else:
            width = first.shape[1]
            self.first = first.reshape(2, 2, 2, -1, width)
            self.second = second.reshape(2, 2, 2, -1, width)

    def sends(self):
        if self.direct:
            return []
        a, b = self.a, self.b
        if self.step == 0:
            return [pick(self.first, 2, 1 - b), pick(self.second, 1, 1 - a)]
        if self.step == 1:
            one, two = self.got
            self.keep = (
                pick(pick(self.first, 2, b), 1, a),
                pick(one, 1, a),
                pick(pick(self.second, 1, a), 1, b),
                pick(two, 1, b),
            )
            return [
                added(pick(pick(self.first, 2, b), 1, 1 - a), pick(one, 1, 1 - a)),
                added(pick(pick(self.second, 1, a), 1, 1 - b), pick(two, 1, 1 - b)),
            ]
        if self.step == 2:
            levels = jnp.concatenate(
                [added(*self.keep[:2], self.got[0]), added(*self.keep[2:], self.got[1])], axis=0
            )
            size = lax.axis_size("row")
            place_z = lax.axis_index("row") + size // 2 * lax.axis_index("col")
            parts = [pick(levels, 0, (place_z + step) % size) for step in range(4)]
            self.mine = parts[0]
            return parts[1:]
        self.total = added(self.mine, *self.got)
        return [self.total]

    def go(self, sends):
        if self.direct:
            return
        if self.step == 0:
            self.got = [partner(sends[0], "dp", 1), partner(sends[1], "dp", 2)]
        elif self.step == 1:
            self.got = [partner(sends[0], "dp", 2), partner(sends[1], "dp", 1)]
        elif self.step == 2:
            self.got = [shifted(part, step) for part, step in zip(sends, (1, 2, 3))]
        else:
            self.got = [sends[0]] + [partner(sends[0], "dp", bit) for bit in (1, 2, 3)]
        self.step = self.step + 1

    def result(self):
        if self.direct:
            whole = natural_order(self.whole)
            part = lax.psum_scatter(whole, ("row", "dp"), scatter_dimension=0, tiled=True)
            return lax.all_gather(part, "dp", axis=0, tiled=True).astype(jnp.float32)
        while self.step < 4:
            self.go(self.sends())
        got = self.got
        return jnp.concatenate(
            [
                jnp.where(
                    self.a == 0,
                    jnp.where(self.b == 0, got[k], got[k ^ 1]),
                    jnp.where(self.b == 0, got[k ^ 2], got[k ^ 3]),
                )
                for k in range(4)
            ],
            axis=0,
        ).astype(jnp.float32)


class VectorSum:
    PARTNERS = (("dp", 1), ("dp", 2), ("row", 1), ("row", 2))

    def __init__(self, values):
        self.values = values.reshape(-1, 128)
        self.direct = not is_small_grid(128)
        self.got = []
        self.step = 0

    def sends(self):
        if self.direct:
            return []
        if self.got:
            self.values = self.values + self.got[0]
        return [self.values]

    def go(self, sends):
        if self.direct:
            return
        self.values = sends[0]
        self.got = [partner(sends[0], *self.PARTNERS[self.step])]
        self.step = self.step + 1

    def result(self):
        if self.direct:
            return lax.psum(self.values, ("row", "dp")).reshape(-1)
        while self.step < 4:
            self.go(self.sends())
        return (self.values + self.got[0]).reshape(-1)


def norm_forward(resid, gain, shift):
    center = jnp.mean(resid, axis=1, keepdims=True)
    inverse = lax.rsqrt(
        jnp.mean(resid * resid, axis=1, keepdims=True) - center * center + EPSILON
    )
    normed = (resid - center) * inverse
    return (normed * gain + shift, normed, inverse)


def norm_backward(grad, normed, inverse, gain):
    scaled = grad * gain
    first = jnp.mean(scaled, axis=1, keepdims=True)
    second = jnp.mean(scaled * normed, axis=1, keepdims=True)
    return inverse * (scaled - first - normed * second)


def body(
    tokens,
    segment,
    cotangent,
    w_query,
    b_query,
    w_key,
    w_value,
    b_value,
    w_out,
    b_out,
    w_up,
    b_up,
    w_down,
    b_down,
    gain_one,
    shift_one,
    gain_two,
    shift_two,
):
    half = w_query.shape[1]
    token_rows = jnp.concatenate([tokens, swapped(tokens)], axis=1)
    take_qkv = Gather([jnp.concatenate([w_query, w_key, w_value], axis=1)], True)
    take_out_up = Gather([w_out, w_up], True)
    take_down = Gather([w_down], False)
    take_qkv.go(take_qkv.sends())
    token_rows = checkpoint(token_rows, take_qkv, take_out_up)
    token_rows = checkpoint(token_rows, take_qkv)
    (w_qkv,) = take_qkv.result()
    cotangent_rows = jnp.concatenate([cotangent, swapped(cotangent)], axis=1)
    own_vectors = jnp.stack([b_out, b_down, gain_one, shift_one, gain_two, shift_two])
    vectors = jnp.concatenate([own_vectors, swapped(own_vectors)], axis=1).astype(jnp.float32)
    bias_out, bias_down, gain1, shift1, gain2, shift2 = [vectors[i] for i in range(6)]
    b_qkv = jnp.concatenate([b_query, jnp.zeros_like(b_query), b_value]).astype(jnp.float32)
    qkv = (matmul(token_rows, w_qkv) + b_qkv).astype(jnp.bfloat16)
    qkv = checkpoint(qkv, take_out_up, take_down)
    context_one, lse_one = attend(qkv, segment, 0, 2)
    context_one = checkpoint(context_one, take_out_up)
    qkv, context_one = sync([qkv, context_one])
    other_one = swapped(context_one)
    context_two, lse_two = attend(qkv, segment, 1, 2)
    context_two = checkpoint(context_two, take_down)
    context_rows = jnp.concatenate(
        [context_one, context_two, other_one, swapped(context_two)], axis=1
    )
    wo_half, wu = take_out_up.result()
    wo_other = swapped(wo_half)
    wo = jnp.concatenate(
        [wo_half, jnp.concatenate([wo_other[half:], wo_other[:half]], axis=0)], axis=1
    )
    first_sum = token_rows.astype(jnp.float32) + (matmul(context_rows, wo) + bias_out)
    hidden_f, normed_one, inverse_one = norm_forward(first_sum, gain1, shift1)
    hidden = hidden_f.astype(jnp.bfloat16)
    hidden = checkpoint(hidden, take_down)
    pre_act = matmul(hidden, wu) + b_up.astype(jnp.float32)
    cdf = 0.5 * (1.0 + lax.erf(pre_act * (0.5**0.5)))
    activated = (pre_act * cdf).astype(jnp.bfloat16)
    slope = cdf + pre_act * (jnp.exp(-0.5 * pre_act * pre_act) * 0.3989422804014327)
    (wd_half,) = take_down.result()
    units = w_up.shape[1]
    wd = jnp.concatenate([wd_half[:units], swapped(wd_half[units:])], axis=1)
    part = matmul(activated, wd).astype(jnp.bfloat16)
    ffn_out = part.astype(jnp.float32) + swapped_rows(part) + bias_down
    second_sum = hidden.astype(jnp.float32) + ffn_out
    final, normed_two, inverse_two = norm_forward(second_sum, gain2, shift2)
    output = final[:, :half].astype(jnp.bfloat16)
    y = cotangent_rows.astype(jnp.float32)
    second_grad = norm_backward(y, normed_two, inverse_two, gain2)
    d_gain_two = jnp.sum(y * normed_two, axis=0)
    d_shift_two = jnp.sum(y, axis=0)
    ffn_grad = second_grad.astype(jnp.bfloat16)
    d_down_other = swapped(matmul_tn(activated, ffn_grad[:, half:]).astype(jnp.bfloat16))
    d_down_own = matmul_tn(activated, ffn_grad[:, :half]).astype(jnp.bfloat16)
    d_b_down = column_sum(ffn_grad)
    pre_grad = (matmul_nt(ffn_grad, wd) * slope).astype(jnp.bfloat16)
    d_b_up = column_sum(pre_grad)
    down = Reduction(d_down_own, d_down_other)
    pre_grad = checkpoint(pre_grad, down)
    hidden_part = matmul_nt(pre_grad, wu).astype(jnp.bfloat16)
    hidden_other = swapped_rows(hidden_part)
    d_w_up = matmul_tn(hidden, pre_grad).astype(jnp.bfloat16)
    up = Reduction(d_w_up[:half], d_w_up[half:])
    hidden_part = checkpoint(hidden_part, up)
    hidden_grad = second_grad + (hidden_part.astype(jnp.float32) + hidden_other)
    first_grad = norm_backward(hidden_grad, normed_one, inverse_one, gain1)
    d_gain_one = jnp.sum(hidden_grad * normed_one, axis=0)
    d_shift_one = jnp.sum(hidden_grad, axis=0)
    branch_grad = first_grad.astype(jnp.bfloat16)
    d_b_out = column_sum(branch_grad)
    wide = jnp.stack([d_b_out, d_b_down, d_gain_one, d_shift_one, d_gain_two, d_shift_two])
    context_grad = matmul_nt(branch_grad, wo[:half]).astype(jnp.bfloat16)
    d_w_out = matmul_tn(context_rows, branch_grad[:, :half]).astype(jnp.bfloat16)
    out = Reduction(d_w_out[:half], d_w_out[half:])
    sum_wide = VectorSum(jnp.concatenate([wide[:, :half].reshape(-1), d_b_up]))
    context_grad = checkpoint(context_grad, down)
    grads_one = list(attend_back(qkv, segment, lse_one, context_grad, 0, 2))
    grads_one[0] = checkpoint(grads_one[0], up, down, out, sum_wide)
    grads_one[0], context_grad = sync([grads_one[0], context_grad])
    grads_two = list(attend_back(qkv, segment, lse_two, context_grad, 1, 2))
    grads_two[0] = checkpoint(grads_two[0], up, down, out, sum_wide)
    qkv_grad = jnp.concatenate(
        [part for pair in zip(grads_one, grads_two) for part in pair], axis=1
    )
    d_w_qkv = matmul_tn(token_rows, qkv_grad).astype(jnp.bfloat16)
    d_b_qkv = column_sum(qkv_grad)
    proj = Reduction(d_w_qkv[:half], d_w_qkv[half:])
    sum_qv = VectorSum(jnp.concatenate([d_b_qkv[:half], d_b_qkv[2 * half :]]))
    qkv_grad = checkpoint(qkv_grad, proj, sum_wide, sum_qv)
    token_part = matmul_nt(qkv_grad, w_qkv).astype(jnp.bfloat16)
    token_other = swapped(token_part[:, half:])
    token_sum = token_part[:, :half].astype(jnp.float32) + token_other.astype(jnp.float32)
    d_tokens = (token_sum + first_grad[:, :half]).astype(jnp.bfloat16)
    d_tokens = checkpoint(d_tokens, up, out, sum_wide, sum_qv)
    d_tokens = checkpoint(d_tokens, proj, sum_qv)
    d_tokens = checkpoint(d_tokens, proj, out, sum_qv)
    o_w_down, o_w_up, o_w_out = down.result(), up.result(), out.result()
    o_w_qkv = proj.result()
    sums, d_b_qv = sum_wide.result(), sum_qv.result()
    pieces = [sums[i * half : (i + 1) * half] for i in range(6)]
    return (
        output,
        d_tokens,
        o_w_qkv[:, :half],
        d_b_qv[:half],
        o_w_qkv[:, half : 2 * half],
        o_w_qkv[:, 2 * half :],
        d_b_qv[half:],
        o_w_out,
        pieces[0],
        o_w_up,
        sums[6 * half :],
        o_w_down,
        pieces[1],
        pieces[2],
        pieces[3],
        pieces[4],
        pieces[5],
    )


def solution(mesh):
    in_specs = (
        P(("dp", "row"), "col"),
        P(("dp", "row"), None),
        P(("dp", "row"), "col"),
        P("row", "col"),
        P("col"),
        P("row", "col"),
        P("row", "col"),
        P("col"),
        P("row", "col"),
        P("col"),
        P("row", "col"),
        P("col"),
        P("row", "col"),
        P("col"),
        P("col"),
        P("col"),
        P("col"),
        P("col"),
    )
    out_specs = (
        P(("dp", "row"), "col"),
        P(("dp", "row"), "col"),
        P("row", "col"),
        P("col"),
        P("row", "col"),
        P("row", "col"),
        P("col"),
        P("row", "col"),
        P("col"),
        P("row", "col"),
        P("col"),
        P("row", "col"),
        P("col"),
        P("col"),
        P("col"),
        P("col"),
        P("col"),
    )
    return jax.shard_map(body, mesh=mesh, in_specs=in_specs, out_specs=out_specs, check_vma=False)
```

```python
import jax
import jax.numpy as jnp
from jax import lax
from jax.experimental import pallas as pl
from jax.experimental.pallas import tpu as pltpu
from jax.sharding import PartitionSpec as P

HEAD_DIM = 64


EPSILON = 1e-05
SCALE = 0.125
LOG2E = 1.4426950408889634
PAIR = 2 * HEAD_DIM
Q_BLOCK = 256
NO_COST = pl.CostEstimate(flops=0, bytes_accessed=0, transcendentals=0)


def dot_nt(left, right):
    return lax.dot_general(
        left, right, (((1,), (1,)), ((), ())), preferred_element_type=jnp.float32
    )


def dot_nn(left, right):
    return lax.dot_general(
        left, right, (((1,), (0,)), ((), ())), preferred_element_type=jnp.float32
    )


def only_head(block, head):
    lane = lax.broadcasted_iota(jnp.int32, block.shape, 1)
    return jnp.where(lane // HEAD_DIM == head, block, jnp.zeros_like(block))


def attend_kernel(seg_col, seg_row, q_ref, k_ref, v_ref, ctx_ref, lse_ref, vt_ref):
    @pl.when(pl.program_id(1) == 0)
    def _():
        vt_ref[...] = v_ref[...].T

    same = seg_col[...] == seg_row[...]
    parts = []
    for head in range(2):
        scores = dot_nt(k_ref[...], only_head(q_ref[...], head)) * (SCALE * LOG2E)
        scores = jnp.where(same, scores, -1e30)
        top = jnp.max(scores, axis=0, keepdims=True)
        expo = jnp.exp2(scores - top)
        total = jnp.sum(expo, axis=0, keepdims=True)
        out = dot_nn(
            vt_ref[head * HEAD_DIM : (head + 1) * HEAD_DIM, :], expo.astype(jnp.bfloat16)
        )
        parts.append(out / total)
        lse_ref[0, head : head + 1, :] = top + jnp.log2(total)
    ctx_ref[...] = jnp.concatenate(parts, axis=0).T.astype(jnp.bfloat16)


def attend_back_kernel(
    seg_col, seg_row, q_ref, k_ref, v_ref, lse_ref, do_ref, dq_ref, dk_ref, dv_ref, kt_ref, dk_acc, dv_acc
):
    step = pl.program_id(1)

    @pl.when(step == 0)
    def _():
        kt_ref[...] = k_ref[...].T
        dk_acc[...] = jnp.zeros_like(dk_acc)
        dv_acc[...] = jnp.zeros_like(dv_acc)

    same = seg_col[...] == seg_row[...]
    parts = []
    for head in range(2):
        query = only_head(q_ref[...], head)
        grad = only_head(do_ref[...], head)
        scores = dot_nt(k_ref[...], query) * (SCALE * LOG2E)
        probs = jnp.where(same, jnp.exp2(scores - lse_ref[0, head : head + 1, :]), 0.0)
        d_probs = dot_nt(v_ref[...], grad)
        inner = jnp.sum(probs * d_probs, axis=0, keepdims=True)
        d_scores = (probs * (d_probs - inner)).astype(jnp.bfloat16)
        dv_acc[...] += dot_nn(probs.astype(jnp.bfloat16), grad)
        dk_acc[...] += dot_nn(d_scores, query)
        parts.append(
            dot_nn(kt_ref[head * HEAD_DIM : (head + 1) * HEAD_DIM, :], d_scores)
        )
    dq_ref[...] = (jnp.concatenate(parts, axis=0) * SCALE).T.astype(jnp.bfloat16)

    @pl.when(step == pl.num_programs(1) - 1)
    def _():
        dk_ref[...] = (dk_acc[...] * SCALE).astype(jnp.bfloat16)
        dv_ref[...] = dv_acc[...].astype(jnp.bfloat16)


def attention_specs(count, pairs, block, skip=0):
    seg_col = pl.BlockSpec((count, 1), lambda h, i: (0, 0))
    seg_row = pl.BlockSpec((1, block), lambda h, i: (0, i))
    query = pl.BlockSpec((block, PAIR), lambda h, i: (i, skip + h))
    key = pl.BlockSpec((count, PAIR), lambda h, i: (0, pairs + skip + h))
    value = pl.BlockSpec((count, PAIR), lambda h, i: (0, 2 * pairs + skip + h))
    lse = pl.BlockSpec((1, 2, block), lambda h, i: (skip + h, 0, i))
    return seg_col, seg_row, query, key, value, lse


def attend(qkv, segment):
    count = qkv.shape[0]
    pairs = qkv.shape[1] // (3 * PAIR)
    block = min(Q_BLOCK, count)
    seg_col, seg_row, query, key, value, lse = attention_specs(count, pairs, block)
    return pl.pallas_call(
        attend_kernel,
        grid=(pairs, count // block),
        in_specs=[seg_col, seg_row, query, key, value],
        out_specs=[query, lse],
        out_shape=[
            jax.ShapeDtypeStruct((count, pairs * PAIR), jnp.bfloat16),
            jax.ShapeDtypeStruct((pairs, 2, count), jnp.float32),
        ],
        scratch_shapes=[pltpu.VMEM((PAIR, count), jnp.bfloat16)],
        compiler_params=pltpu.CompilerParams(vmem_limit_bytes=32 << 20),
        cost_estimate=NO_COST,
    )(segment.reshape(-1, 1), segment, qkv, qkv, qkv)


def attend_back(qkv, segment, lse_rows, d_context, turn, turns):
    count = qkv.shape[0]
    pairs = qkv.shape[1] // (3 * PAIR)
    here = pairs // turns
    block = min(Q_BLOCK, count)
    seg_col, seg_row, query, key, value, lse = attention_specs(count, pairs, block, turn * here)
    d_query = pl.BlockSpec((block, PAIR), lambda h, i: (i, h))
    d_whole = pl.BlockSpec((count, PAIR), lambda h, i: (0, h))
    shape = jax.ShapeDtypeStruct((count, here * PAIR), jnp.bfloat16)
    return pl.pallas_call(
        attend_back_kernel,
        grid=(here, count // block),
        in_specs=[seg_col, seg_row, query, key, value, lse, query],
        out_specs=[d_query, d_whole, d_whole],
        out_shape=[shape, shape, shape],
        scratch_shapes=[
            pltpu.VMEM((PAIR, count), jnp.bfloat16),
            pltpu.VMEM((count, PAIR), jnp.float32),
            pltpu.VMEM((count, PAIR), jnp.float32),
        ],
        compiler_params=pltpu.CompilerParams(vmem_limit_bytes=32 << 20),
        cost_estimate=NO_COST,
    )(segment.reshape(-1, 1), segment, qkv, qkv, qkv, lse_rows, d_context)


def matmul(left, right):
    return jnp.dot(left, right, preferred_element_type=jnp.float32)


def matmul_tn(left, right):
    return lax.dot_general(
        left, right, (((0,), (0,)), ((), ())), preferred_element_type=jnp.float32
    )


def matmul_nt(left, right):
    return lax.dot_general(
        left, right, (((1,), (1,)), ((), ())), preferred_element_type=jnp.float32
    )


def column_sum(values):
    return jnp.sum(values.astype(jnp.float32), axis=0)


def swapped(part):
    return lax.ppermute(part, "col", [(0, 1), (1, 0)])


def swapped_rows(part):
    other = swapped(part)
    cut = other.shape[1] // 2
    return jnp.concatenate([other[:, cut:], other[:, :cut]], axis=1).astype(jnp.float32)


def partner(part, axis, bit):
    size = lax.axis_size(axis)
    return lax.ppermute(part, axis, [(i, i ^ bit) for i in range(size)])


def shifted(part, step):
    size = lax.axis_size("row")
    return lax.ppermute(part, "row", [(i, (i + step) % size) for i in range(size)])


def is_small_grid(rows):
    return lax.axis_size("row") == 4 and lax.axis_size("dp") == 4 and rows % 128 == 0


def place_kernel(idx, own, ring, near_x, near_y, far, *outs):
    quarter = ring.shape[0]
    begin = 0
    for out in outs:
        columns = slice(begin, begin + out.shape[1])
        begin = begin + out.shape[1]

        @pl.when(pl.program_id(0) == 0)
        def _():
            out[...] = own[:, columns]

        @pl.when(pl.program_id(0) > 0)
        def _():
            for corner, piece in enumerate((ring, near_x, near_y, far)):
                start = pl.multiple_of(idx[4 + corner] * quarter, quarter)
                out[pl.ds(start, quarter), :] = piece[:, columns]


def place(idx, own, pieces, widths):
    rows, width = own.shape
    fixed = pl.BlockSpec(own.shape, lambda s, idx: (0, 0))
    moving = pl.BlockSpec((rows // 4, width), lambda s, idx: (jnp.maximum(s - 1, 0), 0))
    return pl.pallas_call(
        place_kernel,
        grid_spec=pltpu.PrefetchScalarGridSpec(
            num_scalar_prefetch=1,
            grid=(4,),
            in_specs=[fixed, moving, moving, moving, moving],
            out_specs=[pl.BlockSpec((rows, w), lambda s, idx: (idx[s], 0)) for w in widths],
        ),
        out_shape=[jax.ShapeDtypeStruct((4 * rows, w), own.dtype) for w in widths],
        compiler_params=pltpu.CompilerParams(vmem_limit_bytes=40 << 20),
        cost_estimate=NO_COST,
    )(idx, own, *pieces)


def natural_order(whole):
    cut = whole.shape[0] // 2
    return jnp.where(
        lax.axis_index("col") == 0, whole, jnp.concatenate([whole[cut:], whole[:cut]], axis=0)
    )


def gathered(block):
    rows = block.shape[0] // lax.axis_size("dp")
    part = lax.dynamic_slice_in_dim(block, lax.axis_index("dp") * rows, rows, 0)
    return natural_order(lax.all_gather(part, ("row", "dp"), axis=0, tiled=True))


def sync_kernel(*refs):
    pass


def sync(arrays):
    arrays = list(arrays)
    return pl.pallas_call(
        sync_kernel,
        in_specs=[pl.BlockSpec(memory_space=pl.ANY)] * len(arrays),
        out_specs=[pl.BlockSpec(memory_space=pl.ANY)] * len(arrays),
        out_shape=[jax.ShapeDtypeStruct(part.shape, part.dtype) for part in arrays],
        input_output_aliases={i: i for i in range(len(arrays))},
        cost_estimate=NO_COST,
    )(*arrays)


def checkpoint(value, *movers):
    counts = [len(mover.got) for mover in movers]
    if sum(counts):
        value, *got = sync([value] + [part for mover in movers for part in mover.got])
        for mover, count in zip(movers, counts):
            mover.got, got = got[:count], got[count:]
    sends = [mover.sends() for mover in movers]
    if sum(len(some) for some in sends):
        value, *flat = sync([value] + [part for some in sends for part in some])
        for mover, some in zip(movers, sends):
            mover.go(flat[: len(some)])
            flat = flat[len(some) :]
    return value


class Gather:
    def __init__(self, group, by_shifts=False, far_too=False):
        self.group, self.by_shifts, self.far_too = group, by_shifts, far_too
        self.got = []
        self.step = 0
        self.direct = not all(is_small_grid(block.shape[0]) for block in group)
        if self.direct:
            return
        core, corner = lax.axis_index("col"), lax.axis_index("dp")
        self.level, self.size = lax.axis_index("row"), lax.axis_size("row")
        place_z = self.level + self.size // 2 * core + self.size - jnp.arange(self.size)
        self.idx = jnp.concatenate([place_z % self.size, corner ^ jnp.arange(4)]).astype(jnp.int32)
        self.own = jnp.concatenate(group, axis=1) if len(group) > 1 else group[0]
        self.quarter = self.own.shape[0] // 4
        self.parts = [
            lax.dynamic_slice_in_dim(self.own, at * self.quarter, self.quarter, 0)
            for at in ((corner, corner ^ 3) if far_too else (corner,))
        ]

    def stacked(self, count, which):
        pieces = []
        for step in (1, 2, 3):
            level = (self.level + self.size - step) % self.size
            begin = (level * count + which) * self.quarter
            pieces.append(lax.dynamic_slice_in_dim(self.got[0], begin, self.quarter, 0))
        return jnp.concatenate(pieces, axis=0)

    def sends(self):
        if self.direct:
            return []
        if self.step == 0:
            return [jnp.concatenate(self.parts, axis=0) if self.far_too else self.parts[0]]
        if self.by_shifts:
            return [jnp.concatenate(self.got, axis=0)]
        return [self.stacked(len(self.parts), which) for which in range(len(self.parts))]

    def go(self, sends):
        if self.direct:
            return
        if self.step == 0 and self.by_shifts:
            self.got = [shifted(sends[0], step) for step in (1, 2, 3)]
        elif self.step == 0:
            self.got = [lax.all_gather(sends[0], "row", axis=0, tiled=True)]
        else:
            bits = (1, 2) if self.far_too else (1, 2, 3)
            self.got = [partner(sends[0], "dp", bit) for bit in bits]
            self.mine = sends
        self.step = self.step + 1

    def result(self):
        if self.direct:
            return [gathered(block) for block in self.group]
        pieces = [self.mine[0], *self.got, *self.mine[1:]]
        return place(self.idx, self.own, pieces, [block.shape[1] for block in self.group])


def pick(values, axis, index):
    return lax.dynamic_index_in_dim(values, index, axis, keepdims=False)


def added(*parts):
    total = parts[0].astype(jnp.float32)
    for part in parts[1:]:
        total = total + part.astype(jnp.float32)
    return total.astype(jnp.bfloat16)


class Reduction:
    def __init__(self, first, second, in_halves):
        corner = lax.axis_index("dp")
        self.corner, self.a, self.b = corner, corner // 2, corner % 2
        self.direct = not is_small_grid(2 * first.shape[0] // lax.axis_size("row"))
        self.step = 0 if in_halves else 10
        self.got = []
        if self.direct:
            self.whole = jnp.concatenate([first, second], axis=0)
        else:
            width = first.shape[1]
            self.first = first.reshape(2, 2, 2, -1, width)
            self.second = second.reshape(2, 2, 2, -1, width)

    def sends(self):
        if self.direct:
            return []
        a, b = self.a, self.b
        if self.step == 0:
            return [pick(self.first, 2, 1 - b), pick(self.second, 1, 1 - a)]
        if self.step == 1:
            one, two = self.got
            self.keep = (
                pick(pick(self.first, 2, b), 1, a),
                pick(one, 1, a),
                pick(pick(self.second, 1, a), 1, b),
                pick(two, 1, b),
            )
            return [
                added(pick(pick(self.first, 2, b), 1, 1 - a), pick(one, 1, 1 - a)),
                added(pick(pick(self.second, 1, a), 1, 1 - b), pick(two, 1, 1 - b)),
            ]
        if self.step == 2:
            parts = [added(*self.keep[:2], self.got[0]), added(*self.keep[2:], self.got[1])]
            return [self.in_row_order(parts)]
        if self.step == 10:
            return [jnp.concatenate(self.quarter_of(bit), axis=0) for bit in (1, 2, 3)]
        if self.step == 11:
            parts = []
            for i, own in enumerate(self.quarter_of(0)):
                parts.append(added(own, *[got[2 * i : 2 * i + 2] for got in self.got]))
            return [self.in_row_order(parts)]
        return self.got

    def quarter_of(self, bit):
        a, b = (self.corner ^ bit) // 2, (self.corner ^ bit) % 2
        return [pick(pick(half, 2, b), 1, a) for half in (self.first, self.second)]

    def in_row_order(self, parts):
        levels = natural_order(jnp.concatenate(parts, axis=0))
        return levels.reshape(-1, levels.shape[-1])

    def go(self, sends):
        if self.direct:
            return
        if self.step == 0:
            self.got = [partner(sends[0], "dp", 1), partner(sends[1], "dp", 2)]
        elif self.step == 1:
            self.got = [partner(sends[0], "dp", 2), partner(sends[1], "dp", 1)]
        elif self.step == 10:
            self.got = [partner(part, "dp", bit) for part, bit in zip(sends, (1, 2, 3))]
        elif self.step in (2, 11):
            self.step = 2
            self.got = [lax.psum_scatter(sends[0], "row", scatter_dimension=0, tiled=True)]
        else:
            self.got = [sends[0]] + [partner(sends[0], "dp", bit) for bit in (1, 2, 3)]
        self.step = self.step + 1

    def result(self):
        if self.direct:
            whole = natural_order(self.whole)
            part = lax.psum_scatter(whole, ("row", "dp"), scatter_dimension=0, tiled=True)
            return lax.all_gather(part, "dp", axis=0, tiled=True).astype(jnp.float32)
        got = self.got
        return jnp.concatenate(
            [
                jnp.where(
                    self.a == 0,
                    jnp.where(self.b == 0, got[k], got[k ^ 1]),
                    jnp.where(self.b == 0, got[k ^ 2], got[k ^ 3]),
                )
                for k in range(4)
            ],
            axis=0,
        ).astype(jnp.float32)


class VectorSum:
    PARTNERS = (("dp", 1), ("dp", 2), ("row", 1), ("row", 2))

    def __init__(self, values):
        self.values = values.reshape(-1, 128)
        self.direct = not is_small_grid(128)
        self.got = []
        self.step = 0

    def sends(self):
        if self.direct:
            return []
        if self.got:
            self.values = self.values + self.got[0]
        return [self.values]

    def go(self, sends):
        if self.direct:
            return
        self.values = sends[0]
        self.got = [partner(sends[0], *self.PARTNERS[self.step])]
        self.step = self.step + 1

    def result(self):
        if self.direct:
            return lax.psum(self.values, ("row", "dp")).reshape(-1)
        while self.step < 4:
            self.go(self.sends())
        return (self.values + self.got[0]).reshape(-1)


def norm_forward(resid, gain, shift):
    center = jnp.mean(resid, axis=1, keepdims=True)
    inverse = lax.rsqrt(
        jnp.mean(resid * resid, axis=1, keepdims=True) - center * center + EPSILON
    )
    normed = (resid - center) * inverse
    return (normed * gain + shift, normed, inverse)


def norm_backward(grad, normed, inverse, gain):
    scaled = grad * gain
    first = jnp.mean(scaled, axis=1, keepdims=True)
    second = jnp.mean(scaled * normed, axis=1, keepdims=True)
    return inverse * (scaled - first - normed * second)


def body(
    tokens,
    segment,
    cotangent,
    w_query,
    b_query,
    w_key,
    w_value,
    b_value,
    w_out,
    b_out,
    w_up,
    b_up,
    w_down,
    b_down,
    gain_one,
    shift_one,
    gain_two,
    shift_two,
):
    half = w_query.shape[1]
    token_rows = jnp.concatenate([tokens, swapped(tokens)], axis=1)
    w_in = jnp.concatenate([w_query, w_key, w_value], axis=1)
    take_qkv = Gather([w_in], by_shifts=True)
    take_out_up = Gather([w_out, w_up])
    take_down = Gather([w_down], far_too=True)
    take_qkv.go(take_qkv.sends())
    token_rows = checkpoint(token_rows, take_qkv, take_out_up, take_down)
    (w_qkv,) = take_qkv.result()
    cotangent_rows = jnp.concatenate([cotangent, swapped(cotangent)], axis=1)
    own_vectors = jnp.stack([b_out, b_down, gain_one, shift_one, gain_two, shift_two])
    vectors = jnp.concatenate([own_vectors, swapped(own_vectors)], axis=1).astype(jnp.float32)
    bias_out, bias_down, gain1, shift1, gain2, shift2 = [vectors[i] for i in range(6)]
    b_qkv = jnp.concatenate([b_query, jnp.zeros_like(b_query), b_value]).astype(jnp.float32)
    qkv = (matmul(token_rows, w_qkv) + b_qkv).astype(jnp.bfloat16)
    qkv = checkpoint(qkv, take_out_up)
    context, lse_rows = attend(qkv, segment)
    context_rows = jnp.concatenate([context, swapped(context)], axis=1)
    context_rows = checkpoint(context_rows, take_down)
    wo_half, wu = take_out_up.result()
    wo_other = swapped(wo_half)
    wo = jnp.concatenate(
        [wo_half, jnp.concatenate([wo_other[half:], wo_other[:half]], axis=0)], axis=1
    )
    first_sum = token_rows.astype(jnp.float32) + (matmul(context_rows, wo) + bias_out)
    hidden_f, normed_one, inverse_one = norm_forward(first_sum, gain1, shift1)
    hidden = hidden_f.astype(jnp.bfloat16)
    pre_act = matmul(hidden, wu) + b_up.astype(jnp.float32)
    cdf = 0.5 * (1.0 + lax.erf(pre_act * (0.5**0.5)))
    activated = (pre_act * cdf).astype(jnp.bfloat16)
    slope = cdf + pre_act * (jnp.exp(-0.5 * pre_act * pre_act) * 0.3989422804014327)
    (wd_half,) = take_down.result()
    units = w_up.shape[1]
    wd = jnp.concatenate([wd_half[:units], swapped(wd_half[units:])], axis=1)
    part = matmul(activated, wd).astype(jnp.bfloat16)
    ffn_out = part.astype(jnp.float32) + swapped_rows(part) + bias_down
    second_sum = hidden.astype(jnp.float32) + ffn_out
    final, normed_two, inverse_two = norm_forward(second_sum, gain2, shift2)
    output = final[:, :half].astype(jnp.bfloat16)
    y = cotangent_rows.astype(jnp.float32)
    second_grad = norm_backward(y, normed_two, inverse_two, gain2)
    d_gain_two = jnp.sum(y * normed_two, axis=0)
    d_shift_two = jnp.sum(y, axis=0)
    ffn_grad = second_grad.astype(jnp.bfloat16)
    d_down_other = swapped(matmul_tn(activated, ffn_grad[:, half:]).astype(jnp.bfloat16))
    d_down_own = matmul_tn(activated, ffn_grad[:, :half]).astype(jnp.bfloat16)
    d_b_down = column_sum(ffn_grad)
    pre_grad = (matmul_nt(ffn_grad, wd) * slope).astype(jnp.bfloat16)
    d_b_up = column_sum(pre_grad)
    down = Reduction(d_down_own, d_down_other, in_halves=True)
    pre_grad = checkpoint(pre_grad, down)
    hidden_part = matmul_nt(pre_grad, wu).astype(jnp.bfloat16)
    hidden_other = swapped_rows(hidden_part)
    d_w_up = matmul_tn(hidden, pre_grad).astype(jnp.bfloat16)
    hidden_grad = second_grad + (hidden_part.astype(jnp.float32) + hidden_other)
    first_grad = norm_backward(hidden_grad, normed_one, inverse_one, gain1)
    d_gain_one = jnp.sum(hidden_grad * normed_one, axis=0)
    d_shift_one = jnp.sum(hidden_grad, axis=0)
    branch_grad = first_grad.astype(jnp.bfloat16)
    d_b_out = column_sum(branch_grad)
    wide = jnp.stack([d_b_out, d_b_down, d_gain_one, d_shift_one, d_gain_two, d_shift_two])
    context_grad = matmul_nt(branch_grad, wo[:half]).astype(jnp.bfloat16)
    d_w_out = matmul_tn(context_rows, branch_grad[:, :half]).astype(jnp.bfloat16)
    d_out_up = jnp.concatenate([d_w_out, d_w_up], axis=1)
    out_up = Reduction(d_out_up[:half], d_out_up[half:], in_halves=True)
    context_grad = checkpoint(context_grad, down, out_up)
    qkv_grad = jnp.concatenate(attend_back(qkv, segment, lse_rows, context_grad, 0, 1), axis=1)
    d_w_qkv = matmul_tn(token_rows, qkv_grad).astype(jnp.bfloat16)
    d_b_qkv = column_sum(qkv_grad)
    proj = Reduction(d_w_qkv[:half], d_w_qkv[half:], in_halves=False)
    vector = VectorSum(
        jnp.concatenate(
            [wide[:, :half].reshape(-1), d_b_qkv[:half], d_b_qkv[2 * half :], d_b_up]
        )
    )
    qkv_grad = checkpoint(qkv_grad, down, out_up, proj, vector)
    token_part = matmul_nt(qkv_grad, w_qkv).astype(jnp.bfloat16)
    token_other = swapped(token_part[:, half:])
    token_sum = token_part[:, :half].astype(jnp.float32) + token_other.astype(jnp.float32)
    d_tokens = (token_sum + first_grad[:, :half]).astype(jnp.bfloat16)
    d_tokens = checkpoint(d_tokens, down, out_up, vector)
    d_tokens = checkpoint(d_tokens, proj, vector)
    d_tokens = checkpoint(d_tokens, out_up, vector)
    d_tokens = checkpoint(d_tokens, proj)
    o_w_down, o_w_out_up, o_w_qkv = down.result(), out_up.result(), proj.result()
    sums = vector.result()
    pieces = [sums[i * half : (i + 1) * half] for i in range(8)]
    return (
        output,
        d_tokens,
        o_w_qkv[:, :half],
        pieces[6],
        o_w_qkv[:, half : 2 * half],
        o_w_qkv[:, 2 * half :],
        pieces[7],
        o_w_out_up[:, :half],
        pieces[0],
        o_w_out_up[:, half:],
        sums[8 * half :],
        o_w_down,
        pieces[1],
        pieces[2],
        pieces[3],
        pieces[4],
        pieces[5],
    )


def solution(mesh):
    in_specs = (
        P(("dp", "row"), "col"),
        P(("dp", "row"), None),
        P(("dp", "row"), "col"),
        P("row", "col"),
        P("col"),
        P("row", "col"),
        P("row", "col"),
        P("col"),
        P("row", "col"),
        P("col"),
        P("row", "col"),
        P("col"),
        P("row", "col"),
        P("col"),
        P("col"),
        P("col"),
        P("col"),
        P("col"),
    )
    out_specs = (
        P(("dp", "row"), "col"),
        P(("dp", "row"), "col"),
        P("row", "col"),
        P("col"),
        P("row", "col"),
        P("row", "col"),
        P("col"),
        P("row", "col"),
        P("col"),
        P("row", "col"),
        P("col"),
        P("row", "col"),
        P("col"),
        P("col"),
        P("col"),
        P("col"),
        P("col"),
    )
    return jax.shard_map(body, mesh=mesh, in_specs=in_specs, out_specs=out_specs, check_vma=False)
```

```python
import jax
import jax.numpy as jnp
from jax import lax
from jax.experimental import pallas as pl
from jax.experimental.pallas import tpu as pltpu
from jax.sharding import PartitionSpec as P

HEAD_DIM = 64


EPSILON = 1e-05
SCALE = 0.125
LOG2E = 1.4426950408889634
PAIR = 2 * HEAD_DIM
Q_BLOCK = 256
NO_COST = pl.CostEstimate(flops=0, bytes_accessed=0, transcendentals=0)


def dot_nt(left, right):
    return lax.dot_general(
        left, right, (((1,), (1,)), ((), ())), preferred_element_type=jnp.float32
    )


def dot_nn(left, right):
    return lax.dot_general(
        left, right, (((1,), (0,)), ((), ())), preferred_element_type=jnp.float32
    )


def only_head(block, head):
    lane = lax.broadcasted_iota(jnp.int32, block.shape, 1)
    return jnp.where(lane // HEAD_DIM == head, block, jnp.zeros_like(block))


def attend_kernel(seg_col, seg_row, q_ref, k_ref, v_ref, ctx_ref, lse_ref, vt_ref):
    @pl.when(pl.program_id(1) == 0)
    def _():
        vt_ref[...] = v_ref[...].T

    same = seg_col[...] == seg_row[...]
    parts = []
    for head in range(2):
        scores = dot_nt(k_ref[...], only_head(q_ref[...], head)) * (SCALE * LOG2E)
        scores = jnp.where(same, scores, -1e30)
        top = jnp.max(scores, axis=0, keepdims=True)
        expo = jnp.exp2(scores - top)
        total = jnp.sum(expo, axis=0, keepdims=True)
        out = dot_nn(
            vt_ref[head * HEAD_DIM : (head + 1) * HEAD_DIM, :], expo.astype(jnp.bfloat16)
        )
        parts.append(out / total)
        lse_ref[0, head : head + 1, :] = top + jnp.log2(total)
    ctx_ref[...] = jnp.concatenate(parts, axis=0).T.astype(jnp.bfloat16)


def attend_back_kernel(
    seg_col, seg_row, q_ref, k_ref, v_ref, lse_ref, do_ref, dq_ref, dk_ref, dv_ref, kt_ref, dk_acc, dv_acc
):
    step = pl.program_id(1)

    @pl.when(step == 0)
    def _():
        kt_ref[...] = k_ref[...].T
        dk_acc[...] = jnp.zeros_like(dk_acc)
        dv_acc[...] = jnp.zeros_like(dv_acc)

    same = seg_col[...] == seg_row[...]
    parts = []
    for head in range(2):
        query = only_head(q_ref[...], head)
        grad = only_head(do_ref[...], head)
        scores = dot_nt(k_ref[...], query) * (SCALE * LOG2E)
        probs = jnp.where(same, jnp.exp2(scores - lse_ref[0, head : head + 1, :]), 0.0)
        d_probs = dot_nt(v_ref[...], grad)
        inner = jnp.sum(probs * d_probs, axis=0, keepdims=True)
        d_scores = (probs * (d_probs - inner)).astype(jnp.bfloat16)
        dv_acc[...] += dot_nn(probs.astype(jnp.bfloat16), grad)
        dk_acc[...] += dot_nn(d_scores, query)
        parts.append(
            dot_nn(kt_ref[head * HEAD_DIM : (head + 1) * HEAD_DIM, :], d_scores)
        )
    dq_ref[...] = (jnp.concatenate(parts, axis=0) * SCALE).T.astype(jnp.bfloat16)

    @pl.when(step == pl.num_programs(1) - 1)
    def _():
        dk_ref[...] = (dk_acc[...] * SCALE).astype(jnp.bfloat16)
        dv_ref[...] = dv_acc[...].astype(jnp.bfloat16)


def attention_specs(count, pairs, block, skip=0):
    seg_col = pl.BlockSpec((count, 1), lambda h, i: (0, 0))
    seg_row = pl.BlockSpec((1, block), lambda h, i: (0, i))
    query = pl.BlockSpec((block, PAIR), lambda h, i: (i, skip + h))
    key = pl.BlockSpec((count, PAIR), lambda h, i: (0, pairs + skip + h))
    value = pl.BlockSpec((count, PAIR), lambda h, i: (0, 2 * pairs + skip + h))
    lse = pl.BlockSpec((1, 2, block), lambda h, i: (skip + h, 0, i))
    return seg_col, seg_row, query, key, value, lse


def attention_cost(count, pairs, products):
    return pl.CostEstimate(
        flops=products * count * count * PAIR * pairs,
        bytes_accessed=20 * count * pairs * PAIR,
        transcendentals=2 * count * count * pairs,
    )


def attend(qkv, segment):
    count = qkv.shape[0]
    pairs = qkv.shape[1] // (3 * PAIR)
    block = min(Q_BLOCK, count)
    seg_col, seg_row, query, key, value, lse = attention_specs(count, pairs, block)
    return pl.pallas_call(
        attend_kernel,
        grid=(pairs, count // block),
        in_specs=[seg_col, seg_row, query, key, value],
        out_specs=[query, lse],
        out_shape=[
            jax.ShapeDtypeStruct((count, pairs * PAIR), jnp.bfloat16),
            jax.ShapeDtypeStruct((pairs, 2, count), jnp.float32),
        ],
        scratch_shapes=[pltpu.VMEM((PAIR, count), jnp.bfloat16)],
        compiler_params=pltpu.CompilerParams(vmem_limit_bytes=32 << 20),
        cost_estimate=attention_cost(count, pairs, 64),
    )(segment.reshape(-1, 1), segment, qkv, qkv, qkv)


def attend_back(qkv, segment, lse_rows, d_context, turn, turns):
    count = qkv.shape[0]
    pairs = qkv.shape[1] // (3 * PAIR)
    here = pairs // turns
    block = min(Q_BLOCK, count)
    seg_col, seg_row, query, key, value, lse = attention_specs(count, pairs, block, turn * here)
    d_query = pl.BlockSpec((block, PAIR), lambda h, i: (i, h))
    d_whole = pl.BlockSpec((count, PAIR), lambda h, i: (0, h))
    shape = jax.ShapeDtypeStruct((count, here * PAIR), jnp.bfloat16)
    return pl.pallas_call(
        attend_back_kernel,
        grid=(here, count // block),
        in_specs=[seg_col, seg_row, query, key, value, lse, query],
        out_specs=[d_query, d_whole, d_whole],
        out_shape=[shape, shape, shape],
        scratch_shapes=[
            pltpu.VMEM((PAIR, count), jnp.bfloat16),
            pltpu.VMEM((count, PAIR), jnp.float32),
            pltpu.VMEM((count, PAIR), jnp.float32),
        ],
        compiler_params=pltpu.CompilerParams(vmem_limit_bytes=32 << 20),
        cost_estimate=attention_cost(count, here, 11),
    )(segment.reshape(-1, 1), segment, qkv, qkv, qkv, lse_rows, d_context)


def matmul(left, right):
    return jnp.dot(left, right, preferred_element_type=jnp.float32)


def matmul_tn(left, right):
    return lax.dot_general(
        left, right, (((0,), (0,)), ((), ())), preferred_element_type=jnp.float32
    )


def matmul_nt(left, right):
    return lax.dot_general(
        left, right, (((1,), (1,)), ((), ())), preferred_element_type=jnp.float32
    )


def column_sum(values):
    return jnp.sum(values.astype(jnp.float32), axis=0)


def swapped(part):
    return lax.ppermute(part, "col", [(0, 1), (1, 0)])


def swapped_rows(part):
    other = swapped(part)
    cut = other.shape[1] // 2
    return jnp.concatenate([other[:, cut:], other[:, :cut]], axis=1).astype(jnp.float32)


def partner(part, axis, bit):
    size = lax.axis_size(axis)
    return lax.ppermute(part, axis, [(i, i ^ bit) for i in range(size)])


def shifted(part, step):
    size = lax.axis_size("row")
    return lax.ppermute(part, "row", [(i, (i + step) % size) for i in range(size)])


def is_small_grid(rows):
    return lax.axis_size("row") == 4 and lax.axis_size("dp") == 4 and rows % 128 == 0


def place_kernel(idx, own, ring, near_x, near_y, far, *outs):
    quarter = ring.shape[0]
    begin = 0
    for out in outs:
        columns = slice(begin, begin + out.shape[1])
        begin = begin + out.shape[1]

        @pl.when(pl.program_id(0) == 0)
        def _():
            out[...] = own[:, columns]

        @pl.when(pl.program_id(0) > 0)
        def _():
            for corner, piece in enumerate((ring, near_x, near_y, far)):
                start = pl.multiple_of(idx[4 + corner] * quarter, quarter)
                out[pl.ds(start, quarter), :] = piece[:, columns]


def place(idx, own, pieces, widths):
    rows, width = own.shape
    fixed = pl.BlockSpec(own.shape, lambda s, idx: (0, 0))
    moving = pl.BlockSpec((rows // 4, width), lambda s, idx: (jnp.maximum(s - 1, 0), 0))
    return pl.pallas_call(
        place_kernel,
        grid_spec=pltpu.PrefetchScalarGridSpec(
            num_scalar_prefetch=1,
            grid=(4,),
            in_specs=[fixed, moving, moving, moving, moving],
            out_specs=[pl.BlockSpec((rows, w), lambda s, idx: (idx[s], 0)) for w in widths],
        ),
        out_shape=[jax.ShapeDtypeStruct((4 * rows, w), own.dtype) for w in widths],
        compiler_params=pltpu.CompilerParams(vmem_limit_bytes=40 << 20),
        cost_estimate=NO_COST,
    )(idx, own, *pieces)


def natural_order(whole):
    cut = whole.shape[0] // 2
    return jnp.where(
        lax.axis_index("col") == 0, whole, jnp.concatenate([whole[cut:], whole[:cut]], axis=0)
    )


def gathered(block):
    rows = block.shape[0] // lax.axis_size("dp")
    part = lax.dynamic_slice_in_dim(block, lax.axis_index("dp") * rows, rows, 0)
    return natural_order(lax.all_gather(part, ("row", "dp"), axis=0, tiled=True))


def sync_kernel(*refs):
    pass


def sync(arrays):
    arrays = list(arrays)
    return pl.pallas_call(
        sync_kernel,
        in_specs=[pl.BlockSpec(memory_space=pl.ANY)] * len(arrays),
        out_specs=[pl.BlockSpec(memory_space=pl.ANY)] * len(arrays),
        out_shape=[jax.ShapeDtypeStruct(part.shape, part.dtype) for part in arrays],
        input_output_aliases={i: i for i in range(len(arrays))},
        cost_estimate=NO_COST,
    )(*arrays)


def checkpoint(value, *movers):
    counts = [len(mover.got) for mover in movers]
    if sum(counts):
        value, *got = sync([value] + [part for mover in movers for part in mover.got])
        for mover, count in zip(movers, counts):
            mover.got, got = got[:count], got[count:]
    sends = [mover.sends() for mover in movers]
    if sum(len(some) for some in sends):
        value, *flat = sync([value] + [part for some in sends for part in some])
        for mover, some in zip(movers, sends):
            mover.go(flat[: len(some)])
            flat = flat[len(some) :]
    return value


class Gather:
    def __init__(self, group, by_shifts=False, far_too=False):
        self.group, self.by_shifts, self.far_too = group, by_shifts, far_too
        self.got = []
        self.step = 0
        self.direct = not all(is_small_grid(block.shape[0]) for block in group)
        if self.direct:
            return
        core, corner = lax.axis_index("col"), lax.axis_index("dp")
        self.level, self.size = lax.axis_index("row"), lax.axis_size("row")
        place_z = self.level + self.size // 2 * core + self.size - jnp.arange(self.size)
        self.idx = jnp.concatenate([place_z % self.size, corner ^ jnp.arange(4)]).astype(jnp.int32)
        self.own = jnp.concatenate(group, axis=1) if len(group) > 1 else group[0]
        self.quarter = self.own.shape[0] // 4
        self.parts = [
            lax.dynamic_slice_in_dim(self.own, at * self.quarter, self.quarter, 0)
            for at in ((corner, corner ^ 3) if far_too else (corner,))
        ]

    def stacked(self, count, which):
        pieces = []
        for step in (1, 2, 3):
            level = (self.level + self.size - step) % self.size
            begin = (level * count + which) * self.quarter
            pieces.append(lax.dynamic_slice_in_dim(self.got[0], begin, self.quarter, 0))
        return jnp.concatenate(pieces, axis=0)

    def sends(self):
        if self.direct:
            return []
        if self.step == 0:
            return [jnp.concatenate(self.parts, axis=0) if self.far_too else self.parts[0]]
        if self.by_shifts:
            return [jnp.concatenate(self.got, axis=0)]
        return [self.stacked(len(self.parts), which) for which in range(len(self.parts))]

    def go(self, sends):
        if self.direct:
            return
        if self.step == 0 and self.by_shifts:
            self.got = [shifted(sends[0], step) for step in (1, 2, 3)]
        elif self.step == 0:
            self.got = [lax.all_gather(sends[0], "row", axis=0, tiled=True)]
        else:
            bits = (1, 2) if self.far_too else (1, 2, 3)
            self.got = [partner(sends[0], "dp", bit) for bit in bits]
            self.mine = sends
        self.step = self.step + 1

    def result(self):
        if self.direct:
            return [gathered(block) for block in self.group]
        pieces = [self.mine[0], *self.got, *self.mine[1:]]
        return place(self.idx, self.own, pieces, [block.shape[1] for block in self.group])


def pick(values, axis, index):
    return lax.dynamic_index_in_dim(values, index, axis, keepdims=False)


def added(*parts):
    total = parts[0].astype(jnp.float32)
    for part in parts[1:]:
        total = total + part.astype(jnp.float32)
    return total.astype(jnp.bfloat16)


class Reduction:
    def __init__(self, first, second, in_halves):
        corner = lax.axis_index("dp")
        self.corner, self.a, self.b = corner, corner // 2, corner % 2
        self.direct = not is_small_grid(2 * first.shape[0] // lax.axis_size("row"))
        self.step = 0 if in_halves else 10
        self.got = []
        if self.direct:
            self.whole = jnp.concatenate([first, second], axis=0)
        else:
            width = first.shape[1]
            self.first = first.reshape(2, 2, 2, -1, width)
            self.second = second.reshape(2, 2, 2, -1, width)

    def sends(self):
        if self.direct:
            return []
        a, b = self.a, self.b
        if self.step == 0:
            return [pick(self.first, 2, 1 - b), pick(self.second, 1, 1 - a)]
        if self.step == 1:
            one, two = self.got
            self.keep = (
                pick(pick(self.first, 2, b), 1, a),
                pick(one, 1, a),
                pick(pick(self.second, 1, a), 1, b),
                pick(two, 1, b),
            )
            return [
                added(pick(pick(self.first, 2, b), 1, 1 - a), pick(one, 1, 1 - a)),
                added(pick(pick(self.second, 1, a), 1, 1 - b), pick(two, 1, 1 - b)),
            ]
        if self.step == 2:
            parts = [added(*self.keep[:2], self.got[0]), added(*self.keep[2:], self.got[1])]
            return [self.in_row_order(parts)]
        if self.step == 10:
            return [jnp.concatenate(self.quarter_of(bit), axis=0) for bit in (1, 2, 3)]
        if self.step == 11:
            parts = []
            for i, own in enumerate(self.quarter_of(0)):
                parts.append(added(own, *[got[2 * i : 2 * i + 2] for got in self.got]))
            return [self.in_row_order(parts)]
        return self.got

    def quarter_of(self, bit):
        a, b = (self.corner ^ bit) // 2, (self.corner ^ bit) % 2
        return [pick(pick(half, 2, b), 1, a) for half in (self.first, self.second)]

    def in_row_order(self, parts):
        levels = natural_order(jnp.concatenate(parts, axis=0))
        return levels.reshape(-1, levels.shape[-1])

    def go(self, sends):
        if self.direct:
            return
        if self.step == 0:
            self.got = [partner(sends[0], "dp", 1), partner(sends[1], "dp", 2)]
        elif self.step == 1:
            self.got = [partner(sends[0], "dp", 2), partner(sends[1], "dp", 1)]
        elif self.step == 10:
            self.got = [partner(part, "dp", bit) for part, bit in zip(sends, (1, 2, 3))]
        elif self.step in (2, 11):
            self.step = 2
            self.got = [lax.psum_scatter(sends[0], "row", scatter_dimension=0, tiled=True)]
        else:
            self.got = [sends[0]] + [partner(sends[0], "dp", bit) for bit in (1, 2, 3)]
        self.step = self.step + 1

    def result(self):
        if self.direct:
            whole = natural_order(self.whole)
            part = lax.psum_scatter(whole, ("row", "dp"), scatter_dimension=0, tiled=True)
            return lax.all_gather(part, "dp", axis=0, tiled=True).astype(jnp.float32)
        got = self.got
        return jnp.concatenate(
            [
                jnp.where(
                    self.a == 0,
                    jnp.where(self.b == 0, got[k], got[k ^ 1]),
                    jnp.where(self.b == 0, got[k ^ 2], got[k ^ 3]),
                )
                for k in range(4)
            ],
            axis=0,
        ).astype(jnp.float32)


class VectorSum:
    PARTNERS = (("dp", 1), ("dp", 2), ("row", 1), ("row", 2))

    def __init__(self, values):
        self.values = values.reshape(-1, 128)
        self.direct = not is_small_grid(128)
        self.got = []
        self.step = 0

    def sends(self):
        if self.direct:
            return []
        if self.got:
            self.values = self.values + self.got[0]
        return [self.values]

    def go(self, sends):
        if self.direct:
            return
        self.values = sends[0]
        self.got = [partner(sends[0], *self.PARTNERS[self.step])]
        self.step = self.step + 1

    def result(self):
        if self.direct:
            return lax.psum(self.values, ("row", "dp")).reshape(-1)
        while self.step < 4:
            self.go(self.sends())
        return (self.values + self.got[0]).reshape(-1)


def norm_forward(resid, gain, shift):
    center = jnp.mean(resid, axis=1, keepdims=True)
    inverse = lax.rsqrt(
        jnp.mean(resid * resid, axis=1, keepdims=True) - center * center + EPSILON
    )
    normed = (resid - center) * inverse
    return (normed * gain + shift, normed, inverse)


def norm_backward(grad, normed, inverse, gain):
    scaled = grad * gain
    first = jnp.mean(scaled, axis=1, keepdims=True)
    second = jnp.mean(scaled * normed, axis=1, keepdims=True)
    return inverse * (scaled - first - normed * second)


def body(
    tokens,
    segment,
    cotangent,
    w_query,
    b_query,
    w_key,
    w_value,
    b_value,
    w_out,
    b_out,
    w_up,
    b_up,
    w_down,
    b_down,
    gain_one,
    shift_one,
    gain_two,
    shift_two,
):
    half = w_query.shape[1]
    token_rows = jnp.concatenate([tokens, swapped(tokens)], axis=1)
    w_in = jnp.concatenate([w_query, w_key, w_value], axis=1)
    take_qkv = Gather([w_in], by_shifts=True)
    take_out_up = Gather([w_out, w_up])
    take_down = Gather([w_down], far_too=True)
    take_qkv.go(take_qkv.sends())
    token_rows = checkpoint(token_rows, take_qkv, take_out_up, take_down)
    (w_qkv,) = take_qkv.result()
    cotangent_rows = jnp.concatenate([cotangent, swapped(cotangent)], axis=1)
    own_vectors = jnp.stack([b_out, b_down, gain_one, shift_one, gain_two, shift_two])
    vectors = jnp.concatenate([own_vectors, swapped(own_vectors)], axis=1).astype(jnp.float32)
    bias_out, bias_down, gain1, shift1, gain2, shift2 = [vectors[i] for i in range(6)]
    b_qkv = jnp.concatenate([b_query, jnp.zeros_like(b_query), b_value]).astype(jnp.float32)
    qkv = (matmul(token_rows, w_qkv) + b_qkv).astype(jnp.bfloat16)
    qkv = checkpoint(qkv, take_out_up)
    context, lse_rows = attend(qkv, segment)
    context_rows = jnp.concatenate([context, swapped(context)], axis=1)
    context_rows = checkpoint(context_rows, take_down)
    wo_half, wu = take_out_up.result()
    wo_other = swapped(wo_half)
    wo = jnp.concatenate(
        [wo_half, jnp.concatenate([wo_other[half:], wo_other[:half]], axis=0)], axis=1
    )
    first_sum = token_rows.astype(jnp.float32) + (matmul(context_rows, wo) + bias_out)
    hidden_f, normed_one, inverse_one = norm_forward(first_sum, gain1, shift1)
    hidden = hidden_f.astype(jnp.bfloat16)
    pre_act = matmul(hidden, wu) + b_up.astype(jnp.float32)
    cdf = 0.5 * (1.0 + lax.erf(pre_act * (0.5**0.5)))
    activated = (pre_act * cdf).astype(jnp.bfloat16)
    slope = cdf + pre_act * (jnp.exp(-0.5 * pre_act * pre_act) * 0.3989422804014327)
    (wd_half,) = take_down.result()
    units = w_up.shape[1]
    wd = jnp.concatenate([wd_half[:units], swapped(wd_half[units:])], axis=1)
    part = matmul(activated, wd).astype(jnp.bfloat16)
    ffn_out = part.astype(jnp.float32) + swapped_rows(part) + bias_down
    second_sum = hidden.astype(jnp.float32) + ffn_out
    final, normed_two, inverse_two = norm_forward(second_sum, gain2, shift2)
    output = final[:, :half].astype(jnp.bfloat16)
    y = cotangent_rows.astype(jnp.float32)
    second_grad = norm_backward(y, normed_two, inverse_two, gain2)
    d_gain_two = jnp.sum(y * normed_two, axis=0)
    d_shift_two = jnp.sum(y, axis=0)
    ffn_grad = second_grad.astype(jnp.bfloat16)
    d_down_other = swapped(matmul_tn(activated, ffn_grad[:, half:]).astype(jnp.bfloat16))
    d_down_own = matmul_tn(activated, ffn_grad[:, :half]).astype(jnp.bfloat16)
    d_b_down = column_sum(ffn_grad)
    pre_grad = (matmul_nt(ffn_grad, wd) * slope).astype(jnp.bfloat16)
    d_b_up = column_sum(pre_grad)
    down = Reduction(d_down_own, d_down_other, in_halves=True)
    pre_grad = checkpoint(pre_grad, down)
    hidden_part = matmul_nt(pre_grad, wu).astype(jnp.bfloat16)
    hidden_other = swapped_rows(hidden_part)
    d_w_up = matmul_tn(hidden, pre_grad).astype(jnp.bfloat16)
    up = Reduction(d_w_up[:half], d_w_up[half:], in_halves=True)
    hidden_part = checkpoint(hidden_part, up)
    hidden_grad = second_grad + (hidden_part.astype(jnp.float32) + hidden_other)
    first_grad = norm_backward(hidden_grad, normed_one, inverse_one, gain1)
    d_gain_one = jnp.sum(hidden_grad * normed_one, axis=0)
    d_shift_one = jnp.sum(hidden_grad, axis=0)
    branch_grad = first_grad.astype(jnp.bfloat16)
    d_b_out = column_sum(branch_grad)
    wide = jnp.stack([d_b_out, d_b_down, d_gain_one, d_shift_one, d_gain_two, d_shift_two])
    context_grad = matmul_nt(branch_grad, wo[:half]).astype(jnp.bfloat16)
    d_w_out = matmul_tn(context_rows, branch_grad[:, :half]).astype(jnp.bfloat16)
    context_grad = checkpoint(context_grad, down)
    qkv_grad = jnp.concatenate(attend_back(qkv, segment, lse_rows, context_grad, 0, 1), axis=1)
    qkv_grad = checkpoint(qkv_grad, down, up)
    d_w_qkv = matmul_tn(token_rows, qkv_grad).astype(jnp.bfloat16)
    d_b_qkv = column_sum(qkv_grad)
    d_last = jnp.concatenate([d_w_out, d_w_qkv], axis=1)
    last = Reduction(d_last[:half], d_last[half:], in_halves=False)
    vector = VectorSum(
        jnp.concatenate(
            [wide[:, :half].reshape(-1), d_b_qkv[:half], d_b_qkv[2 * half :], d_b_up]
        )
    )
    token = checkpoint(d_b_qkv[:128].reshape(1, 128), last, vector)
    token_part = matmul_nt(qkv_grad, w_qkv).astype(jnp.bfloat16)
    token_other = swapped(token_part[:, half:])
    token_sum = token_part[:, :half].astype(jnp.float32) + token_other.astype(jnp.float32)
    d_tokens = (token_sum + first_grad[:, :half]).astype(jnp.bfloat16)
    token = checkpoint(token, up, vector)
    token = checkpoint(token, last, down, vector)
    token = checkpoint(token, up, vector)
    token = checkpoint(token, last)
    o_w_down, o_w_up, o_last = down.result(), up.result(), last.result()
    sums = vector.result()
    pieces = [sums[i * half : (i + 1) * half] for i in range(8)]
    return (
        output,
        d_tokens,
        o_last[:, half : 2 * half],
        pieces[6],
        o_last[:, 2 * half : 3 * half],
        o_last[:, 3 * half :],
        pieces[7],
        o_last[:, :half],
        pieces[0],
        o_w_up,
        sums[8 * half :],
        o_w_down,
        pieces[1],
        pieces[2],
        pieces[3],
        pieces[4],
        pieces[5],
    )


def solution(mesh):
    in_specs = (
        P(("dp", "row"), "col"),
        P(("dp", "row"), None),
        P(("dp", "row"), "col"),
        P("row", "col"),
        P("col"),
        P("row", "col"),
        P("row", "col"),
        P("col"),
        P("row", "col"),
        P("col"),
        P("row", "col"),
        P("col"),
        P("row", "col"),
        P("col"),
        P("col"),
        P("col"),
        P("col"),
        P("col"),
    )
    out_specs = (
        P(("dp", "row"), "col"),
        P(("dp", "row"), "col"),
        P("row", "col"),
        P("col"),
        P("row", "col"),
        P("row", "col"),
        P("col"),
        P("row", "col"),
        P("col"),
        P("row", "col"),
        P("col"),
        P("row", "col"),
        P("col"),
        P("col"),
        P("col"),
        P("col"),
        P("col"),
    )
    return jax.shard_map(body, mesh=mesh, in_specs=in_specs, out_specs=out_specs, check_vma=False)
```

```python
import jax
import jax.numpy as jnp
from jax import lax
from jax.experimental import pallas as pl
from jax.experimental.pallas import tpu as pltpu
from jax.sharding import PartitionSpec as P

HEAD_DIM = 64


EPSILON = 1e-05
SCALE = 0.125
LOG2E = 1.4426950408889634
PAIR = 2 * HEAD_DIM
Q_BLOCK = 256
NO_COST = pl.CostEstimate(flops=0, bytes_accessed=0, transcendentals=0)


def dot_nt(left, right):
    return lax.dot_general(
        left, right, (((1,), (1,)), ((), ())), preferred_element_type=jnp.float32
    )


def dot_nn(left, right):
    return lax.dot_general(
        left, right, (((1,), (0,)), ((), ())), preferred_element_type=jnp.float32
    )


def only_head(block, head):
    lane = lax.broadcasted_iota(jnp.int32, block.shape, 1)
    return jnp.where(lane // HEAD_DIM == head, block, jnp.zeros_like(block))


def attend_kernel(seg_col, seg_row, q_ref, k_ref, v_ref, ctx_ref, lse_ref, vt_ref):
    @pl.when(pl.program_id(1) == 0)
    def _():
        vt_ref[...] = v_ref[...].T

    same = seg_col[...] == seg_row[...]
    parts = []
    for head in range(2):
        scores = dot_nt(k_ref[...], only_head(q_ref[...], head)) * (SCALE * LOG2E)
        scores = jnp.where(same, scores, -1e30)
        top = jnp.max(scores, axis=0, keepdims=True)
        expo = jnp.exp2(scores - top)
        total = jnp.sum(expo, axis=0, keepdims=True)
        out = dot_nn(
            vt_ref[head * HEAD_DIM : (head + 1) * HEAD_DIM, :], expo.astype(jnp.bfloat16)
        )
        parts.append(out / total)
        lse_ref[0, head : head + 1, :] = top + jnp.log2(total)
    ctx_ref[...] = jnp.concatenate(parts, axis=0).T.astype(jnp.bfloat16)


def attend_back_kernel(
    seg_col, seg_row, q_ref, k_ref, v_ref, lse_ref, do_ref, dq_ref, dk_ref, dv_ref, kt_ref, dk_acc, dv_acc
):
    step = pl.program_id(1)

    @pl.when(step == 0)
    def _():
        kt_ref[...] = k_ref[...].T
        dk_acc[...] = jnp.zeros_like(dk_acc)
        dv_acc[...] = jnp.zeros_like(dv_acc)

    same = seg_col[...] == seg_row[...]
    parts = []
    for head in range(2):
        query = only_head(q_ref[...], head)
        grad = only_head(do_ref[...], head)
        scores = dot_nt(k_ref[...], query) * (SCALE * LOG2E)
        probs = jnp.where(same, jnp.exp2(scores - lse_ref[0, head : head + 1, :]), 0.0)
        d_probs = dot_nt(v_ref[...], grad)
        inner = jnp.sum(probs * d_probs, axis=0, keepdims=True)
        d_scores = (probs * (d_probs - inner)).astype(jnp.bfloat16)
        dv_acc[...] += dot_nn(probs.astype(jnp.bfloat16), grad)
        dk_acc[...] += dot_nn(d_scores, query)
        parts.append(
            dot_nn(kt_ref[head * HEAD_DIM : (head + 1) * HEAD_DIM, :], d_scores)
        )
    dq_ref[...] = (jnp.concatenate(parts, axis=0) * SCALE).T.astype(jnp.bfloat16)

    @pl.when(step == pl.num_programs(1) - 1)
    def _():
        dk_ref[...] = (dk_acc[...] * SCALE).astype(jnp.bfloat16)
        dv_ref[...] = dv_acc[...].astype(jnp.bfloat16)


def attention_specs(count, pairs, block, skip=0):
    seg_col = pl.BlockSpec((count, 1), lambda h, i: (0, 0))
    seg_row = pl.BlockSpec((1, block), lambda h, i: (0, i))
    query = pl.BlockSpec((block, PAIR), lambda h, i: (i, skip + h))
    key = pl.BlockSpec((count, PAIR), lambda h, i: (0, pairs + skip + h))
    value = pl.BlockSpec((count, PAIR), lambda h, i: (0, 2 * pairs + skip + h))
    lse = pl.BlockSpec((1, 2, block), lambda h, i: (skip + h, 0, i))
    return seg_col, seg_row, query, key, value, lse


def attention_cost(count, pairs, products):
    return pl.CostEstimate(
        flops=products * count * count * PAIR * pairs,
        bytes_accessed=20 * count * pairs * PAIR,
        transcendentals=2 * count * count * pairs,
    )


def attend(qkv, segment):
    count = qkv.shape[0]
    pairs = qkv.shape[1] // (3 * PAIR)
    block = min(Q_BLOCK, count)
    seg_col, seg_row, query, key, value, lse = attention_specs(count, pairs, block)
    return pl.pallas_call(
        attend_kernel,
        grid=(pairs, count // block),
        in_specs=[seg_col, seg_row, query, key, value],
        out_specs=[query, lse],
        out_shape=[
            jax.ShapeDtypeStruct((count, pairs * PAIR), jnp.bfloat16),
            jax.ShapeDtypeStruct((pairs, 2, count), jnp.float32),
        ],
        scratch_shapes=[pltpu.VMEM((PAIR, count), jnp.bfloat16)],
        compiler_params=pltpu.CompilerParams(vmem_limit_bytes=32 << 20),
        cost_estimate=attention_cost(count, pairs, 64),
    )(segment.reshape(-1, 1), segment, qkv, qkv, qkv)


def attend_back(qkv, segment, lse_rows, d_context, turn, turns):
    count = qkv.shape[0]
    pairs = qkv.shape[1] // (3 * PAIR)
    here = pairs // turns
    block = min(Q_BLOCK, count)
    seg_col, seg_row, query, key, value, lse = attention_specs(count, pairs, block, turn * here)
    d_query = pl.BlockSpec((block, PAIR), lambda h, i: (i, h))
    d_whole = pl.BlockSpec((count, PAIR), lambda h, i: (0, h))
    shape = jax.ShapeDtypeStruct((count, here * PAIR), jnp.bfloat16)
    return pl.pallas_call(
        attend_back_kernel,
        grid=(here, count // block),
        in_specs=[seg_col, seg_row, query, key, value, lse, query],
        out_specs=[d_query, d_whole, d_whole],
        out_shape=[shape, shape, shape],
        scratch_shapes=[
            pltpu.VMEM((PAIR, count), jnp.bfloat16),
            pltpu.VMEM((count, PAIR), jnp.float32),
            pltpu.VMEM((count, PAIR), jnp.float32),
        ],
        compiler_params=pltpu.CompilerParams(vmem_limit_bytes=32 << 20),
        cost_estimate=attention_cost(count, here, 11),
    )(segment.reshape(-1, 1), segment, qkv, qkv, qkv, lse_rows, d_context)


def matmul(left, right):
    return jnp.dot(left, right, preferred_element_type=jnp.float32)


def matmul_tn(left, right):
    return lax.dot_general(
        left, right, (((0,), (0,)), ((), ())), preferred_element_type=jnp.float32
    )


def matmul_nt(left, right):
    return lax.dot_general(
        left, right, (((1,), (1,)), ((), ())), preferred_element_type=jnp.float32
    )


def column_sum(values):
    return jnp.sum(values.astype(jnp.float32), axis=0)


def swapped(part):
    return lax.ppermute(part, "col", [(0, 1), (1, 0)])


def swapped_rows(part):
    other = swapped(part)
    cut = other.shape[1] // 2
    return jnp.concatenate([other[:, cut:], other[:, :cut]], axis=1).astype(jnp.float32)


def partner(part, axis, bit):
    size = lax.axis_size(axis)
    return lax.ppermute(part, axis, [(i, i ^ bit) for i in range(size)])


def shifted(part, step):
    size = lax.axis_size("row")
    return lax.ppermute(part, "row", [(i, (i + step) % size) for i in range(size)])


def is_small_grid(rows):
    return lax.axis_size("row") == 4 and lax.axis_size("dp") == 4 and rows % 128 == 0


def place_kernel(idx, own, ring, near_x, near_y, far, *outs):
    quarter = ring.shape[0]
    begin = 0
    for out in outs:
        columns = slice(begin, begin + out.shape[1])
        begin = begin + out.shape[1]

        @pl.when(pl.program_id(0) == 0)
        def _():
            out[...] = own[:, columns]

        @pl.when(pl.program_id(0) > 0)
        def _():
            for corner, piece in enumerate((ring, near_x, near_y, far)):
                start = pl.multiple_of(idx[4 + corner] * quarter, quarter)
                out[pl.ds(start, quarter), :] = piece[:, columns]


def place(idx, own, pieces, widths):
    rows, width = own.shape
    fixed = pl.BlockSpec(own.shape, lambda s, idx: (0, 0))
    moving = pl.BlockSpec((rows // 4, width), lambda s, idx: (jnp.maximum(s - 1, 0), 0))
    return pl.pallas_call(
        place_kernel,
        grid_spec=pltpu.PrefetchScalarGridSpec(
            num_scalar_prefetch=1,
            grid=(4,),
            in_specs=[fixed, moving, moving, moving, moving],
            out_specs=[pl.BlockSpec((rows, w), lambda s, idx: (idx[s], 0)) for w in widths],
        ),
        out_shape=[jax.ShapeDtypeStruct((4 * rows, w), own.dtype) for w in widths],
        compiler_params=pltpu.CompilerParams(vmem_limit_bytes=40 << 20),
        cost_estimate=NO_COST,
    )(idx, own, *pieces)


def natural_order(whole):
    cut = whole.shape[0] // 2
    return jnp.where(
        lax.axis_index("col") == 0, whole, jnp.concatenate([whole[cut:], whole[:cut]], axis=0)
    )


def gathered(block):
    rows = block.shape[0] // lax.axis_size("dp")
    part = lax.dynamic_slice_in_dim(block, lax.axis_index("dp") * rows, rows, 0)
    return natural_order(lax.all_gather(part, ("row", "dp"), axis=0, tiled=True))


def sync_kernel(*refs):
    pass


def sync(arrays):
    arrays = list(arrays)
    return pl.pallas_call(
        sync_kernel,
        in_specs=[pl.BlockSpec(memory_space=pl.ANY)] * len(arrays),
        out_specs=[pl.BlockSpec(memory_space=pl.ANY)] * len(arrays),
        out_shape=[jax.ShapeDtypeStruct(part.shape, part.dtype) for part in arrays],
        input_output_aliases={i: i for i in range(len(arrays))},
        cost_estimate=NO_COST,
    )(*arrays)


def checkpoint(value, *movers):
    counts = [len(mover.got) for mover in movers]
    if sum(counts):
        value, *got = sync([value] + [part for mover in movers for part in mover.got])
        for mover, count in zip(movers, counts):
            mover.got, got = got[:count], got[count:]
    sends = [mover.sends() for mover in movers]
    if sum(len(some) for some in sends):
        value, *flat = sync([value] + [part for some in sends for part in some])
        for mover, some in zip(movers, sends):
            mover.go(flat[: len(some)])
            flat = flat[len(some) :]
    return value


class Gather:
    def __init__(self, group, by_shifts=False, far_too=False):
        self.group, self.by_shifts, self.far_too = group, by_shifts, far_too
        self.got = []
        self.step = 0
        self.direct = not all(is_small_grid(block.shape[0]) for block in group)
        if self.direct:
            return
        core, corner = lax.axis_index("col"), lax.axis_index("dp")
        self.level, self.size = lax.axis_index("row"), lax.axis_size("row")
        place_z = self.level + self.size // 2 * core + self.size - jnp.arange(self.size)
        self.idx = jnp.concatenate([place_z % self.size, corner ^ jnp.arange(4)]).astype(jnp.int32)
        self.own = jnp.concatenate(group, axis=1) if len(group) > 1 else group[0]
        self.quarter = self.own.shape[0] // 4
        self.parts = [
            lax.dynamic_slice_in_dim(self.own, at * self.quarter, self.quarter, 0)
            for at in ((corner, corner ^ 3) if far_too else (corner,))
        ]

    def stacked(self, count, which):
        pieces = []
        for step in (1, 2, 3):
            level = (self.level + self.size - step) % self.size
            begin = (level * count + which) * self.quarter
            pieces.append(lax.dynamic_slice_in_dim(self.got[0], begin, self.quarter, 0))
        return jnp.concatenate(pieces, axis=0)

    def sends(self):
        if self.direct:
            return []
        if self.step == 0:
            return [jnp.concatenate(self.parts, axis=0) if self.far_too else self.parts[0]]
        if self.by_shifts:
            return [jnp.concatenate(self.got, axis=0)]
        return [self.stacked(len(self.parts), which) for which in range(len(self.parts))]

    def go(self, sends):
        if self.direct:
            return
        if self.step == 0 and self.by_shifts:
            self.got = [shifted(sends[0], step) for step in (1, 2, 3)]
        elif self.step == 0:
            self.got = [lax.all_gather(sends[0], "row", axis=0, tiled=True)]
        else:
            bits = (1, 2) if self.far_too else (1, 2, 3)
            self.got = [partner(sends[0], "dp", bit) for bit in bits]
            self.mine = sends
        self.step = self.step + 1

    def result(self):
        if self.direct:
            return [gathered(block) for block in self.group]
        pieces = [self.mine[0], *self.got, *self.mine[1:]]
        return place(self.idx, self.own, pieces, [block.shape[1] for block in self.group])


def pick(values, axis, index):
    return lax.dynamic_index_in_dim(values, index, axis, keepdims=False)


def added(*parts):
    total = parts[0].astype(jnp.float32)
    for part in parts[1:]:
        total = total + part.astype(jnp.float32)
    return total.astype(jnp.bfloat16)


class Reduction:
    def __init__(self, first, second, in_halves):
        corner = lax.axis_index("dp")
        self.corner, self.a, self.b = corner, corner // 2, corner % 2
        self.direct = not is_small_grid(2 * first.shape[0] // lax.axis_size("row"))
        self.step = 0 if in_halves else 10
        self.got = []
        if self.direct:
            self.whole = jnp.concatenate([first, second], axis=0)
        else:
            width = first.shape[1]
            self.first = first.reshape(2, 2, 2, -1, width)
            self.second = second.reshape(2, 2, 2, -1, width)

    def sends(self):
        if self.direct:
            return []
        a, b = self.a, self.b
        if self.step == 0:
            return [pick(self.first, 2, 1 - b), pick(self.second, 1, 1 - a)]
        if self.step == 1:
            one, two = self.got
            self.keep = (
                pick(pick(self.first, 2, b), 1, a),
                pick(one, 1, a),
                pick(pick(self.second, 1, a), 1, b),
                pick(two, 1, b),
            )
            return [
                added(pick(pick(self.first, 2, b), 1, 1 - a), pick(one, 1, 1 - a)),
                added(pick(pick(self.second, 1, a), 1, 1 - b), pick(two, 1, 1 - b)),
            ]
        if self.step == 2:
            parts = [added(*self.keep[:2], self.got[0]), added(*self.keep[2:], self.got[1])]
            return [self.in_row_order(parts)]
        if self.step == 10:
            return [jnp.concatenate(self.quarter_of(bit), axis=0) for bit in (1, 2, 3)]
        if self.step == 11:
            parts = []
            for i, own in enumerate(self.quarter_of(0)):
                parts.append(added(own, *[got[2 * i : 2 * i + 2] for got in self.got]))
            return [self.in_row_order(parts)]
        return self.got

    def quarter_of(self, bit):
        a, b = (self.corner ^ bit) // 2, (self.corner ^ bit) % 2
        return [pick(pick(half, 2, b), 1, a) for half in (self.first, self.second)]

    def in_row_order(self, parts):
        levels = natural_order(jnp.concatenate(parts, axis=0))
        return levels.reshape(-1, levels.shape[-1])

    def go(self, sends):
        if self.direct:
            return
        if self.step == 0:
            self.got = [partner(sends[0], "dp", 1), partner(sends[1], "dp", 2)]
        elif self.step == 1:
            self.got = [partner(sends[0], "dp", 2), partner(sends[1], "dp", 1)]
        elif self.step == 10:
            self.got = [partner(part, "dp", bit) for part, bit in zip(sends, (1, 2, 3))]
        elif self.step in (2, 11):
            self.step = 2
            self.got = [lax.psum_scatter(sends[0], "row", scatter_dimension=0, tiled=True)]
        else:
            self.got = [sends[0]] + [partner(sends[0], "dp", bit) for bit in (1, 2, 3)]
        self.step = self.step + 1

    def result(self):
        if self.direct:
            whole = natural_order(self.whole)
            part = lax.psum_scatter(whole, ("row", "dp"), scatter_dimension=0, tiled=True)
            return lax.all_gather(part, "dp", axis=0, tiled=True).astype(jnp.float32)
        got = self.got
        return jnp.concatenate(
            [
                jnp.where(
                    self.a == 0,
                    jnp.where(self.b == 0, got[k], got[k ^ 1]),
                    jnp.where(self.b == 0, got[k ^ 2], got[k ^ 3]),
                )
                for k in range(4)
            ],
            axis=0,
        ).astype(jnp.float32)


class VectorSum:
    PARTNERS = (("dp", 1), ("dp", 2), ("row", 1), ("row", 2))

    def __init__(self, values):
        self.values = values.reshape(-1, 128)
        self.direct = not is_small_grid(128)
        self.got = []
        self.step = 0

    def sends(self):
        if self.direct:
            return []
        if self.got:
            self.values = self.values + self.got[0]
        return [self.values]

    def go(self, sends):
        if self.direct:
            return
        self.values = sends[0]
        self.got = [partner(sends[0], *self.PARTNERS[self.step])]
        self.step = self.step + 1

    def result(self):
        if self.direct:
            return lax.psum(self.values, ("row", "dp")).reshape(-1)
        while self.step < 4:
            self.go(self.sends())
        return (self.values + self.got[0]).reshape(-1)


def norm_forward(resid, gain, shift):
    center = jnp.mean(resid, axis=1, keepdims=True)
    inverse = lax.rsqrt(
        jnp.mean(resid * resid, axis=1, keepdims=True) - center * center + EPSILON
    )
    normed = (resid - center) * inverse
    return (normed * gain + shift, normed, inverse)


def norm_backward(grad, normed, inverse, gain):
    scaled = grad * gain
    first = jnp.mean(scaled, axis=1, keepdims=True)
    second = jnp.mean(scaled * normed, axis=1, keepdims=True)
    return inverse * (scaled - first - normed * second)


def body(
    tokens,
    segment,
    cotangent,
    w_query,
    b_query,
    w_key,
    w_value,
    b_value,
    w_out,
    b_out,
    w_up,
    b_up,
    w_down,
    b_down,
    gain_one,
    shift_one,
    gain_two,
    shift_two,
):
    half = w_query.shape[1]
    token_rows = jnp.concatenate([tokens, swapped(tokens)], axis=1)
    w_in = jnp.concatenate([w_query, w_key, w_value], axis=1)
    take_qkv = Gather([w_in], by_shifts=True)
    take_out_up = Gather([w_out, w_up])
    take_down = Gather([w_down], far_too=True)
    take_qkv.go(take_qkv.sends())
    token_rows = checkpoint(token_rows, take_qkv, take_out_up, take_down)
    (w_qkv,) = take_qkv.result()
    cotangent_rows = jnp.concatenate([cotangent, swapped(cotangent)], axis=1)
    own_vectors = jnp.stack([b_out, b_down, gain_one, shift_one, gain_two, shift_two])
    vectors = jnp.concatenate([own_vectors, swapped(own_vectors)], axis=1).astype(jnp.float32)
    bias_out, bias_down, gain1, shift1, gain2, shift2 = [vectors[i] for i in range(6)]
    b_qkv = jnp.concatenate([b_query, jnp.zeros_like(b_query), b_value]).astype(jnp.float32)
    qkv = (matmul(token_rows, w_qkv) + b_qkv).astype(jnp.bfloat16)
    qkv = checkpoint(qkv, take_out_up)
    context, lse_rows = attend(qkv, segment)
    context, *take_out_up.got = sync([context, *take_out_up.got])
    context_rows = jnp.concatenate([context, swapped(context)], axis=1)
    context_rows = checkpoint(context_rows, take_down)
    wo_half, wu = take_out_up.result()
    wo_other = swapped(wo_half)
    wo = jnp.concatenate(
        [wo_half, jnp.concatenate([wo_other[half:], wo_other[:half]], axis=0)], axis=1
    )
    first_sum = token_rows.astype(jnp.float32) + (matmul(context_rows, wo) + bias_out)
    hidden_f, normed_one, inverse_one = norm_forward(first_sum, gain1, shift1)
    hidden = hidden_f.astype(jnp.bfloat16)
    pre_act = matmul(hidden, wu) + b_up.astype(jnp.float32)
    cdf = 0.5 * (1.0 + lax.erf(pre_act * (0.5**0.5)))
    activated = (pre_act * cdf).astype(jnp.bfloat16)
    slope = cdf + pre_act * (jnp.exp(-0.5 * pre_act * pre_act) * 0.3989422804014327)
    (wd_half,) = take_down.result()
    units = w_up.shape[1]
    wd_own, wd_other = wd_half[:units], swapped(wd_half[units:])
    wd = jnp.concatenate([wd_own, wd_other], axis=1)
    part_other = matmul(activated, wd_other).astype(jnp.bfloat16)
    part_own = matmul(activated, wd_own).astype(jnp.bfloat16)
    ffn_out = jnp.concatenate(
        [
            part_own.astype(jnp.float32) + swapped(part_other).astype(jnp.float32),
            part_other.astype(jnp.float32) + swapped(part_own).astype(jnp.float32),
        ],
        axis=1,
    ) + bias_down
    second_sum = hidden.astype(jnp.float32) + ffn_out
    final, normed_two, inverse_two = norm_forward(second_sum, gain2, shift2)
    output = final[:, :half].astype(jnp.bfloat16)
    y = cotangent_rows.astype(jnp.float32)
    second_grad = norm_backward(y, normed_two, inverse_two, gain2)
    d_gain_two = jnp.sum(y * normed_two, axis=0)
    d_shift_two = jnp.sum(y, axis=0)
    ffn_grad = second_grad.astype(jnp.bfloat16)
    d_down_other = swapped(matmul_tn(activated, ffn_grad[:, half:]).astype(jnp.bfloat16))
    d_down_own = matmul_tn(activated, ffn_grad[:, :half]).astype(jnp.bfloat16)
    d_b_down = column_sum(ffn_grad)
    pre_grad = (matmul_nt(ffn_grad, wd) * slope).astype(jnp.bfloat16)
    d_b_up = column_sum(pre_grad)
    down = Reduction(d_down_own, d_down_other, in_halves=True)
    pre_grad = checkpoint(pre_grad, down)
    hidden_part = matmul_nt(pre_grad, wu).astype(jnp.bfloat16)
    hidden_other = swapped_rows(hidden_part)
    d_w_up = matmul_tn(hidden, pre_grad).astype(jnp.bfloat16)
    up = Reduction(d_w_up[:half], d_w_up[half:], in_halves=True)
    hidden_part = checkpoint(hidden_part, up)
    hidden_grad = second_grad + (hidden_part.astype(jnp.float32) + hidden_other)
    first_grad = norm_backward(hidden_grad, normed_one, inverse_one, gain1)
    d_gain_one = jnp.sum(hidden_grad * normed_one, axis=0)
    d_shift_one = jnp.sum(hidden_grad, axis=0)
    branch_grad = first_grad.astype(jnp.bfloat16)
    d_b_out = column_sum(branch_grad)
    wide = jnp.stack([d_b_out, d_b_down, d_gain_one, d_shift_one, d_gain_two, d_shift_two])
    context_grad = matmul_nt(branch_grad, wo[:half]).astype(jnp.bfloat16)
    d_w_out = matmul_tn(context_rows, branch_grad[:, :half]).astype(jnp.bfloat16)
    context_grad = checkpoint(context_grad, down)
    qkv_grad = jnp.concatenate(attend_back(qkv, segment, lse_rows, context_grad, 0, 1), axis=1)
    qkv_grad = checkpoint(qkv_grad, down, up)
    d_w_qkv = matmul_tn(token_rows, qkv_grad).astype(jnp.bfloat16)
    d_b_qkv = column_sum(qkv_grad)
    d_last = jnp.concatenate([d_w_out, d_w_qkv], axis=1)
    last = Reduction(d_last[:half], d_last[half:], in_halves=False)
    vector = VectorSum(
        jnp.concatenate(
            [wide[:, :half].reshape(-1), d_b_qkv[:half], d_b_qkv[2 * half :], d_b_up]
        )
    )
    token = checkpoint(d_b_qkv[:128].reshape(1, 128), last, vector)
    token_part = matmul_nt(qkv_grad, w_qkv).astype(jnp.bfloat16)
    token_other = swapped(token_part[:, half:])
    token_sum = token_part[:, :half].astype(jnp.float32) + token_other.astype(jnp.float32)
    d_tokens = (token_sum + first_grad[:, :half]).astype(jnp.bfloat16)
    ahead = len(last.got[:2])
    token, *got = sync([token, *last.got[:ahead], *up.got])
    last.got[:ahead], up.got = got[:ahead], got[ahead:]
    token = checkpoint(token, up, vector)
    token = checkpoint(token, last, down, vector)
    token = checkpoint(token, up, vector)
    token = checkpoint(token, last)
    o_w_down, o_w_up, o_last = down.result(), up.result(), last.result()
    sums = vector.result()
    pieces = [sums[i * half : (i + 1) * half] for i in range(8)]
    return (
        output,
        d_tokens,
        o_last[:, half : 2 * half],
        pieces[6],
        o_last[:, 2 * half : 3 * half],
        o_last[:, 3 * half :],
        pieces[7],
        o_last[:, :half],
        pieces[0],
        o_w_up,
        sums[8 * half :],
        o_w_down,
        pieces[1],
        pieces[2],
        pieces[3],
        pieces[4],
        pieces[5],
    )


def solution(mesh):
    in_specs = (
        P(("dp", "row"), "col"),
        P(("dp", "row"), None),
        P(("dp", "row"), "col"),
        P("row", "col"),
        P("col"),
        P("row", "col"),
        P("row", "col"),
        P("col"),
        P("row", "col"),
        P("col"),
        P("row", "col"),
        P("col"),
        P("row", "col"),
        P("col"),
        P("col"),
        P("col"),
        P("col"),
        P("col"),
    )
    out_specs = (
        P(("dp", "row"), "col"),
        P(("dp", "row"), "col"),
        P("row", "col"),
        P("col"),
        P("row", "col"),
        P("row", "col"),
        P("col"),
        P("row", "col"),
        P("col"),
        P("row", "col"),
        P("col"),
        P("row", "col"),
        P("col"),
        P("col"),
        P("col"),
        P("col"),
        P("col"),
    )
    return jax.shard_map(body, mesh=mesh, in_specs=in_specs, out_specs=out_specs, check_vma=False)
```

```python
import jax
import jax.numpy as jnp
from jax import lax
from jax.experimental import pallas as pl
from jax.experimental.pallas import tpu as pltpu
from jax.sharding import PartitionSpec as P

HEAD_DIM = 64


EPSILON = 1e-05
SCALE = 0.125
LOG2E = 1.4426950408889634
PAIR = 2 * HEAD_DIM
Q_BLOCK = 256
NO_COST = pl.CostEstimate(flops=0, bytes_accessed=0, transcendentals=0)


def dot_nt(left, right):
    return lax.dot_general(
        left, right, (((1,), (1,)), ((), ())), preferred_element_type=jnp.float32
    )


def dot_nn(left, right):
    return lax.dot_general(
        left, right, (((1,), (0,)), ((), ())), preferred_element_type=jnp.float32
    )


def only_head(block, head):
    lane = lax.broadcasted_iota(jnp.int32, block.shape, 1)
    return jnp.where(lane // HEAD_DIM == head, block, jnp.zeros_like(block))


def attend_kernel(seg_col, seg_row, q_ref, k_ref, v_ref, ctx_ref, lse_ref, vt_ref):
    @pl.when(pl.program_id(1) == 0)
    def _():
        vt_ref[...] = v_ref[...].T

    same = seg_col[...] == seg_row[...]
    parts = []
    for head in range(2):
        scores = dot_nt(k_ref[...], only_head(q_ref[...], head)) * (SCALE * LOG2E)
        scores = jnp.where(same, scores, -1e30)
        top = jnp.max(scores, axis=0, keepdims=True)
        expo = jnp.exp2(scores - top)
        total = jnp.sum(expo, axis=0, keepdims=True)
        out = dot_nn(
            vt_ref[head * HEAD_DIM : (head + 1) * HEAD_DIM, :], expo.astype(jnp.bfloat16)
        )
        parts.append(out / total)
        lse_ref[0, head : head + 1, :] = top + jnp.log2(total)
    ctx_ref[...] = jnp.concatenate(parts, axis=0).T.astype(jnp.bfloat16)


def attend_back_kernel(
    seg_col, seg_row, q_ref, k_ref, v_ref, lse_ref, do_ref, dq_ref, dk_ref, dv_ref, kt_ref, dk_acc, dv_acc
):
    step = pl.program_id(1)

    @pl.when(step == 0)
    def _():
        kt_ref[...] = k_ref[...].T
        dk_acc[...] = jnp.zeros_like(dk_acc)
        dv_acc[...] = jnp.zeros_like(dv_acc)

    same = seg_col[...] == seg_row[...]
    parts = []
    for head in range(2):
        query = only_head(q_ref[...], head)
        grad = only_head(do_ref[...], head)
        scores = dot_nt(k_ref[...], query) * (SCALE * LOG2E)
        probs = jnp.where(same, jnp.exp2(scores - lse_ref[0, head : head + 1, :]), 0.0)
        d_probs = dot_nt(v_ref[...], grad)
        inner = jnp.sum(probs * d_probs, axis=0, keepdims=True)
        d_scores = (probs * (d_probs - inner)).astype(jnp.bfloat16)
        dv_acc[...] += dot_nn(probs.astype(jnp.bfloat16), grad)
        dk_acc[...] += dot_nn(d_scores, query)
        parts.append(
            dot_nn(kt_ref[head * HEAD_DIM : (head + 1) * HEAD_DIM, :], d_scores)
        )
    dq_ref[...] = (jnp.concatenate(parts, axis=0) * SCALE).T.astype(jnp.bfloat16)

    @pl.when(step == pl.num_programs(1) - 1)
    def _():
        dk_ref[...] = (dk_acc[...] * SCALE).astype(jnp.bfloat16)
        dv_ref[...] = dv_acc[...].astype(jnp.bfloat16)


def attention_specs(count, pairs, block, skip=0):
    seg_col = pl.BlockSpec((count, 1), lambda h, i: (0, 0))
    seg_row = pl.BlockSpec((1, block), lambda h, i: (0, i))
    query = pl.BlockSpec((block, PAIR), lambda h, i: (i, skip + h))
    key = pl.BlockSpec((count, PAIR), lambda h, i: (0, pairs + skip + h))
    value = pl.BlockSpec((count, PAIR), lambda h, i: (0, 2 * pairs + skip + h))
    lse = pl.BlockSpec((1, 2, block), lambda h, i: (skip + h, 0, i))
    return seg_col, seg_row, query, key, value, lse


def attention_cost(count, pairs, products):
    return pl.CostEstimate(
        flops=products * count * count * PAIR * pairs,
        bytes_accessed=20 * count * pairs * PAIR,
        transcendentals=2 * count * count * pairs,
    )


def attend(qkv, segment):
    count = qkv.shape[0]
    pairs = qkv.shape[1] // (3 * PAIR)
    block = min(Q_BLOCK, count)
    seg_col, seg_row, query, key, value, lse = attention_specs(count, pairs, block)
    return pl.pallas_call(
        attend_kernel,
        grid=(pairs, count // block),
        in_specs=[seg_col, seg_row, query, key, value],
        out_specs=[query, lse],
        out_shape=[
            jax.ShapeDtypeStruct((count, pairs * PAIR), jnp.bfloat16),
            jax.ShapeDtypeStruct((pairs, 2, count), jnp.float32),
        ],
        scratch_shapes=[pltpu.VMEM((PAIR, count), jnp.bfloat16)],
        compiler_params=pltpu.CompilerParams(vmem_limit_bytes=32 << 20),
        cost_estimate=attention_cost(count, pairs, 64),
    )(segment.reshape(-1, 1), segment, qkv, qkv, qkv)


def attend_back(qkv, segment, lse_rows, d_context, turn, turns):
    count = qkv.shape[0]
    pairs = qkv.shape[1] // (3 * PAIR)
    here = pairs // turns
    block = min(Q_BLOCK, count)
    seg_col, seg_row, query, key, value, lse = attention_specs(count, pairs, block, turn * here)
    d_query = pl.BlockSpec((block, PAIR), lambda h, i: (i, h))
    d_whole = pl.BlockSpec((count, PAIR), lambda h, i: (0, h))
    shape = jax.ShapeDtypeStruct((count, here * PAIR), jnp.bfloat16)
    return pl.pallas_call(
        attend_back_kernel,
        grid=(here, count // block),
        in_specs=[seg_col, seg_row, query, key, value, lse, query],
        out_specs=[d_query, d_whole, d_whole],
        out_shape=[shape, shape, shape],
        scratch_shapes=[
            pltpu.VMEM((PAIR, count), jnp.bfloat16),
            pltpu.VMEM((count, PAIR), jnp.float32),
            pltpu.VMEM((count, PAIR), jnp.float32),
        ],
        compiler_params=pltpu.CompilerParams(vmem_limit_bytes=32 << 20),
        cost_estimate=attention_cost(count, here, 11),
    )(segment.reshape(-1, 1), segment, qkv, qkv, qkv, lse_rows, d_context)


def matmul(left, right):
    return jnp.dot(left, right, preferred_element_type=jnp.float32)


def matmul_tn(left, right):
    return lax.dot_general(
        left, right, (((0,), (0,)), ((), ())), preferred_element_type=jnp.float32
    )


def matmul_nt(left, right):
    return lax.dot_general(
        left, right, (((1,), (1,)), ((), ())), preferred_element_type=jnp.float32
    )


def column_sum(values):
    return jnp.sum(values.astype(jnp.float32), axis=0)


def swapped(part):
    return lax.ppermute(part, "col", [(0, 1), (1, 0)])


def swapped_rows(part):
    other = swapped(part)
    cut = other.shape[1] // 2
    return jnp.concatenate([other[:, cut:], other[:, :cut]], axis=1).astype(jnp.float32)


def partner(part, axis, bit):
    size = lax.axis_size(axis)
    return lax.ppermute(part, axis, [(i, i ^ bit) for i in range(size)])


def shifted(part, step):
    size = lax.axis_size("row")
    return lax.ppermute(part, "row", [(i, (i + step) % size) for i in range(size)])


def is_small_grid(rows):
    return lax.axis_size("row") == 4 and lax.axis_size("dp") == 4 and rows % 128 == 0


def place_kernel(idx, own, ring, near_x, near_y, far, *outs):
    quarter = ring.shape[0]
    begin = 0
    for out in outs:
        columns = slice(begin, begin + out.shape[1])
        begin = begin + out.shape[1]

        @pl.when(pl.program_id(0) == 0)
        def _():
            out[...] = own[:, columns]

        @pl.when(pl.program_id(0) > 0)
        def _():
            for corner, piece in enumerate((ring, near_x, near_y, far)):
                start = pl.multiple_of(idx[4 + corner] * quarter, quarter)
                out[pl.ds(start, quarter), :] = piece[:, columns]


def place(idx, own, pieces, widths):
    rows, width = own.shape
    fixed = pl.BlockSpec(own.shape, lambda s, idx: (0, 0))
    moving = pl.BlockSpec((rows // 4, width), lambda s, idx: (jnp.maximum(s - 1, 0), 0))
    return pl.pallas_call(
        place_kernel,
        grid_spec=pltpu.PrefetchScalarGridSpec(
            num_scalar_prefetch=1,
            grid=(4,),
            in_specs=[fixed, moving, moving, moving, moving],
            out_specs=[pl.BlockSpec((rows, w), lambda s, idx: (idx[s], 0)) for w in widths],
        ),
        out_shape=[jax.ShapeDtypeStruct((4 * rows, w), own.dtype) for w in widths],
        compiler_params=pltpu.CompilerParams(vmem_limit_bytes=40 << 20),
        cost_estimate=NO_COST,
    )(idx, own, *pieces)


def natural_order(whole):
    cut = whole.shape[0] // 2
    return jnp.where(
        lax.axis_index("col") == 0, whole, jnp.concatenate([whole[cut:], whole[:cut]], axis=0)
    )


def gathered(block):
    rows = block.shape[0] // lax.axis_size("dp")
    part = lax.dynamic_slice_in_dim(block, lax.axis_index("dp") * rows, rows, 0)
    return natural_order(lax.all_gather(part, ("row", "dp"), axis=0, tiled=True))


def sync_kernel(*refs):
    pass


def sync(arrays):
    arrays = list(arrays)
    return pl.pallas_call(
        sync_kernel,
        in_specs=[pl.BlockSpec(memory_space=pl.ANY)] * len(arrays),
        out_specs=[pl.BlockSpec(memory_space=pl.ANY)] * len(arrays),
        out_shape=[jax.ShapeDtypeStruct(part.shape, part.dtype) for part in arrays],
        input_output_aliases={i: i for i in range(len(arrays))},
        cost_estimate=NO_COST,
    )(*arrays)


def checkpoint(value, *movers):
    counts = [len(mover.got) for mover in movers]
    if sum(counts):
        value, *got = sync([value] + [part for mover in movers for part in mover.got])
        for mover, count in zip(movers, counts):
            mover.got, got = got[:count], got[count:]
    sends = [mover.sends() for mover in movers]
    if sum(len(some) for some in sends):
        value, *flat = sync([value] + [part for some in sends for part in some])
        for mover, some in zip(movers, sends):
            mover.go(flat[: len(some)])
            flat = flat[len(some) :]
    return value


class Gather:
    def __init__(self, group, by_shifts=False, far_too=False):
        self.group, self.by_shifts, self.far_too = group, by_shifts, far_too
        self.got = []
        self.step = 0
        self.direct = not all(is_small_grid(block.shape[0]) for block in group)
        if self.direct:
            return
        core, corner = lax.axis_index("col"), lax.axis_index("dp")
        self.level, self.size = lax.axis_index("row"), lax.axis_size("row")
        place_z = self.level + self.size // 2 * core + self.size - jnp.arange(self.size)
        self.idx = jnp.concatenate([place_z % self.size, corner ^ jnp.arange(4)]).astype(jnp.int32)
        self.own = jnp.concatenate(group, axis=1) if len(group) > 1 else group[0]
        self.quarter = self.own.shape[0] // 4
        self.parts = [
            lax.dynamic_slice_in_dim(self.own, at * self.quarter, self.quarter, 0)
            for at in ((corner, corner ^ 3) if far_too else (corner,))
        ]

    def stacked(self, count, which):
        pieces = []
        for step in (1, 2, 3):
            level = (self.level + self.size - step) % self.size
            begin = (level * count + which) * self.quarter
            pieces.append(lax.dynamic_slice_in_dim(self.got[0], begin, self.quarter, 0))
        return jnp.concatenate(pieces, axis=0)

    def sends(self):
        if self.direct:
            return []
        if self.step == 0:
            return [jnp.concatenate(self.parts, axis=0) if self.far_too else self.parts[0]]
        if self.by_shifts:
            return [jnp.concatenate(self.got, axis=0)]
        return [self.stacked(len(self.parts), which) for which in range(len(self.parts))]

    def go(self, sends):
        if self.direct:
            return
        if self.step == 0 and self.by_shifts:
            self.got = [shifted(sends[0], step) for step in (1, 2, 3)]
        elif self.step == 0:
            self.got = [lax.all_gather(sends[0], "row", axis=0, tiled=True)]
        else:
            bits = (1, 2) if self.far_too else (1, 2, 3)
            self.got = [partner(sends[0], "dp", bit) for bit in bits]
            self.mine = sends
        self.step = self.step + 1

    def result(self):
        if self.direct:
            return [gathered(block) for block in self.group]
        pieces = [self.mine[0], *self.got, *self.mine[1:]]
        return place(self.idx, self.own, pieces, [block.shape[1] for block in self.group])


def pick(values, axis, index):
    return lax.dynamic_index_in_dim(values, index, axis, keepdims=False)


def added(*parts):
    total = parts[0].astype(jnp.float32)
    for part in parts[1:]:
        total = total + part.astype(jnp.float32)
    return total.astype(jnp.bfloat16)


class Reduction:
    def __init__(self, first, second, in_halves):
        corner = lax.axis_index("dp")
        self.corner, self.a, self.b = corner, corner // 2, corner % 2
        self.direct = not is_small_grid(2 * first.shape[0] // lax.axis_size("row"))
        self.step = 0 if in_halves else 10
        self.got = []
        if self.direct:
            self.whole = jnp.concatenate([first, second], axis=0)
        else:
            width = first.shape[1]
            self.first = first.reshape(2, 2, 2, -1, width)
            self.second = second.reshape(2, 2, 2, -1, width)

    def sends(self):
        if self.direct:
            return []
        a, b = self.a, self.b
        if self.step == 0:
            return [pick(self.first, 2, 1 - b), pick(self.second, 1, 1 - a)]
        if self.step == 1:
            one, two = self.got
            self.keep = (
                pick(pick(self.first, 2, b), 1, a),
                pick(one, 1, a),
                pick(pick(self.second, 1, a), 1, b),
                pick(two, 1, b),
            )
            return [
                added(pick(pick(self.first, 2, b), 1, 1 - a), pick(one, 1, 1 - a)),
                added(pick(pick(self.second, 1, a), 1, 1 - b), pick(two, 1, 1 - b)),
            ]
        if self.step == 2:
            parts = [added(*self.keep[:2], self.got[0]), added(*self.keep[2:], self.got[1])]
            return [self.in_row_order(parts)]
        if self.step == 10:
            return [jnp.concatenate(self.quarter_of(bit), axis=0) for bit in (1, 2, 3)]
        if self.step == 11:
            parts = []
            for i, own in enumerate(self.quarter_of(0)):
                parts.append(added(own, *[got[2 * i : 2 * i + 2] for got in self.got]))
            return [self.in_row_order(parts)]
        return self.got

    def quarter_of(self, bit):
        a, b = (self.corner ^ bit) // 2, (self.corner ^ bit) % 2
        return [pick(pick(half, 2, b), 1, a) for half in (self.first, self.second)]

    def in_row_order(self, parts):
        levels = natural_order(jnp.concatenate(parts, axis=0))
        return levels.reshape(-1, levels.shape[-1])

    def go(self, sends):
        if self.direct:
            return
        if self.step == 0:
            self.got = [partner(sends[0], "dp", 1), partner(sends[1], "dp", 2)]
        elif self.step == 1:
            self.got = [partner(sends[0], "dp", 2), partner(sends[1], "dp", 1)]
        elif self.step == 10:
            self.got = [partner(part, "dp", bit) for part, bit in zip(sends, (1, 2, 3))]
        elif self.step in (2, 11):
            self.step = 2
            self.got = [lax.psum_scatter(sends[0], "row", scatter_dimension=0, tiled=True)]
        else:
            self.got = [sends[0]] + [partner(sends[0], "dp", bit) for bit in (1, 2, 3)]
        self.step = self.step + 1

    def result(self):
        if self.direct:
            whole = natural_order(self.whole)
            part = lax.psum_scatter(whole, ("row", "dp"), scatter_dimension=0, tiled=True)
            return lax.all_gather(part, "dp", axis=0, tiled=True).astype(jnp.float32)
        got = self.got
        return jnp.concatenate(
            [
                jnp.where(
                    self.a == 0,
                    jnp.where(self.b == 0, got[k], got[k ^ 1]),
                    jnp.where(self.b == 0, got[k ^ 2], got[k ^ 3]),
                )
                for k in range(4)
            ],
            axis=0,
        ).astype(jnp.float32)


class VectorSum:
    PARTNERS = (("dp", 1), ("dp", 2), ("row", 1), ("row", 2))

    def __init__(self, values):
        self.values = values.reshape(-1, 128)
        self.direct = not is_small_grid(128)
        self.got = []
        self.step = 0

    def sends(self):
        if self.direct:
            return []
        if self.got:
            self.values = self.values + self.got[0]
        return [self.values]

    def go(self, sends):
        if self.direct:
            return
        self.values = sends[0]
        self.got = [partner(sends[0], *self.PARTNERS[self.step])]
        self.step = self.step + 1

    def result(self):
        if self.direct:
            return lax.psum(self.values, ("row", "dp")).reshape(-1)
        while self.step < 4:
            self.go(self.sends())
        return (self.values + self.got[0]).reshape(-1)


def norm_forward(resid, gain, shift):
    center = jnp.mean(resid, axis=1, keepdims=True)
    inverse = lax.rsqrt(
        jnp.mean(resid * resid, axis=1, keepdims=True) - center * center + EPSILON
    )
    normed = (resid - center) * inverse
    return (normed * gain + shift, normed, inverse)


def norm_backward(grad, normed, inverse, gain):
    scaled = grad * gain
    first = jnp.mean(scaled, axis=1, keepdims=True)
    second = jnp.mean(scaled * normed, axis=1, keepdims=True)
    return inverse * (scaled - first - normed * second)


def body(
    tokens,
    segment,
    cotangent,
    w_query,
    b_query,
    w_key,
    w_value,
    b_value,
    w_out,
    b_out,
    w_up,
    b_up,
    w_down,
    b_down,
    gain_one,
    shift_one,
    gain_two,
    shift_two,
):
    half = w_query.shape[1]
    token_rows = jnp.concatenate([tokens, swapped(tokens)], axis=1)
    w_in = jnp.concatenate([w_query, w_key, w_value], axis=1)
    take_qkv = Gather([w_in], by_shifts=True)
    take_out_up = Gather([w_out, w_up])
    take_down = Gather([w_down], far_too=True)
    take_qkv.go(take_qkv.sends())
    token_rows = checkpoint(token_rows, take_qkv, take_out_up, take_down)
    (w_qkv,) = take_qkv.result()
    cotangent_rows = jnp.concatenate([cotangent, swapped(cotangent)], axis=1)
    own_vectors = jnp.stack([b_out, b_down, gain_one, shift_one, gain_two, shift_two])
    vectors = jnp.concatenate([own_vectors, swapped(own_vectors)], axis=1).astype(jnp.float32)
    bias_out, bias_down, gain1, shift1, gain2, shift2 = [vectors[i] for i in range(6)]
    b_qkv = jnp.concatenate([b_query, jnp.zeros_like(b_query), b_value]).astype(jnp.float32)
    qkv = (matmul(token_rows, w_qkv) + b_qkv).astype(jnp.bfloat16)
    qkv = checkpoint(qkv, take_out_up)
    context, lse_rows = attend(qkv, segment)
    context, *take_out_up.got = sync([context, *take_out_up.got])
    context = checkpoint(context, take_down)
    context_rows = jnp.concatenate([context, swapped(context)], axis=1)
    wo_half, wu = take_out_up.result()
    wo_other = swapped(wo_half)
    wo = jnp.concatenate(
        [wo_half, jnp.concatenate([wo_other[half:], wo_other[:half]], axis=0)], axis=1
    )
    first_sum = token_rows.astype(jnp.float32) + (matmul(context_rows, wo) + bias_out)
    hidden_f, normed_one, inverse_one = norm_forward(first_sum, gain1, shift1)
    hidden = hidden_f.astype(jnp.bfloat16)
    hidden, *take_down.got = sync([hidden, *take_down.got])
    pre_act = matmul(hidden, wu) + b_up.astype(jnp.float32)
    cdf = 0.5 * (1.0 + lax.erf(pre_act * (0.5**0.5)))
    activated = (pre_act * cdf).astype(jnp.bfloat16)
    slope = cdf + pre_act * (jnp.exp(-0.5 * pre_act * pre_act) * 0.3989422804014327)
    (wd_half,) = take_down.result()
    units = w_up.shape[1]
    wd_own, wd_other = wd_half[:units], swapped(wd_half[units:])
    wd = jnp.concatenate([wd_own, wd_other], axis=1)
    part_other = matmul(activated, wd_other).astype(jnp.bfloat16)
    part_own = matmul(activated, wd_own).astype(jnp.bfloat16)
    ffn_out = jnp.concatenate(
        [
            part_own.astype(jnp.float32) + swapped(part_other).astype(jnp.float32),
            part_other.astype(jnp.float32) + swapped(part_own).astype(jnp.float32),
        ],
        axis=1,
    ) + bias_down
    second_sum = hidden.astype(jnp.float32) + ffn_out
    final, normed_two, inverse_two = norm_forward(second_sum, gain2, shift2)
    output = final[:, :half].astype(jnp.bfloat16)
    y = cotangent_rows.astype(jnp.float32)
    second_grad = norm_backward(y, normed_two, inverse_two, gain2)
    d_gain_two = jnp.sum(y * normed_two, axis=0)
    d_shift_two = jnp.sum(y, axis=0)
    ffn_grad = second_grad.astype(jnp.bfloat16)
    d_down_other = swapped(matmul_tn(activated, ffn_grad[:, half:]).astype(jnp.bfloat16))
    d_down_own = matmul_tn(activated, ffn_grad[:, :half]).astype(jnp.bfloat16)
    d_b_down = column_sum(ffn_grad)
    pre_grad = (matmul_nt(ffn_grad, wd) * slope).astype(jnp.bfloat16)
    d_b_up = column_sum(pre_grad)
    down = Reduction(d_down_own, d_down_other, in_halves=True)
    pre_grad = checkpoint(pre_grad, down)
    hidden_part = matmul_nt(pre_grad, wu).astype(jnp.bfloat16)
    hidden_other = swapped_rows(hidden_part)
    d_w_up = matmul_tn(hidden, pre_grad).astype(jnp.bfloat16)
    up = Reduction(d_w_up[:half], d_w_up[half:], in_halves=True)
    hidden_part = checkpoint(hidden_part, up)
    hidden_grad = second_grad + (hidden_part.astype(jnp.float32) + hidden_other)
    first_grad = norm_backward(hidden_grad, normed_one, inverse_one, gain1)
    d_gain_one = jnp.sum(hidden_grad * normed_one, axis=0)
    d_shift_one = jnp.sum(hidden_grad, axis=0)
    branch_grad = first_grad.astype(jnp.bfloat16)
    d_b_out = column_sum(branch_grad)
    wide = jnp.stack([d_b_out, d_b_down, d_gain_one, d_shift_one, d_gain_two, d_shift_two])
    context_grad = matmul_nt(branch_grad, wo[:half]).astype(jnp.bfloat16)
    d_w_out = matmul_tn(context_rows, branch_grad[:, :half]).astype(jnp.bfloat16)
    context_grad = checkpoint(context_grad, down)
    qkv_grad = jnp.concatenate(attend_back(qkv, segment, lse_rows, context_grad, 0, 1), axis=1)
    qkv_grad = checkpoint(qkv_grad, down, up)
    d_w_qkv = matmul_tn(token_rows, qkv_grad).astype(jnp.bfloat16)
    d_b_qkv = column_sum(qkv_grad)
    d_last = jnp.concatenate([d_w_out, d_w_qkv], axis=1)
    last = Reduction(d_last[:half], d_last[half:], in_halves=False)
    vector = VectorSum(
        jnp.concatenate(
            [wide[:, :half].reshape(-1), d_b_qkv[:half], d_b_qkv[2 * half :], d_b_up]
        )
    )
    token = checkpoint(d_b_qkv[:128].reshape(1, 128), last, up, vector)
    token, qkv_grad = sync([token, qkv_grad])
    token = checkpoint(token, last, down, up, vector)
    token_part = matmul_nt(qkv_grad, w_qkv).astype(jnp.bfloat16)
    token_other = swapped(token_part[:, half:])
    token_sum = token_part[:, :half].astype(jnp.float32) + token_other.astype(jnp.float32)
    d_tokens = (token_sum + first_grad[:, :half]).astype(jnp.bfloat16)
    token = checkpoint(token, last, vector)
    o_w_down, o_w_up, o_last = down.result(), up.result(), last.result()
    sums = vector.result()
    pieces = [sums[i * half : (i + 1) * half] for i in range(8)]
    return (
        output,
        d_tokens,
        o_last[:, half : 2 * half],
        pieces[6],
        o_last[:, 2 * half : 3 * half],
        o_last[:, 3 * half :],
        pieces[7],
        o_last[:, :half],
        pieces[0],
        o_w_up,
        sums[8 * half :],
        o_w_down,
        pieces[1],
        pieces[2],
        pieces[3],
        pieces[4],
        pieces[5],
    )


def solution(mesh):
    in_specs = (
        P(("dp", "row"), "col"),
        P(("dp", "row"), None),
        P(("dp", "row"), "col"),
        P("row", "col"),
        P("col"),
        P("row", "col"),
        P("row", "col"),
        P("col"),
        P("row", "col"),
        P("col"),
        P("row", "col"),
        P("col"),
        P("row", "col"),
        P("col"),
        P("col"),
        P("col"),
        P("col"),
        P("col"),
    )
    out_specs = (
        P(("dp", "row"), "col"),
        P(("dp", "row"), "col"),
        P("row", "col"),
        P("col"),
        P("row", "col"),
        P("row", "col"),
        P("col"),
        P("row", "col"),
        P("col"),
        P("row", "col"),
        P("col"),
        P("row", "col"),
        P("col"),
        P("col"),
        P("col"),
        P("col"),
        P("col"),
    )
    return jax.shard_map(body, mesh=mesh, in_specs=in_specs, out_specs=out_specs, check_vma=False)
```

```python
import jax
import jax.numpy as jnp
from jax import lax
from jax.experimental import pallas as pl
from jax.experimental.pallas import tpu as pltpu
from jax.sharding import PartitionSpec as P

HEAD_DIM = 64


EPSILON = 1e-05
SCALE = 0.125
LOG2E = 1.4426950408889634
PAIR = 2 * HEAD_DIM
Q_BLOCK = 256
NO_COST = pl.CostEstimate(flops=0, bytes_accessed=0, transcendentals=0)


def dot_nt(left, right):
    return lax.dot_general(
        left, right, (((1,), (1,)), ((), ())), preferred_element_type=jnp.float32
    )


def dot_nn(left, right):
    return lax.dot_general(
        left, right, (((1,), (0,)), ((), ())), preferred_element_type=jnp.float32
    )


def only_head(block, head):
    lane = lax.broadcasted_iota(jnp.int32, block.shape, 1)
    return jnp.where(lane // HEAD_DIM == head, block, jnp.zeros_like(block))


def attend_kernel(seg_col, seg_row, q_ref, k_ref, v_ref, ctx_ref, lse_ref, vt_ref):
    @pl.when(pl.program_id(1) == 0)
    def _():
        vt_ref[...] = v_ref[...].T

    same = seg_col[...] == seg_row[...]
    parts = []
    for head in range(2):
        scores = dot_nt(k_ref[...], only_head(q_ref[...], head)) * (SCALE * LOG2E)
        scores = jnp.where(same, scores, -1e30)
        top = jnp.max(scores, axis=0, keepdims=True)
        expo = jnp.exp2(scores - top)
        total = jnp.sum(expo, axis=0, keepdims=True)
        out = dot_nn(
            vt_ref[head * HEAD_DIM : (head + 1) * HEAD_DIM, :], expo.astype(jnp.bfloat16)
        )
        parts.append(out / total)
        lse_ref[0, head : head + 1, :] = top + jnp.log2(total)
    ctx_ref[...] = jnp.concatenate(parts, axis=0).T.astype(jnp.bfloat16)


def attend_back_kernel(
    seg_col, seg_row, q_ref, k_ref, v_ref, lse_ref, do_ref, dq_ref, dk_ref, dv_ref, kt_ref, dk_acc, dv_acc
):
    step = pl.program_id(1)

    @pl.when(step == 0)
    def _():
        kt_ref[...] = k_ref[...].T
        dk_acc[...] = jnp.zeros_like(dk_acc)
        dv_acc[...] = jnp.zeros_like(dv_acc)

    same = seg_col[...] == seg_row[...]
    parts = []
    for head in range(2):
        query = only_head(q_ref[...], head)
        grad = only_head(do_ref[...], head)
        scores = dot_nt(k_ref[...], query) * (SCALE * LOG2E)
        probs = jnp.where(same, jnp.exp2(scores - lse_ref[0, head : head + 1, :]), 0.0)
        d_probs = dot_nt(v_ref[...], grad)
        inner = jnp.sum(probs * d_probs, axis=0, keepdims=True)
        d_scores = (probs * (d_probs - inner)).astype(jnp.bfloat16)
        dv_acc[...] += dot_nn(probs.astype(jnp.bfloat16), grad)
        dk_acc[...] += dot_nn(d_scores, query)
        parts.append(
            dot_nn(kt_ref[head * HEAD_DIM : (head + 1) * HEAD_DIM, :], d_scores)
        )
    dq_ref[...] = (jnp.concatenate(parts, axis=0) * SCALE).T.astype(jnp.bfloat16)

    @pl.when(step == pl.num_programs(1) - 1)
    def _():
        dk_ref[...] = (dk_acc[...] * SCALE).astype(jnp.bfloat16)
        dv_ref[...] = dv_acc[...].astype(jnp.bfloat16)


def attention_specs(count, pairs, block, skip=0):
    seg_col = pl.BlockSpec((count, 1), lambda h, i: (0, 0))
    seg_row = pl.BlockSpec((1, block), lambda h, i: (0, i))
    query = pl.BlockSpec((block, PAIR), lambda h, i: (i, skip + h))
    key = pl.BlockSpec((count, PAIR), lambda h, i: (0, pairs + skip + h))
    value = pl.BlockSpec((count, PAIR), lambda h, i: (0, 2 * pairs + skip + h))
    lse = pl.BlockSpec((1, 2, block), lambda h, i: (skip + h, 0, i))
    return seg_col, seg_row, query, key, value, lse


def attention_cost(count, pairs, products):
    return pl.CostEstimate(
        flops=products * count * count * PAIR * pairs,
        bytes_accessed=20 * count * pairs * PAIR,
        transcendentals=2 * count * count * pairs,
    )


def attend(qkv, segment):
    count = qkv.shape[0]
    pairs = qkv.shape[1] // (3 * PAIR)
    block = min(Q_BLOCK, count)
    seg_col, seg_row, query, key, value, lse = attention_specs(count, pairs, block)
    return pl.pallas_call(
        attend_kernel,
        grid=(pairs, count // block),
        in_specs=[seg_col, seg_row, query, key, value],
        out_specs=[query, lse],
        out_shape=[
            jax.ShapeDtypeStruct((count, pairs * PAIR), jnp.bfloat16),
            jax.ShapeDtypeStruct((pairs, 2, count), jnp.float32),
        ],
        scratch_shapes=[pltpu.VMEM((PAIR, count), jnp.bfloat16)],
        compiler_params=pltpu.CompilerParams(vmem_limit_bytes=32 << 20),
        cost_estimate=attention_cost(count, pairs, 64),
    )(segment.reshape(-1, 1), segment, qkv, qkv, qkv)


def attend_back(qkv, segment, lse_rows, d_context, turn, turns):
    count = qkv.shape[0]
    pairs = qkv.shape[1] // (3 * PAIR)
    here = pairs // turns
    block = min(Q_BLOCK, count)
    seg_col, seg_row, query, key, value, lse = attention_specs(count, pairs, block, turn * here)
    d_query = pl.BlockSpec((block, PAIR), lambda h, i: (i, h))
    d_whole = pl.BlockSpec((count, PAIR), lambda h, i: (0, h))
    shape = jax.ShapeDtypeStruct((count, here * PAIR), jnp.bfloat16)
    return pl.pallas_call(
        attend_back_kernel,
        grid=(here, count // block),
        in_specs=[seg_col, seg_row, query, key, value, lse, query],
        out_specs=[d_query, d_whole, d_whole],
        out_shape=[shape, shape, shape],
        scratch_shapes=[
            pltpu.VMEM((PAIR, count), jnp.bfloat16),
            pltpu.VMEM((count, PAIR), jnp.float32),
            pltpu.VMEM((count, PAIR), jnp.float32),
        ],
        compiler_params=pltpu.CompilerParams(vmem_limit_bytes=32 << 20),
        cost_estimate=attention_cost(count, here, 11),
    )(segment.reshape(-1, 1), segment, qkv, qkv, qkv, lse_rows, d_context)


def matmul(left, right):
    return jnp.dot(left, right, preferred_element_type=jnp.float32)


def matmul_tn(left, right):
    return lax.dot_general(
        left, right, (((0,), (0,)), ((), ())), preferred_element_type=jnp.float32
    )


def matmul_nt(left, right):
    return lax.dot_general(
        left, right, (((1,), (1,)), ((), ())), preferred_element_type=jnp.float32
    )


def column_sum(values):
    return jnp.sum(values.astype(jnp.float32), axis=0)


def swapped(part):
    return lax.ppermute(part, "col", [(0, 1), (1, 0)])


def swapped_rows(part):
    other = swapped(part)
    cut = other.shape[1] // 2
    return jnp.concatenate([other[:, cut:], other[:, :cut]], axis=1).astype(jnp.float32)


def partner(part, axis, bit):
    size = lax.axis_size(axis)
    return lax.ppermute(part, axis, [(i, i ^ bit) for i in range(size)])


def shifted(part, step):
    size = lax.axis_size("row")
    return lax.ppermute(part, "row", [(i, (i + step) % size) for i in range(size)])


def is_small_grid(rows):
    return lax.axis_size("row") == 4 and lax.axis_size("dp") == 4 and rows % 128 == 0


def place_kernel(idx, own, ring, near_x, near_y, far, *outs):
    quarter = ring.shape[0]
    begin = 0
    for out in outs:
        columns = slice(begin, begin + out.shape[1])
        begin = begin + out.shape[1]

        @pl.when(pl.program_id(0) == 0)
        def _():
            out[...] = own[:, columns]

        @pl.when(pl.program_id(0) > 0)
        def _():
            for corner, piece in enumerate((ring, near_x, near_y, far)):
                start = pl.multiple_of(idx[4 + corner] * quarter, quarter)
                out[pl.ds(start, quarter), :] = piece[:, columns]


def place(idx, own, pieces, widths):
    rows, width = own.shape
    fixed = pl.BlockSpec(own.shape, lambda s, idx: (0, 0))
    moving = pl.BlockSpec((rows // 4, width), lambda s, idx: (jnp.maximum(s - 1, 0), 0))
    return pl.pallas_call(
        place_kernel,
        grid_spec=pltpu.PrefetchScalarGridSpec(
            num_scalar_prefetch=1,
            grid=(4,),
            in_specs=[fixed, moving, moving, moving, moving],
            out_specs=[pl.BlockSpec((rows, w), lambda s, idx: (idx[s], 0)) for w in widths],
        ),
        out_shape=[jax.ShapeDtypeStruct((4 * rows, w), own.dtype) for w in widths],
        compiler_params=pltpu.CompilerParams(vmem_limit_bytes=40 << 20),
        cost_estimate=NO_COST,
    )(idx, own, *pieces)


def natural_order(whole):
    cut = whole.shape[0] // 2
    return jnp.where(
        lax.axis_index("col") == 0, whole, jnp.concatenate([whole[cut:], whole[:cut]], axis=0)
    )


def gathered(block):
    rows = block.shape[0] // lax.axis_size("dp")
    part = lax.dynamic_slice_in_dim(block, lax.axis_index("dp") * rows, rows, 0)
    return natural_order(lax.all_gather(part, ("row", "dp"), axis=0, tiled=True))


def sync_kernel(*refs):
    pass


def sync(arrays):
    arrays = list(arrays)
    return pl.pallas_call(
        sync_kernel,
        in_specs=[pl.BlockSpec(memory_space=pl.ANY)] * len(arrays),
        out_specs=[pl.BlockSpec(memory_space=pl.ANY)] * len(arrays),
        out_shape=[jax.ShapeDtypeStruct(part.shape, part.dtype) for part in arrays],
        input_output_aliases={i: i for i in range(len(arrays))},
        cost_estimate=NO_COST,
    )(*arrays)


def checkpoint(value, *movers):
    counts = [len(mover.got) for mover in movers]
    if sum(counts):
        value, *got = sync([value] + [part for mover in movers for part in mover.got])
        for mover, count in zip(movers, counts):
            mover.got, got = got[:count], got[count:]
    sends = [mover.sends() for mover in movers]
    if sum(len(some) for some in sends):
        value, *flat = sync([value] + [part for some in sends for part in some])
        for mover, some in zip(movers, sends):
            mover.go(flat[: len(some)])
            flat = flat[len(some) :]
    return value


class Gather:
    def __init__(self, group, by_shifts=False, far_too=False):
        self.group, self.by_shifts, self.far_too = group, by_shifts, far_too
        self.got = []
        self.step = 0
        self.direct = not all(is_small_grid(block.shape[0]) for block in group)
        if self.direct:
            return
        core, corner = lax.axis_index("col"), lax.axis_index("dp")
        self.level, self.size = lax.axis_index("row"), lax.axis_size("row")
        place_z = self.level + self.size // 2 * core + self.size - jnp.arange(self.size)
        self.idx = jnp.concatenate([place_z % self.size, corner ^ jnp.arange(4)]).astype(jnp.int32)
        self.own = jnp.concatenate(group, axis=1) if len(group) > 1 else group[0]
        self.quarter = self.own.shape[0] // 4
        self.parts = [
            lax.dynamic_slice_in_dim(self.own, at * self.quarter, self.quarter, 0)
            for at in ((corner, corner ^ 3) if far_too else (corner,))
        ]

    def stacked(self, count, which):
        pieces = []
        for step in (1, 2, 3):
            level = (self.level + self.size - step) % self.size
            begin = (level * count + which) * self.quarter
            pieces.append(lax.dynamic_slice_in_dim(self.got[0], begin, self.quarter, 0))
        return jnp.concatenate(pieces, axis=0)

    def sends(self):
        if self.direct:
            return []
        if self.step == 0:
            return [jnp.concatenate(self.parts, axis=0) if self.far_too else self.parts[0]]
        if self.by_shifts:
            return [jnp.concatenate(self.got, axis=0)]
        return [self.stacked(len(self.parts), which) for which in range(len(self.parts))]

    def go(self, sends):
        if self.direct:
            return
        if self.step == 0 and self.by_shifts:
            self.got = [shifted(sends[0], step) for step in (1, 2, 3)]
        elif self.step == 0:
            self.got = [lax.all_gather(sends[0], "row", axis=0, tiled=True)]
        else:
            bits = (1, 2) if self.far_too else (1, 2, 3)
            self.got = [partner(sends[0], "dp", bit) for bit in bits]
            self.mine = sends
        self.step = self.step + 1

    def result(self):
        if self.direct:
            return [gathered(block) for block in self.group]
        pieces = [self.mine[0], *self.got, *self.mine[1:]]
        return place(self.idx, self.own, pieces, [block.shape[1] for block in self.group])


def pick(values, axis, index):
    return lax.dynamic_index_in_dim(values, index, axis, keepdims=False)


def added(*parts):
    total = parts[0].astype(jnp.float32)
    for part in parts[1:]:
        total = total + part.astype(jnp.float32)
    return total.astype(jnp.bfloat16)


class Reduction:
    def __init__(self, first, second, in_halves):
        corner = lax.axis_index("dp")
        self.corner, self.a, self.b = corner, corner // 2, corner % 2
        self.direct = not is_small_grid(2 * first.shape[0] // lax.axis_size("row"))
        self.step = 0 if in_halves else 10
        self.got = []
        if self.direct:
            self.whole = jnp.concatenate([first, second], axis=0)
        else:
            width = first.shape[1]
            self.first = first.reshape(2, 2, 2, -1, width)
            self.second = second.reshape(2, 2, 2, -1, width)

    def sends(self):
        if self.direct:
            return []
        a, b = self.a, self.b
        if self.step == 0:
            return [pick(self.first, 2, 1 - b), pick(self.second, 1, 1 - a)]
        if self.step == 1:
            one, two = self.got
            self.keep = (
                pick(pick(self.first, 2, b), 1, a),
                pick(one, 1, a),
                pick(pick(self.second, 1, a), 1, b),
                pick(two, 1, b),
            )
            return [
                added(pick(pick(self.first, 2, b), 1, 1 - a), pick(one, 1, 1 - a)),
                added(pick(pick(self.second, 1, a), 1, 1 - b), pick(two, 1, 1 - b)),
            ]
        if self.step == 2:
            parts = [added(*self.keep[:2], self.got[0]), added(*self.keep[2:], self.got[1])]
            return [self.in_row_order(parts)]
        if self.step == 10:
            return [jnp.concatenate(self.quarter_of(bit), axis=0) for bit in (1, 2, 3)]
        if self.step == 11:
            parts = []
            for i, own in enumerate(self.quarter_of(0)):
                parts.append(added(own, *[got[2 * i : 2 * i + 2] for got in self.got]))
            return [self.in_row_order(parts)]
        return self.got

    def quarter_of(self, bit):
        a, b = (self.corner ^ bit) // 2, (self.corner ^ bit) % 2
        return [pick(pick(half, 2, b), 1, a) for half in (self.first, self.second)]

    def in_row_order(self, parts):
        levels = natural_order(jnp.concatenate(parts, axis=0))
        return levels.reshape(-1, levels.shape[-1])

    def go(self, sends):
        if self.direct:
            return
        if self.step == 0:
            self.got = [partner(sends[0], "dp", 1), partner(sends[1], "dp", 2)]
        elif self.step == 1:
            self.got = [partner(sends[0], "dp", 2), partner(sends[1], "dp", 1)]
        elif self.step == 10:
            self.got = [partner(part, "dp", bit) for part, bit in zip(sends, (1, 2, 3))]
        elif self.step in (2, 11):
            self.step = 2
            self.got = [lax.psum_scatter(sends[0], "row", scatter_dimension=0, tiled=True)]
        else:
            self.got = [sends[0]] + [partner(sends[0], "dp", bit) for bit in (1, 2, 3)]
        self.step = self.step + 1

    def result(self):
        if self.direct:
            whole = natural_order(self.whole)
            part = lax.psum_scatter(whole, ("row", "dp"), scatter_dimension=0, tiled=True)
            return lax.all_gather(part, "dp", axis=0, tiled=True).astype(jnp.float32)
        got = self.got
        return jnp.concatenate(
            [
                jnp.where(
                    self.a == 0,
                    jnp.where(self.b == 0, got[k], got[k ^ 1]),
                    jnp.where(self.b == 0, got[k ^ 2], got[k ^ 3]),
                )
                for k in range(4)
            ],
            axis=0,
        ).astype(jnp.float32)


class VectorSum:
    PARTNERS = (("dp", 1), ("dp", 2), ("row", 1), ("row", 2))

    def __init__(self, values):
        self.values = values.reshape(-1, 128)
        self.direct = not is_small_grid(128)
        self.got = []
        self.step = 0

    def sends(self):
        if self.direct:
            return []
        if self.got:
            self.values = self.values + self.got[0]
        return [self.values]

    def go(self, sends):
        if self.direct:
            return
        self.values = sends[0]
        self.got = [partner(sends[0], *self.PARTNERS[self.step])]
        self.step = self.step + 1

    def result(self):
        if self.direct:
            return lax.psum(self.values, ("row", "dp")).reshape(-1)
        while self.step < 4:
            self.go(self.sends())
        return (self.values + self.got[0]).reshape(-1)


def norm_forward(resid, gain, shift):
    center = jnp.mean(resid, axis=1, keepdims=True)
    inverse = lax.rsqrt(
        jnp.mean(resid * resid, axis=1, keepdims=True) - center * center + EPSILON
    )
    normed = (resid - center) * inverse
    return (normed * gain + shift, normed, inverse)


def norm_backward(grad, normed, inverse, gain):
    scaled = grad * gain
    first = jnp.mean(scaled, axis=1, keepdims=True)
    second = jnp.mean(scaled * normed, axis=1, keepdims=True)
    return inverse * (scaled - first - normed * second)


def body(
    tokens,
    segment,
    cotangent,
    w_query,
    b_query,
    w_key,
    w_value,
    b_value,
    w_out,
    b_out,
    w_up,
    b_up,
    w_down,
    b_down,
    gain_one,
    shift_one,
    gain_two,
    shift_two,
):
    half = w_query.shape[1]
    token_rows = jnp.concatenate([tokens, swapped(tokens)], axis=1)
    w_in = jnp.concatenate([w_query, w_key, w_value], axis=1)
    take_qkv = Gather([w_in], by_shifts=True)
    take_out_up = Gather([w_out, w_up])
    take_down = Gather([w_down], far_too=True)
    take_qkv.go(take_qkv.sends())
    token_rows = checkpoint(token_rows, take_qkv, take_out_up, take_down)
    (w_qkv,) = take_qkv.result()
    cotangent_rows = jnp.concatenate([cotangent, swapped(cotangent)], axis=1)
    own_vectors = jnp.stack([b_out, b_down, gain_one, shift_one, gain_two, shift_two])
    vectors = jnp.concatenate([own_vectors, swapped(own_vectors)], axis=1).astype(jnp.float32)
    bias_out, bias_down, gain1, shift1, gain2, shift2 = [vectors[i] for i in range(6)]
    b_qkv = jnp.concatenate([b_query, jnp.zeros_like(b_query), b_value]).astype(jnp.float32)
    qkv = (matmul(token_rows, w_qkv) + b_qkv).astype(jnp.bfloat16)
    qkv = checkpoint(qkv, take_out_up)
    context, lse_rows = attend(qkv, segment)
    count = len(take_out_up.got)
    context, *got = sync([context, *take_out_up.got, *take_down.got])
    take_out_up.got, take_down.got = got[:count], got[count:]
    context, *got = sync([context, *take_out_up.got, *take_down.sends()])
    take_out_up.got = got[:count]
    take_down.go(got[count:])
    context_rows = jnp.concatenate([context, swapped(context)], axis=1)
    wo_half, wu = take_out_up.result()
    wo_other = swapped(wo_half)
    wo = jnp.concatenate(
        [wo_half, jnp.concatenate([wo_other[half:], wo_other[:half]], axis=0)], axis=1
    )
    first_sum = token_rows.astype(jnp.float32) + (matmul(context_rows, wo) + bias_out)
    hidden_f, normed_one, inverse_one = norm_forward(first_sum, gain1, shift1)
    hidden = hidden_f.astype(jnp.bfloat16)
    hidden, *take_down.got = sync([hidden, *take_down.got])
    pre_act = matmul(hidden, wu) + b_up.astype(jnp.float32)
    cdf = 0.5 * (1.0 + lax.erf(pre_act * (0.5**0.5)))
    activated = (pre_act * cdf).astype(jnp.bfloat16)
    slope = cdf + pre_act * (jnp.exp(-0.5 * pre_act * pre_act) * 0.3989422804014327)
    (wd_half,) = take_down.result()
    units = w_up.shape[1]
    wd_own, wd_other = wd_half[:units], swapped(wd_half[units:])
    wd = jnp.concatenate([wd_own, wd_other], axis=1)
    part_other = matmul(activated, wd_other).astype(jnp.bfloat16)
    part_own = matmul(activated, wd_own).astype(jnp.bfloat16)
    ffn_out = jnp.concatenate(
        [
            part_own.astype(jnp.float32) + swapped(part_other).astype(jnp.float32),
            part_other.astype(jnp.float32) + swapped(part_own).astype(jnp.float32),
        ],
        axis=1,
    ) + bias_down
    second_sum = hidden.astype(jnp.float32) + ffn_out
    final, normed_two, inverse_two = norm_forward(second_sum, gain2, shift2)
    output = final[:, :half].astype(jnp.bfloat16)
    y = cotangent_rows.astype(jnp.float32)
    second_grad = norm_backward(y, normed_two, inverse_two, gain2)
    d_gain_two = jnp.sum(y * normed_two, axis=0)
    d_shift_two = jnp.sum(y, axis=0)
    ffn_grad = second_grad.astype(jnp.bfloat16)
    d_down_other = swapped(matmul_tn(activated, ffn_grad[:, half:]).astype(jnp.bfloat16))
    d_down_own = matmul_tn(activated, ffn_grad[:, :half]).astype(jnp.bfloat16)
    d_b_down = column_sum(ffn_grad)
    pre_grad = (matmul_nt(ffn_grad, wd) * slope).astype(jnp.bfloat16)
    d_b_up = column_sum(pre_grad)
    down = Reduction(d_down_own, d_down_other, in_halves=True)
    pre_grad = checkpoint(pre_grad, down)
    hidden_part = matmul_nt(pre_grad, wu).astype(jnp.bfloat16)
    hidden_other = swapped_rows(hidden_part)
    d_w_up = matmul_tn(hidden, pre_grad).astype(jnp.bfloat16)
    up = Reduction(d_w_up[:half], d_w_up[half:], in_halves=True)
    hidden_part = checkpoint(hidden_part, up)
    hidden_grad = second_grad + (hidden_part.astype(jnp.float32) + hidden_other)
    first_grad = norm_backward(hidden_grad, normed_one, inverse_one, gain1)
    d_gain_one = jnp.sum(hidden_grad * normed_one, axis=0)
    d_shift_one = jnp.sum(hidden_grad, axis=0)
    branch_grad = first_grad.astype(jnp.bfloat16)
    d_b_out = column_sum(branch_grad)
    wide = jnp.stack([d_b_out, d_b_down, d_gain_one, d_shift_one, d_gain_two, d_shift_two])
    context_grad = matmul_nt(branch_grad, wo[:half]).astype(jnp.bfloat16)
    d_w_out = matmul_tn(context_rows, branch_grad[:, :half]).astype(jnp.bfloat16)
    context_grad = checkpoint(context_grad, down)
    qkv_grad = jnp.concatenate(attend_back(qkv, segment, lse_rows, context_grad, 0, 1), axis=1)
    qkv_grad = checkpoint(qkv_grad, down, up)
    d_w_qkv = matmul_tn(token_rows, qkv_grad).astype(jnp.bfloat16)
    d_b_qkv = column_sum(qkv_grad)
    d_last = jnp.concatenate([d_w_out, d_w_qkv], axis=1)
    last = Reduction(d_last[:half], d_last[half:], in_halves=False)
    vector = VectorSum(
        jnp.concatenate(
            [wide[:, :half].reshape(-1), d_b_qkv[:half], d_b_qkv[2 * half :], d_b_up]
        )
    )
    token = checkpoint(d_b_qkv[:128].reshape(1, 128), last, up, vector)
    token, qkv_grad = sync([token, qkv_grad])
    token = checkpoint(token, vector)
    token = checkpoint(token, last, down, up, vector)
    token_part = matmul_nt(qkv_grad, w_qkv).astype(jnp.bfloat16)
    token_other = swapped(token_part[:, half:])
    token_sum = token_part[:, :half].astype(jnp.float32) + token_other.astype(jnp.float32)
    d_tokens = (token_sum + first_grad[:, :half]).astype(jnp.bfloat16)
    token = checkpoint(token, last, vector)
    o_w_down, o_w_up, o_last = down.result(), up.result(), last.result()
    sums = vector.result()
    pieces = [sums[i * half : (i + 1) * half] for i in range(8)]
    return (
        output,
        d_tokens,
        o_last[:, half : 2 * half],
        pieces[6],
        o_last[:, 2 * half : 3 * half],
        o_last[:, 3 * half :],
        pieces[7],
        o_last[:, :half],
        pieces[0],
        o_w_up,
        sums[8 * half :],
        o_w_down,
        pieces[1],
        pieces[2],
        pieces[3],
        pieces[4],
        pieces[5],
    )


def solution(mesh):
    in_specs = (
        P(("dp", "row"), "col"),
        P(("dp", "row"), None),
        P(("dp", "row"), "col"),
        P("row", "col"),
        P("col"),
        P("row", "col"),
        P("row", "col"),
        P("col"),
        P("row", "col"),
        P("col"),
        P("row", "col"),
        P("col"),
        P("row", "col"),
        P("col"),
        P("col"),
        P("col"),
        P("col"),
        P("col"),
    )
    out_specs = (
        P(("dp", "row"), "col"),
        P(("dp", "row"), "col"),
        P("row", "col"),
        P("col"),
        P("row", "col"),
        P("row", "col"),
        P("col"),
        P("row", "col"),
        P("col"),
        P("row", "col"),
        P("col"),
        P("row", "col"),
        P("col"),
        P("col"),
        P("col"),
        P("col"),
        P("col"),
    )
    return jax.shard_map(body, mesh=mesh, in_specs=in_specs, out_specs=out_specs, check_vma=False)
```
